32 devices in a mesh: dp: 8 (over z, x), row: 2 (over y), col: 2 (over core).
Axes of the slice: x: 2, y: 2, z: 4, core: 2. Of those that a mesh axis runs over, the one named last changes fastest.
Arguments:
- residual: bfloat16 [2, 16384, 1024], P(None, ('dp', 'row'), 'col'), may hold values from -6 to 6
- attend_norm_gain: float32 [1024], replicated, may hold values from 0.25 to 1.75
- attend_norm_bias: float32 [1024], replicated, may hold values from -3 to 3
- expand_norm_gain: float32 [1024], replicated, may hold values from 0.25 to 1.75
- expand_norm_bias: float32 [1024], replicated, may hold values from -3 to 3
- attend_weight: bfloat16 [1024, 16, 192], P('col', 'row', 'dp'), may hold values from -0.1875 to 0.1875
- attend_bias: float32 [16, 192], replicated, may hold values from -3 to 3
- output_weight: bfloat16 [16, 64, 1024], P('row', 'dp', 'col'), may hold values from -2 to 2
- output_bias: float32 [1024], replicated, may hold values from -4 to 4
- expand_weight: bfloat16 [1024, 4096], P('col', ('dp', 'row')), may hold values from -0.1875 to 0.1875
- expand_bias: float32 [4096], replicated, may hold values from -4 to 4
- shrink_weight: bfloat16 [4096, 1024], P(('dp', 'row'), 'col'), may hold values from -0.09375 to 0.09375
- shrink_bias: float32 [1024], replicated, may hold values from -4 to 4
- cotangent: bfloat16 [2, 16384, 1024], P(None, ('dp', 'row'), 'col'), may hold values from -6 to 6
Outputs:
- layer_output: bfloat16 [2, 16384, 1024], P(None, ('dp', 'row'), 'col')
- residual_grad: float32 [2, 16384, 1024], P(None, ('dp', 'row'), 'col')
- attend_norm_gain_grad: float32 [1024], replicated
- attend_norm_bias_grad: float32 [1024], replicated
- expand_norm_gain_grad: float32 [1024], replicated
- expand_norm_bias_grad: float32 [1024], replicated
- attend_weight_grad: float32 [1024, 16, 192], P('col', 'row', 'dp')
- attend_bias_grad: float32 [16, 192], replicated
- output_weight_grad: float32 [16, 64, 1024], P('row', 'dp', 'col')
- output_bias_grad: float32 [1024], replicated
- expand_weight_grad: float32 [1024, 4096], P('col', ('dp', 'row'))
- expand_bias_grad: float32 [4096], replicated
- shrink_weight_grad: float32 [4096, 1024], P(('dp', 'row'), 'col')
- shrink_bias_grad: float32 [1024], replicated
The draws below stay inside these ranges and needn't reach their ends.
All inputs are finite; a program needn't handle non-finite values.
Results may differ from the reference program's by a relative error of at most 0.013.
Values may be sent and summed in bfloat16 or wider, within the bound.
A program may use at most 256 MiB of HBM per device.

```python
import jax
import jax.numpy as jnp
from jax import lax

D = 1024
HEADS = 16
HS = 64
ROT = 16
FF = 4096
LEN = 2048
MICRO = 2
TOKENS = 16384
N_DP = 8


def block_scale(stream_key, shape, split, low, high):
    loudness, own = 1.0, jax.random.fold_in(stream_key, 6)
    for axis_at, parts in split:
        draws = jnp.exp(jax.random.uniform(jax.random.fold_in(own, axis_at), (parts,), jnp.float32, low / len(split), high / len(split)))
        loudness = loudness * jnp.repeat(draws, shape[axis_at] // parts).reshape([-1 if axis == axis_at else 1 for axis in range(len(shape))])
    return loudness


def scatter_about(stream_key, dims, deviation, reach, cuts=(), kind=jnp.bfloat16):
    values = jax.random.normal(stream_key, dims, jnp.float32) * deviation
    if len(cuts) > 0:
        values = block_scale(stream_key, dims, cuts, -0.22, 0.18) * values
    return jnp.clip(values, min=-reach, max=reach).astype(kind)


def setup_inputs(seed: int = 0) -> dict:
    streams_of = jax.random.split(jax.random.key(seed), 15)
    residual = scatter_about(streams_of[0], (MICRO, TOKENS, D), 1.0, 6.0, ((1, 16), (2, 2)))
    attend_norm_gain = jnp.clip(1.0 + 0.15 * jax.random.normal(streams_of[1], (D,), jnp.float32), 0.25, 1.75)
    attend_norm_bias = scatter_about(streams_of[2], (D,), 0.3, 3.0, (), jnp.float32)
    expand_norm_gain = jnp.clip(1.0 + 0.15 * jax.random.normal(streams_of[3], (D,), jnp.float32), 0.25, 1.75)
    expand_norm_bias = scatter_about(streams_of[4], (D,), 0.3, 3.0, (), jnp.float32)
    attend_weight = scatter_about(streams_of[5], (D, HEADS, 3 * HS), D ** -0.5, 0.1875, ((0, 2), (1, 2), (2, 8)))
    attend_bias = scatter_about(streams_of[6], (HEADS, 3 * HS), 0.3, 3.0, (), jnp.float32)
    output_weight = scatter_about(streams_of[7], (HEADS, HS, D), (HS // 8) ** -0.5, 2.0, ((0, 2), (1, 8), (2, 2)))
    output_bias = scatter_about(streams_of[8], (D,), 0.5, 4.0, (), jnp.float32)
    expand_weight = scatter_about(streams_of[9], (D, FF), D ** -0.5, 0.1875, ((0, 2), (1, 16)))
    expand_bias = scatter_about(streams_of[10], (FF,), 0.5, 4.0, (), jnp.float32)
    shrink_weight = scatter_about(streams_of[11], (FF, D), FF ** -0.5, 0.09375, ((0, 16), (1, 2)))
    shrink_bias = scatter_about(streams_of[12], (D,), 0.5, 4.0, (), jnp.float32)
    cotangent = scatter_about(streams_of[13], (MICRO, TOKENS, D), 1.0, 6.0, ((1, 16), (2, 2)))
    return dict(residual=residual, attend_norm_gain=attend_norm_gain, attend_norm_bias=attend_norm_bias, expand_norm_gain=expand_norm_gain, expand_norm_bias=expand_norm_bias, attend_weight=attend_weight, attend_bias=attend_bias, output_weight=output_weight, output_bias=output_bias, expand_weight=expand_weight, expand_bias=expand_bias, shrink_weight=shrink_weight, shrink_bias=shrink_bias, cotangent=cotangent)


@jax.custom_vjp
def low(v):
    return lax.optimization_barrier(v.astype(jnp.bfloat16)).astype(jnp.float32)

@jax.custom_vjp
def low_back(v):
    return v

def low_keep(v):
    return (low(v), None)

def low_pass(kept, grad):
    return (grad,)

def back_keep(v):
    return (v, None)

def back_low(kept, grad):
    return (low(grad),)
low.defvjp(low_keep, low_pass)
low_back.defvjp(back_keep, back_low)
EPSILON = 1e-05
MASKED = -1e+30
PRECISE = lax.Precision.HIGHEST

def rotary_tables(length):
    places = jnp.arange(length, dtype=jnp.float32)
    powers = jnp.arange(ROT // 2, dtype=jnp.float32) * (2.0 / ROT)
    inverse = jnp.power(10000.0, -powers)
    angles = places[:, None] * inverse[None, :]
    angles = jnp.concatenate([angles, angles], axis=1)
    return (jnp.cos(angles)[:, None, :], jnp.sin(angles)[:, None, :])

def rotate(features, cosine_table, sine_table):
    halfway = ROT // 2
    turned = jnp.concatenate([-features[..., halfway:ROT], features[..., :halfway]], axis=-1)
    spun_part = features[..., :ROT] * cosine_table + turned * sine_table
    return jnp.concatenate([spun_part, features[..., ROT:]], axis=-1)

def sequence_layer(tokens, params):
    attend_norm_gain, attend_norm_bias, expand_norm_gain, expand_norm_bias, attend_weight, attend_bias, output_weight, output_bias, expand_weight, expand_bias, shrink_weight, shrink_bias = params
    length = tokens.shape[0]
    center = lax.optimization_barrier(jnp.mean(tokens, axis=-1, keepdims=True))
    spread = lax.optimization_barrier(jnp.mean(tokens * tokens, axis=-1, keepdims=True)) - center * center
    normed = (tokens - center) * lax.rsqrt(spread + EPSILON)
    first_in = low(normed * attend_norm_gain + attend_norm_bias)
    second_in = low(normed * expand_norm_gain + expand_norm_bias)
    triple = jnp.einsum('td,dhe->the', first_in, attend_weight, precision=PRECISE) + attend_bias
    triple = low_back(triple)
    cosine_table, sine_table = rotary_tables(length)
    queries = low(rotate(triple[..., :HS], cosine_table, sine_table))
    keys_all = low(rotate(triple[..., HS:2 * HS], cosine_table, sine_table))
    values = low(triple[..., 2 * HS:])
    block_rows = min(512, length)

    def attend(begin_row):
        query_block = lax.dynamic_slice_in_dim(queries, begin_row, block_rows, 0)
        scores = jnp.einsum('qhe,khe->hqk', query_block, keys_all, precision=PRECISE) * HS ** (-0.5)
        scores = low_back(scores)
        query_places = begin_row + jnp.arange(block_rows)
        allowed = jnp.arange(length)[None, :] <= query_places[:, None]
        scores = jnp.where(allowed[None], scores, MASKED)
        weights = jax.nn.softmax(scores, axis=-1)
        return jnp.einsum('hqk,khe->qhe', low(weights), values, precision=PRECISE)
    starts = (jnp.arange(length // block_rows) * block_rows).astype(jnp.int32)
    attended = lax.map(jax.checkpoint(attend), starts).reshape(length, HEADS, HS)
    attended = low_back(low(attended))
    attend_out = jnp.einsum('the,hef->tf', attended, output_weight, precision=PRECISE) + output_bias
    expanded = low_back(jnp.dot(second_in, expand_weight, precision=PRECISE) + expand_bias)
    activated = low(jax.nn.gelu(expanded, approximate=False))
    shrunk = jnp.dot(activated, shrink_weight, precision=PRECISE) + shrink_bias
    return tokens + attend_out + shrunk

def forward(tokens_all, *params):
    sequences = tokens_all.reshape(MICRO * N_DP, LEN, D)

    def scan_step(running, one_sequence):
        return (running, sequence_layer(one_sequence, params))
    _, outputs = lax.scan(jax.checkpoint(scan_step), jnp.zeros((), jnp.float32), sequences)
    return outputs.reshape(MICRO, N_DP * LEN, D)

def reference(residual, attend_norm_gain, attend_norm_bias, expand_norm_gain, expand_norm_bias, attend_weight, attend_bias, output_weight, output_bias, expand_weight, expand_bias, shrink_weight, shrink_bias, cotangent):
    inputs = tuple((member.astype(jnp.float32) for member in (residual, attend_norm_gain, attend_norm_bias, expand_norm_gain, expand_norm_bias, attend_weight, attend_bias, output_weight, output_bias, expand_weight, expand_bias, shrink_weight, shrink_bias)))
    result, pullback = jax.vjp(forward, *inputs)
    gradients = pullback(cotangent.astype(jnp.float32))
    return (result.astype(jnp.bfloat16), gradients[0], gradients[1], gradients[2], gradients[3], gradients[4], gradients[5], gradients[6], gradients[7], gradients[8], gradients[9], gradients[10], gradients[11], gradients[12])
```

```python
from functools import partial

import jax
import jax.numpy as jnp
import numpy as np
from jax import lax
from jax.experimental import pallas as pl
from jax.experimental.pallas import tpu as pltpu
from jax.sharding import PartitionSpec as P

D = 1024
HS = 64
ROT = 16
HALF = ROT // 2
EPSILON = 1e-05
MASKED = -1e30
NN = (((1,), (0,)), ((), ()))
NT = (((1,), (1,)), ((), ()))
TN = (((0,), (0,)), ((), ()))
VMEM_LIMIT = 56 << 20
F32 = jnp.float32
BF16 = jnp.bfloat16


def mm(a, b, dims):
    return lax.dot_general(a, b, dims, preferred_element_type=F32)


def params(**extra):
    return pltpu.CompilerParams(vmem_limit_bytes=VMEM_LIMIT, **extra)


def cost(flops, nbytes):
    return pl.CostEstimate(flops=int(flops), bytes_accessed=int(nbytes), transcendentals=0)


def whole(shape):
    return pl.BlockSpec(shape, lambda *_: (0,) * len(shape))


def project_kernel(xa, xc, weight, bias, vectors, cosine, sine, first, second, triple):
    wide = xa.shape[1]
    near = xa[...].astype(F32)
    far = xc[...].astype(F32)
    total = jnp.sum(near + far, axis=1, keepdims=True)
    squares = jnp.sum(near * near + far * far, axis=1, keepdims=True)
    width = 2 * wide
    center = total / width
    inv = lax.rsqrt(squares / width - center * center + EPSILON)
    for part, values in ((0, near), (1, far)):
        cols = slice(part * wide, (part + 1) * wide)
        normed = (values - center) * inv
        first[:, cols] = (normed * vectors[0:1, cols] + vectors[1:2, cols]).astype(BF16)
        second[:, cols] = (normed * vectors[2:3, cols] + vectors[3:4, cols]).astype(BF16)
    heads = weight.shape[0] // (3 * HS)
    cos, sin = cosine[...], sine[...]
    for head in range(heads):
        base = head * 3 * HS
        rows = mm(weight[base : base + 3 * HS, :], first[...], NT) + bias[base : base + 3 * HS, :]
        for which in range(3):
            lo = which * HS
            scale = HS ** (-0.5) if which == 0 else 1.0
            out = base + lo
            if which < 2:
                u1, u2 = rows[lo : lo + HALF], rows[lo + HALF : lo + ROT]
                spun = jnp.concatenate([u1 * cos - u2 * sin, u2 * cos + u1 * sin], axis=0)
                triple[out : out + ROT, :] = (spun * scale).astype(BF16)
                triple[out + ROT : out + HS, :] = (rows[lo + ROT : lo + HS] * scale).astype(BF16)
            else:
                triple[out : out + HS, :] = rows[lo : lo + HS].astype(BF16)


def project(xa, xc, weight, bias, vectors, cosine, sine, block=512):
    tokens, wide = xa.shape
    rows = weight.shape[0]
    block = min(block, tokens)
    tile = pl.BlockSpec((block, wide), lambda i: (i, 0))
    full = pl.BlockSpec((block, 2 * wide), lambda i: (i, 0))
    table = pl.BlockSpec((HALF, block), lambda i: (0, i))
    return pl.pallas_call(
        project_kernel,
        grid=(tokens // block,),
        in_specs=[tile, tile, whole(weight.shape), whole(bias.shape), whole(vectors.shape), table, table],
        out_specs=[full, full, pl.BlockSpec((rows, block), lambda i: (0, i))],
        out_shape=[
            jax.ShapeDtypeStruct((tokens, 2 * wide), BF16),
            jax.ShapeDtypeStruct((tokens, 2 * wide), BF16),
            jax.ShapeDtypeStruct((rows, tokens), BF16),
        ],
        compiler_params=params(),
        cost_estimate=cost(3 * tokens * rows * wide * 2, tokens * wide * 2 * 2 * 3),
        name="project",
    )(xa, xc, weight, bias, vectors, cosine, sine)


def causal_tile(size):
    keys = lax.broadcasted_iota(jnp.int32, (size, size), 0)
    places = lax.broadcasted_iota(jnp.int32, (size, size), 1)
    return keys <= places


def lanes(index, tokens):
    return pl.ds(pl.multiple_of(index * tokens, tokens), tokens)


def attend_kernel(row, own, far, out_own, out_far, logsum, q_s, k_s, v_s, o_s, *, step):
    tokens = own.shape[1]
    length = 2 * tokens
    here = row[0]
    there = 1 - here
    for ref, place in ((own, here), (far, there)):
        at = lanes(place, tokens)
        q_s[:, at] = ref[0:HS, :]
        k_s[:, at] = ref[HS : 2 * HS, :]
        v_s[0:HS, at] = ref[2 * HS : 3 * HS, :]
    extra = lax.broadcasted_iota(jnp.int32, (16, length), 0)
    v_s[HS : HS + 16, :] = jnp.where(extra == 0, 1.0, 0.0).astype(BF16)
    allowed = causal_tile(step)
    for i in range(length // step):
        lo, hi = i * step, (i + 1) * step
        query = q_s[:, lo:hi]
        diag = jnp.where(allowed, mm(k_s[:, lo:hi], query, TN), MASKED)
        highest = jnp.max(diag, axis=0, keepdims=True)
        if i:
            past = mm(k_s[:, :lo], query, TN)
            highest = jnp.maximum(highest, jnp.max(past, axis=0, keepdims=True))
        raised = jnp.exp(diag - highest).astype(BF16)
        result = mm(v_s[:, lo:hi], raised, NN)
        if i:
            raised = jnp.exp(past - highest).astype(BF16)
            result = result + mm(v_s[:, :lo], raised, NN)
        total = result[HS : HS + 1]
        o_s[:, lo:hi] = (result[:HS] / total).astype(BF16)
        logsum[0, :, lo:hi] = highest + jnp.log(total)
    out_own[...] = o_s[:, lanes(here, tokens)]
    out_far[...] = o_s[:, lanes(there, tokens)]


def attend(row, own, far, step=256):
    rows, tokens = own.shape
    heads = rows // (3 * HS)
    length = 2 * tokens
    source = pl.BlockSpec((3 * HS, tokens), lambda h: (h, 0))
    result = pl.BlockSpec((HS, tokens), lambda h: (h, 0))
    return pl.pallas_call(
        partial(attend_kernel, step=min(step, length)),
        grid=(heads,),
        in_specs=[pl.BlockSpec(memory_space=pltpu.SMEM), source, source],
        out_specs=[result, result, pl.BlockSpec((1, 1, length), lambda h: (h, 0, 0))],
        out_shape=[
            jax.ShapeDtypeStruct((heads * HS, tokens), BF16),
            jax.ShapeDtypeStruct((heads * HS, tokens), BF16),
            jax.ShapeDtypeStruct((heads, 1, length), F32),
        ],
        scratch_shapes=[
            pltpu.VMEM((HS, length), BF16),
            pltpu.VMEM((HS, length), BF16),
            pltpu.VMEM((HS + 16, length), BF16),
            pltpu.VMEM((HS, length), BF16),
        ],
        compiler_params=params(),
        cost_estimate=cost(heads * length * length * 256 * 2, 8 * rows * tokens),
        name="attend",
    )(row, own, far)


def attend_back_kernel(
    row, own, far, grad_own, grad_far, att_own, att_far, logsum, cosine, sine,
    out_own, out_far, bias_grad, q_s, k_s, v_s, g_s, delta_s, dq_s, dk_s, dv_s, t_s, *, step,
):
    tokens = own.shape[1]
    length = 2 * tokens
    here = row[0]
    there = 1 - here
    for ref, grad, att, place in (
        (own, grad_own, att_own, here),
        (far, grad_far, att_far, there),
    ):
        at = lanes(place, tokens)
        q_s[:, at] = ref[0:HS, :]
        k_s[:, at] = ref[HS : 2 * HS, :]
        v_s[:, at] = ref[2 * HS : 3 * HS, :]
        g_s[:, at] = grad[...]
        delta_s[:, at] = jnp.sum(
            grad[...].astype(F32) * att[...].astype(F32), axis=0, keepdims=True
        )
    dk_s[...] = jnp.zeros_like(dk_s)
    dv_s[...] = jnp.zeros_like(dv_s)
    allowed = causal_tile(step)
    for i in range(length // step):
        lo, hi = i * step, (i + 1) * step
        query, grad = q_s[:, lo:hi], g_s[:, lo:hi]
        base, delta = logsum[0, :, lo:hi], delta_s[:, lo:hi]
        query_grad = None
        for begin, end in ((0, lo), (lo, hi)):
            if end == begin:
                continue
            raised = jnp.exp(mm(k_s[:, begin:end], query, TN) - base)
            if begin == lo:
                raised = jnp.where(allowed, raised, 0.0)
            prob_grad = mm(v_s[:, begin:end], grad, TN)
            score_grad = (raised * (prob_grad - delta)).astype(BF16)
            dv_s[:, begin:end] += mm(grad, raised.astype(BF16), NT)
            dk_s[:, begin:end] += mm(query, score_grad, NT)
            term = mm(k_s[:, begin:end], score_grad, NN)
            query_grad = term if query_grad is None else query_grad + term
        dq_s[:, lo:hi] = query_grad * HS ** (-0.5)
    cos, sin = cosine[...], sine[...]
    for which, ref in ((0, dq_s), (1, dk_s)):
        g1, g2 = ref[0:HALF, :], ref[HALF:ROT, :]
        spun = jnp.concatenate([g1 * cos + g2 * sin, g2 * cos - g1 * sin], axis=0)
        t_s[which * HS : which * HS + ROT, :] = spun.astype(BF16)
        t_s[which * HS + ROT : (which + 1) * HS, :] = ref[ROT:HS, :].astype(BF16)
    t_s[2 * HS : 3 * HS, :] = dv_s[...].astype(BF16)
    bias_grad[...] = jnp.sum(t_s[...].astype(F32), axis=1, keepdims=True)
    out_own[...] = t_s[:, lanes(here, tokens)]
    out_far[...] = t_s[:, lanes(there, tokens)]


def attend_back(row, own, far, grad_own, grad_far, att_own, att_far, logsum, cosine, sine, step=256):
    rows, tokens = own.shape
    heads = rows // (3 * HS)
    length = 2 * tokens
    source = pl.BlockSpec((3 * HS, tokens), lambda h: (h, 0))
    narrow = pl.BlockSpec((HS, tokens), lambda h: (h, 0))
    table = whole((HALF, length))
    return pl.pallas_call(
        partial(attend_back_kernel, step=min(step, length)),
        grid=(heads,),
        in_specs=[
            pl.BlockSpec(memory_space=pltpu.SMEM), source, source, narrow, narrow, narrow, narrow,
            pl.BlockSpec((1, 1, length), lambda h: (h, 0, 0)), table, table,
        ],
        out_specs=[source, source, pl.BlockSpec((3 * HS, 1), lambda h: (h, 0))],
        out_shape=[
            jax.ShapeDtypeStruct((rows, tokens), BF16),
            jax.ShapeDtypeStruct((rows, tokens), BF16),
            jax.ShapeDtypeStruct((rows, 1), F32),
        ],
        scratch_shapes=[
            pltpu.VMEM((HS, length), BF16),
            pltpu.VMEM((HS, length), BF16),
            pltpu.VMEM((HS, length), BF16),
            pltpu.VMEM((HS, length), BF16),
            pltpu.VMEM((1, length), F32),
            pltpu.VMEM((HS, length), F32),
            pltpu.VMEM((HS, length), F32),
            pltpu.VMEM((HS, length), F32),
            pltpu.VMEM((3 * HS, length), BF16),
        ],
        compiler_params=params(),
        cost_estimate=cost(heads * length * length * 256 * 5, 16 * rows * tokens),
        name="attend_back",
    )(row, own, far, grad_own, grad_far, att_own, att_far, logsum, cosine, sine)


POLY = (0.254829592, -0.284496736, 1.421413741, -1.453152027, 1.061405429)


def gelu_pair(value):
    magnitude = jnp.abs(value)
    t = 1.0 / (1.0 + magnitude * (0.3275911 * 0.5**0.5))
    bell = jnp.exp(value * value * -0.5)
    series = POLY[4]
    for term in (POLY[3], POLY[2], POLY[1], POLY[0]):
        series = series * t + term
    tail = 0.5 * series * t * bell
    cumulative = jnp.where(value >= 0.0, 1.0 - tail, tail)
    return value * cumulative, cumulative + value * bell * (1.0 / (2.0 * np.pi) ** 0.5)


def middle_kernel(
    second_own, second_far, ca, cb, cc, cd, att_own, att_far, w1, w2, wo, bias,
    out_near, out_other, heads_own, heads_far, part_own, part_far, dw1, dw2, dwo, dbias,
    s_s, c_s, a_s, act_s, eg_s, h_s, *, chunk,
):
    half, at = pl.program_id(0), pl.program_id(1)
    wide = ca.shape[1]

    @pl.when((half == 0) & (at == 0))
    def _():
        dw1[...] = jnp.zeros_like(dw1)
        dw2[...] = jnp.zeros_like(dw2)
        dwo[...] = jnp.zeros_like(dwo)
        dbias[...] = jnp.zeros_like(dbias)

    for this, second, near, other, att in (
        (0, second_far, cb, cd, att_far),
        (1, second_own, ca, cc, att_own),
    ):
        @pl.when(half == this)
        def _():
            s_s[...] = second[...]
            c_s[:, :wide] = near[...]
            c_s[:, wide:] = other[...]
            a_s[...] = att[...]

    hidden = w1.shape[0]
    for lo in range(0, hidden, chunk):
        hi = lo + chunk
        expanded = mm(s_s[...], w1[lo:hi, :], NT) + bias[:, lo:hi]
        active, slope = gelu_pair(expanded)
        act_s[:, lo:hi] = active.astype(BF16)
        expand_grad = mm(c_s[...], w2[lo:hi, :], NT) * slope
        rounded = expand_grad.astype(BF16)
        eg_s[:, lo:hi] = rounded
        dbias[:, lo:hi] += jnp.sum(rounded.astype(F32), axis=0, keepdims=True)
    for lo in range(0, hidden, chunk):
        hi = lo + chunk
        dw2[lo:hi, :] += mm(act_s[:, lo:hi], c_s[...], TN)
        dw1[lo:hi, :] += mm(eg_s[:, lo:hi], s_s[...], TN)
    dwo[...] += mm(a_s[...], c_s[...], NN)
    h_s[...] = mm(wo[...], c_s[...], NT).astype(BF16)
    near = mm(act_s[...], w2[:, :wide], NN) + mm(a_s[...], wo[:, :wide], TN)
    out_near[0] = near.astype(BF16)
    other = mm(act_s[...], w2[:, wide:], NN) + mm(a_s[...], wo[:, wide:], TN)
    out_other[0] = other.astype(BF16)
    part = mm(eg_s[...], w1[...], NN).astype(BF16)
    for this, heads, ref in ((0, heads_far, part_far), (1, heads_own, part_own)):
        @pl.when(half == this)
        def _():
            heads[...] = h_s[...]
            ref[...] = part


def middle(second_own, second_far, ca, cb, cc, cd, att_own, att_far, w1, w2, wo, bias, block=256, chunk=256):
    tokens, wide = ca.shape
    width = 2 * wide
    block = min(block, tokens)
    steps = tokens // block
    hidden, head_rows = w1.shape[0], wo.shape[0]
    last = steps - 1
    far_at = lambda h, i: i * (1 - h) + last * h
    own_at = lambda h, i: i * h
    rows_far = lambda n: pl.BlockSpec((block, n), lambda h, i: (far_at(h, i), 0))
    rows_own = lambda n: pl.BlockSpec((block, n), lambda h, i: (own_at(h, i), 0))
    cols_far = pl.BlockSpec((head_rows, block), lambda h, i: (0, far_at(h, i)))
    cols_own = pl.BlockSpec((head_rows, block), lambda h, i: (0, own_at(h, i)))
    both = pl.BlockSpec((1, block, wide), lambda h, i: (h, i, 0))
    return pl.pallas_call(
        partial(middle_kernel, chunk=min(chunk, hidden)),
        grid=(2, steps),
        in_specs=[
            rows_own(width), rows_far(width), rows_own(wide), rows_far(wide), rows_own(wide), rows_far(wide),
            cols_own, cols_far, whole(w1.shape), whole(w2.shape), whole(wo.shape), whole(bias.shape),
        ],
        out_specs=[
            both, both, cols_own, cols_far, rows_own(width), rows_far(width),
            whole(w1.shape), whole(w2.shape), whole(wo.shape), whole(bias.shape),
        ],
        out_shape=[
            jax.ShapeDtypeStruct((2, tokens, wide), BF16),
            jax.ShapeDtypeStruct((2, tokens, wide), BF16),
            jax.ShapeDtypeStruct((head_rows, tokens), BF16),
            jax.ShapeDtypeStruct((head_rows, tokens), BF16),
            jax.ShapeDtypeStruct((tokens, width), BF16),
            jax.ShapeDtypeStruct((tokens, width), BF16),
            jax.ShapeDtypeStruct(w1.shape, F32),
            jax.ShapeDtypeStruct(w2.shape, F32),
            jax.ShapeDtypeStruct(wo.shape, F32),
            jax.ShapeDtypeStruct(bias.shape, F32),
        ],
        scratch_shapes=[
            pltpu.VMEM((block, width), BF16),
            pltpu.VMEM((block, width), BF16),
            pltpu.VMEM((head_rows, block), BF16),
            pltpu.VMEM((block, hidden), BF16),
            pltpu.VMEM((block, hidden), BF16),
            pltpu.VMEM((head_rows, block), BF16),
        ],
        compiler_params=params(),
        cost_estimate=cost(2 * tokens * 2 * width * (6 * hidden + 3 * head_rows), 2 * tokens * width * 10),
        name="middle",
    )(second_own, second_far, ca, cb, cc, cd, att_own, att_far, w1, w2, wo, bias)


def last_kernel(
    t_own, t_far, first_own, first_far, part_own, part_far, xa, xb, xc, xd, weight, vectors,
    ng_near, ng_other, sums, dweight, dvec, t_s, f_s, p_s, x_s,
):
    half, at = pl.program_id(0), pl.program_id(1)
    wide = xa.shape[1]

    @pl.when((half == 0) & (at == 0))
    def _():
        dweight[...] = jnp.zeros_like(dweight)
        dvec[...] = jnp.zeros_like(dvec)

    for this, t, first, part, near, other in (
        (0, t_far, first_far, part_far, xb, xd),
        (1, t_own, first_own, part_own, xa, xc),
    ):
        @pl.when(half == this)
        def _():
            t_s[...] = t[...]
            f_s[...] = first[...]
            p_s[...] = part[...]
            x_s[:, :wide] = near[...]
            x_s[:, wide:] = other[...]

    values = x_s[...].astype(F32)
    width = 2 * wide
    center = jnp.sum(values, axis=1, keepdims=True) / width
    spread = jnp.sum(values * values, axis=1, keepdims=True) / width - center * center
    inv = lax.rsqrt(spread + EPSILON)
    dweight[...] += mm(t_s[...], f_s[...], NN)
    first_sum = second_sum = 0.0
    for part, ref in ((0, ng_near), (1, ng_other)):
        cols = slice(part * wide, (part + 1) * wide)
        normed = (x_s[:, cols].astype(F32) - center) * inv
        first_grad = mm(t_s[...], weight[:, cols], TN)
        second_grad = p_s[:, cols].astype(F32)
        dvec[0:1, cols] += jnp.sum(first_grad * normed, axis=0, keepdims=True)
        dvec[1:2, cols] += jnp.sum(first_grad, axis=0, keepdims=True)
        dvec[2:3, cols] += jnp.sum(second_grad * normed, axis=0, keepdims=True)
        dvec[3:4, cols] += jnp.sum(second_grad, axis=0, keepdims=True)
        grad = first_grad * vectors[0:1, cols] + second_grad * vectors[2:3, cols]
        first_sum = first_sum + jnp.sum(grad, axis=1, keepdims=True)
        second_sum = second_sum + jnp.sum(grad * normed, axis=1, keepdims=True)
        ref[0] = grad.astype(BF16)
    column = lax.broadcasted_iota(jnp.int32, (x_s.shape[0], 128), 1)
    sums[0] = jnp.where(column == 0, first_sum, jnp.where(column == 1, second_sum, 0.0))


def last(t_own, t_far, first_own, first_far, part_own, part_far, xa, xb, xc, xd, weight, vectors, block=512):
    tokens, wide = xa.shape
    width = 2 * wide
    block = min(block, tokens)
    steps = tokens // block
    rows = weight.shape[0]
    end = steps - 1
    far_at = lambda h, i: i * (1 - h) + end * h
    own_at = lambda h, i: i * h
    rows_far = lambda n: pl.BlockSpec((block, n), lambda h, i: (far_at(h, i), 0))
    rows_own = lambda n: pl.BlockSpec((block, n), lambda h, i: (own_at(h, i), 0))
    cols_far = pl.BlockSpec((rows, block), lambda h, i: (0, far_at(h, i)))
    cols_own = pl.BlockSpec((rows, block), lambda h, i: (0, own_at(h, i)))
    both = pl.BlockSpec((1, block, wide), lambda h, i: (h, i, 0))
    return pl.pallas_call(
        last_kernel,
        grid=(2, steps),
        in_specs=[
            cols_own, cols_far, rows_own(width), rows_far(width), rows_own(width), rows_far(width),
            rows_own(wide), rows_far(wide), rows_own(wide), rows_far(wide),
            whole(weight.shape), whole(vectors.shape),
        ],
        out_specs=[
            both, both, pl.BlockSpec((1, block, 128), lambda h, i: (h, i, 0)),
            whole(weight.shape), whole((8, width)),
        ],
        out_shape=[
            jax.ShapeDtypeStruct((2, tokens, wide), BF16),
            jax.ShapeDtypeStruct((2, tokens, wide), BF16),
            jax.ShapeDtypeStruct((2, tokens, 128), F32),
            jax.ShapeDtypeStruct(weight.shape, F32),
            jax.ShapeDtypeStruct((8, width), F32),
        ],
        scratch_shapes=[
            pltpu.VMEM((rows, block), BF16),
            pltpu.VMEM((block, width), BF16),
            pltpu.VMEM((block, width), BF16),
            pltpu.VMEM((block, width), BF16),
        ],
        compiler_params=params(),
        cost_estimate=cost(2 * tokens * 2 * width * 2 * rows, 2 * tokens * width * 10),
        name="last",
    )(t_own, t_far, first_own, first_far, part_own, part_far, xa, xb, xc, xd, weight, vectors)


def swap(value, axis):
    return lax.ppermute(value, axis, [(0, 1), (1, 0)])


def across(value, count):
    return lax.ppermute(value, "dp", [(i, i ^ 1) for i in range(count)])


def shifted(value, steps, count):
    return lax.ppermute(value, "dp", [(i, (i + 2 * steps) % count) for i in range(count)])


def spread(piece, count):
    pieces = []
    for s in range(count // 2):
        here = shifted(piece, s, count) if s else piece
        pieces += [here, across(here, count)]
    return pieces


def collect(tiles, count):
    depth = count // 2
    kept = tiles[:, 0].astype(F32) + across(tiles[:, 1], count).astype(F32)
    total = kept[0]
    for s in range(1, depth):
        total = total + shifted(kept[s].astype(BF16), -s, count).astype(F32)
    return total


def rows_from_cores(mine, col):
    wide = mine.shape[-1] // 2
    other = swap(mine[..., wide:], "col")
    mine = mine[..., :wide]
    return jnp.where(col == 0, jnp.concatenate([mine, other], 0), jnp.concatenate([other, mine], 0))


def part_of(value, index, size):
    return lax.dynamic_slice_in_dim(value, index * size, size, 0)


def body(
    residual, attend_norm_gain, attend_norm_bias, expand_norm_gain, expand_norm_bias,
    attend_weight, attend_bias, output_weight, output_bias, expand_weight, expand_bias,
    shrink_weight, shrink_bias, cotangent,
):
    count = lax.axis_size("dp")
    depth = count // 2
    row, col, dp = lax.axis_index("row"), lax.axis_index("col"), lax.axis_index("dp")
    place_z, place_x = dp // 2, dp % 2
    micros, tokens, wide = residual.shape
    length = 2 * tokens
    heads = attend_weight.shape[1] // 2
    head_part, out_part = attend_weight.shape[2], output_weight.shape[1]
    hid = expand_weight.shape[1] // 2
    order = (((place_z - jnp.arange(depth)) % depth)[:, None] * 2 + (place_x ^ jnp.arange(2))[None]).reshape(-1)

    xs = [[residual[m]] for m in range(micros)]
    cs = [[cotangent[m]] for m in range(micros)]
    for group in (xs, cs):
        for entry in group:
            entry.append(swap(entry[0], "row"))
    for group in (xs, cs):
        for entry in group:
            entry += [swap(entry[0], "col"), swap(entry[1], "col")]

    by_rows = (
        attend_weight.transpose(1, 2, 0).reshape(2, heads * head_part, wide),
        output_weight.reshape(2, heads * out_part, wide),
        expand_weight.T.reshape(2, hid, wide),
        shrink_weight.reshape(2, hid, wide),
    )
    first_rows = by_rows[0]
    rest_rows = jnp.concatenate(by_rows[1:], axis=1)

    def piece_of(rows):
        mine = lax.dynamic_index_in_dim(rows, col, 0, keepdims=False)
        theirs = lax.dynamic_index_in_dim(rows, 1 - col, 0, keepdims=False)
        return jnp.concatenate([mine, swap(theirs, "col")], axis=1)

    width = 2 * wide
    attend_all = jnp.stack(spread(piece_of(first_rows), count))
    wq = attend_all[order].reshape(count, heads, head_part, width).transpose(1, 0, 2, 3)
    wq = wq.reshape(heads * 3 * HS, width)
    rest = spread(piece_of(rest_rows), count)
    lo = heads * out_part
    wo = jnp.stack([piece[:lo] for piece in rest])[order]
    wo = wo.reshape(count, heads, out_part, width).transpose(1, 0, 2, 3).reshape(heads * HS, width)
    w1 = jnp.concatenate([piece[lo : lo + hid] for piece in rest])
    w2 = jnp.concatenate([piece[lo + hid :] for piece in rest])

    vectors = jnp.stack([attend_norm_gain, attend_norm_bias, expand_norm_gain, expand_norm_bias])
    vectors = jnp.concatenate([jnp.roll(vectors, -col * wide, axis=1), jnp.zeros((4, width), F32)])
    head_begin = row * 2 * heads + col * heads
    bias_q = lax.dynamic_slice_in_dim(attend_bias, head_begin, heads, 0).reshape(-1, 1)
    bias_1 = expand_bias.reshape(count, 4, hid)
    bias_1 = lax.dynamic_index_in_dim(bias_1, row * 2 + col, 1, keepdims=False)[order].reshape(1, -1)
    out_bias = part_of(output_bias + shrink_bias, col, wide)

    powers = 10000.0 ** (-np.arange(HALF) * (2.0 / ROT))
    angles = powers[:, None] * np.arange(length)[None, :]
    cosine, sine = jnp.asarray(np.cos(angles), F32), jnp.asarray(np.sin(angles), F32)
    tables = [
        (lax.dynamic_slice_in_dim(cosine, at * tokens, tokens, 1), lax.dynamic_slice_in_dim(sine, at * tokens, tokens, 1))
        for at in (row, 1 - row)
    ]
    where = row.astype(jnp.int32).reshape(1)

    outputs, input_grads, vector_grads = [], [], []
    tile_grads, dq_grads = [], []
    saved = []
    for m in range(micros):
        xa, xb, xc, xd = xs[m]
        first_own, second_own, own = project(xa, xc, wq, bias_q, vectors, *tables[0])
        first_far, second_far, far = project(xb, xd, wq, bias_q, vectors, *tables[1])
        att_own, att_far, logsum = attend(where, own, far)
        saved.append((first_own, first_far, second_own, second_far, own, far, att_own, att_far, logsum))
    middles = []
    for m in range(micros):
        first_own, first_far, second_own, second_far, own, far, att_own, att_far, logsum = saved[m]
        ca, cb, cc, cd = cs[m]
        middles.append(middle(second_own, second_far, ca, cb, cc, cd, att_own, att_far, w1, w2, wo, bias_1))
        near, other = middles[m][:2]
        crossed = swap(other, "col")
        moved = swap((near[0].astype(F32) + crossed[0].astype(F32)).astype(BF16), "row")
        outputs.append(
            (
                xs[m][0].astype(F32) + near[1].astype(F32) + crossed[1].astype(F32) + moved.astype(F32) + out_bias
            ).astype(BF16)
        )
    tile_grads = [sum(middles[m][6 + i] for m in range(micros)) for i in range(3)]
    dw1, dw2, dwo = tile_grads
    dwo = dwo.reshape(heads, count, out_part, width).transpose(1, 0, 2, 3)[order].reshape(count, -1, width)
    tiles = jnp.concatenate(
        [dwo.astype(BF16), dw1.astype(BF16).reshape(count, hid, width), dw2.astype(BF16).reshape(count, hid, width)], axis=1
    )
    rest_sum = collect(tiles.reshape(depth, 2, -1, width), count)
    for m in range(micros):
        first_own, first_far, second_own, second_far, own, far, att_own, att_far, logsum = saved[m]
        xa, xb, xc, xd = xs[m]
        heads_own, heads_far, part_own, part_far = middles[m][2:6]
        t_own, t_far, bias_grad = attend_back(
            where, own, far, heads_own, heads_far, att_own, att_far, logsum, cosine, sine
        )
        near, other, sums, dweight, dvec = last(
            t_own, t_far, first_own, first_far, part_own, part_far, xa, xb, xc, xd, wq, vectors
        )
        dq_grads.append(dweight)
        vector_grads.append((dvec, bias_grad, middles[m][9]))
        crossed = swap(other, "col")
        moved = swap((near[0].astype(F32) + crossed[0].astype(F32)).astype(BF16), "row")
        sums = sums[:, :, :2].transpose(0, 2, 1)
        sums = sums + swap(sums, "col")
        sums = sums[1] + swap(sums[0], "row")
        grad = near[1].astype(F32) + crossed[1].astype(F32) + moved.astype(F32)
        near_x, far_x = xa.astype(F32), xc.astype(F32)
        center = (jnp.sum(near_x, 1) + jnp.sum(far_x, 1)) / width
        spread_x = (jnp.sum(near_x * near_x, 1) + jnp.sum(far_x * far_x, 1)) / width - center * center
        inv = lax.rsqrt(spread_x + EPSILON)[:, None]
        normed = (near_x - center[:, None]) * inv
        input_grads.append(
            cs[m][0].astype(F32) + inv * (grad - sums[0][:, None] / width - normed * sums[1][:, None] / width)
        )
    dq = sum(dq_grads).reshape(heads, count, head_part, width).transpose(1, 0, 2, 3)[order]
    dq_sum = collect(dq.astype(BF16).reshape(depth, 2, -1, width), count)

    attend_weight_grad = rows_from_cores(dq_sum.reshape(heads, head_part, width), col).transpose(2, 0, 1)
    output_weight_grad = rows_from_cores(rest_sum[:lo].reshape(heads, out_part, width), col)
    expand_weight_grad = rows_from_cores(rest_sum[lo : lo + hid], col).T
    shrink_weight_grad = rows_from_cores(rest_sum[lo + hid :], col)

    dvec, dbq, db1 = (sum(v[i] for v in vector_grads) for i in range(3))
    dvec = jnp.roll(dvec[:4], col * wide, axis=1)
    dout = jnp.sum(cotangent.astype(F32), axis=(0, 1))
    dout = lax.dynamic_update_slice_in_dim(jnp.zeros((width,), F32), dout, col * wide, 0)
    dbq = lax.dynamic_update_slice_in_dim(jnp.zeros(attend_bias.shape, F32), dbq.reshape(heads, -1), head_begin, 0)
    db1 = db1.reshape(count, 1, hid)[order]
    db1 = lax.dynamic_update_slice_in_dim(jnp.zeros((count, 4, hid), F32), db1, row * 2 + col, 1).reshape(-1)
    dvec, dout, dbq, db1 = lax.psum((dvec, dout, dbq, db1), ("dp", "row", "col"))
    return (
        jnp.stack(outputs), jnp.stack(input_grads), dvec[0], dvec[1], dvec[2], dvec[3],
        attend_weight_grad, dbq, output_weight_grad, dout, expand_weight_grad, db1, shrink_weight_grad, dout,
    )


def solution(mesh):
    tokens = P(None, ("dp", "row"), "col")
    weights = (P("col", "row", "dp"), P("row", "dp", "col"), P("col", ("dp", "row")), P(("dp", "row"), "col"))
    one = P()
    in_specs = (tokens, one, one, one, one, weights[0], one, weights[1], one, weights[2], one, weights[3], one, tokens)
    out_specs = (tokens, tokens, one, one, one, one, weights[0], one, weights[1], one, weights[2], one, weights[3], one)
    return jax.shard_map(body, mesh=mesh, in_specs=in_specs, out_specs=out_specs, check_vma=False)
```

```python
from functools import partial

import jax
import jax.numpy as jnp
import numpy as np
from jax import lax
from jax.experimental import pallas as pl
from jax.experimental.pallas import tpu as pltpu
from jax.sharding import PartitionSpec as P

D = 1024
HS = 64
ROT = 16
HALF = ROT // 2
EPSILON = 1e-05
MASKED = -1e30
NN = (((1,), (0,)), ((), ()))
NT = (((1,), (1,)), ((), ()))
TN = (((0,), (0,)), ((), ()))
VMEM_LIMIT = 56 << 20
F32 = jnp.float32
BF16 = jnp.bfloat16


def mm(a, b, dims):
    return lax.dot_general(a, b, dims, preferred_element_type=F32)


def params(**extra):
    return pltpu.CompilerParams(vmem_limit_bytes=VMEM_LIMIT, **extra)


def cost(flops, nbytes):
    return pl.CostEstimate(flops=int(flops), bytes_accessed=int(nbytes), transcendentals=0)


def whole(shape):
    return pl.BlockSpec(shape, lambda *_: (0,) * len(shape))


MESH = pl.DeviceIdType.MESH
ANYWHERE = pl.BlockSpec(memory_space=pl.ANY)


class Spot:
    def __init__(self):
        self.count = lax.axis_size("dp")
        self.depth = self.count // 2
        self.dp, self.row, self.col = (lax.axis_index(a) for a in ("dp", "row", "col"))
        self.z, self.x = self.dp // 2, self.dp % 2

    def along(self, steps):
        return ((self.z + steps) % self.depth) * 2 + self.x

    def device(self, which):
        return {
            "row": {"row": 1 - self.row},
            "col": {"col": 1 - self.col},
            "x": {"dp": self.z * 2 + (1 - self.x)},
            "right": {"dp": self.along(1)},
            "left": {"dp": self.along(self.depth - 1)},
        }[which]

    def greet(self, *names):
        barrier = pltpu.get_barrier_semaphore()
        for name in names:
            pl.semaphore_signal(barrier, inc=1, device_id=self.device(name), device_id_type=MESH)
        pl.semaphore_wait(barrier, len(names))


def remote(spot, which, source, target, send, recv):
    return pltpu.make_async_remote_copy(
        src_ref=source, dst_ref=target, send_sem=send, recv_sem=recv,
        device_id=spot.device(which), device_id_type=MESH,
    )


class Gather:
    def __init__(self, spot, mine, theirs, all_ref, local, send, recv):
        self.spot, self.all = spot, all_ref
        wide = mine.shape[1]
        here = all_ref.at[spot.dp]
        depth = spot.depth
        self.local = pltpu.make_async_copy(mine, here.at[:, pl.ds(0, wide)], local)
        self.core = remote(spot, "col", theirs, here.at[:, pl.ds(wide, wide)], send.at[0], recv.at[0])
        self.ring, self.cross = [], []
        for k in range(depth):
            slot = all_ref.at[spot.along(depth - k)]
            self.cross.append(remote(spot, "x", slot, slot, send.at[1 + k], recv.at[1 + k]))
            if k < depth - 1:
                at = 1 + depth + k
                self.ring.append(remote(spot, "right", slot, slot, send.at[at], recv.at[at]))

    @staticmethod
    def sems(count):
        return pltpu.SemaphoreType.DMA((count,))

    def begin(self):
        self.local.start()
        self.core.start()

    def first(self):
        self.local.wait()
        self.core.wait_recv()
        self.ring[0].start()
        self.cross[0].start()

    def forward(self, k):
        self.ring[k - 1].wait_recv()
        if k < len(self.ring):
            self.ring[k].start()
        self.cross[k].start()

    def finish(self):
        for copy in self.cross:
            copy.wait_recv()
        for copy in (self.core, *self.ring, *self.cross):
            copy.wait_send()


def enter_kernel(mine, theirs, tokens, all_ref, xb, xc, xd, local, send, recv, y_send, y_recv, c_send, c_recv, *, chunks):
    spot = Spot()
    spot.greet("row", "col", "x", "right", "left")
    gather = Gather(spot, mine, theirs, all_ref, local, send, recv)
    size = xb.shape[0] // chunks
    part = lambda k: pl.ds(k * size, size)
    over_row = [
        remote(spot, "row", tokens.at[0, part(k)], xb.at[part(k)], y_send.at[k], y_recv.at[k]) for k in range(chunks)
    ]
    over_col = [
        remote(spot, "col", xb.at[part(k)], xd.at[part(k)], c_send.at[k], c_recv.at[k]) for k in range(chunks)
    ]
    core = remote(spot, "col", tokens, xc, c_send.at[chunks], c_recv.at[chunks])
    gather.begin()
    for copy in over_row:
        copy.start()
    gather.first()
    core.start()
    depth = spot.depth
    for k in range(max(depth - 1, chunks)):
        if k + 1 < depth:
            gather.forward(k + 1)
        if k < chunks:
            over_row[k].wait_recv()
            over_col[k].start()
    gather.finish()
    core.wait()
    for k in range(chunks):
        over_col[k].wait()
        over_row[k].wait_send()


def enter(mine, theirs, tokens, count, chunks=4):
    rows, wide = mine.shape
    micros, length, _ = tokens.shape
    depth = count // 2
    half = jax.ShapeDtypeStruct((length, wide), BF16)
    return pl.pallas_call(
        partial(enter_kernel, chunks=chunks),
        in_specs=[ANYWHERE] * 3,
        out_specs=[ANYWHERE] * 4,
        out_shape=[
            jax.ShapeDtypeStruct((count, rows, 2 * wide), BF16), half,
            jax.ShapeDtypeStruct(tokens.shape, BF16), half,
        ],
        scratch_shapes=[
            pltpu.SemaphoreType.DMA, Gather.sems(2 * depth), Gather.sems(2 * depth),
            Gather.sems(chunks), Gather.sems(chunks), Gather.sems(chunks + 1), Gather.sems(chunks + 1),
        ],
        compiler_params=pltpu.CompilerParams(collective_id=0, has_side_effects=True),
        name="enter",
    )(mine, theirs, tokens)


def forward_kernel(
    xa, xc, xb0, xd0, weight, bias, vectors, cosine, sine, mine, theirs, tokens, grads,
    first, second, triple, att_own, att_far, logsum, all_ref, xb1, xd1, cb0, cc, cd0,
    x_s, q_s, v_s, o_s, n_s, f_s, local, send, recv, y_send, y_recv, c_send, c_recv, t_sem, l_sem, *, block, step,
):
    spot = Spot()
    now = pl.program_id(0)
    wide = xa.shape[2]
    width = 2 * wide
    own_tokens = tokens.shape[1]
    length = 2 * own_tokens
    blocks = own_tokens // block
    heads = weight.shape[0] // (3 * HS)
    depth = spot.depth
    attend0, far1, attend1 = 3 * blocks, 3 * blocks + heads, 4 * blocks + heads
    end = attend1 + heads - 1
    here, there = spot.row, 1 - spot.row

    gather = Gather(spot, mine, theirs, all_ref, local, send, recv)
    x_row = remote(spot, "row", tokens.at[1], xb1, y_send.at[0], y_recv.at[0])
    x_col = remote(spot, "col", xb1, xd1, c_send.at[0], c_recv.at[0])
    g_row = remote(spot, "row", grads.at[0], cb0, y_send.at[1], y_recv.at[1])
    g_col = remote(spot, "col", cb0, cd0, c_send.at[1], c_recv.at[1])
    g_core = remote(spot, "col", grads, cc, c_send.at[2], c_recv.at[2])
    load_near = pltpu.make_async_copy(xb1, n_s, l_sem.at[0])
    load_far = pltpu.make_async_copy(xd1, f_s, l_sem.at[1])
    keep = [pltpu.make_async_copy(q_s.at[m], triple.at[m], t_sem.at[m]) for m in range(2)]

    at = lambda k: pl.when(now == k)

    @at(0)
    def _():
        spot.greet("row", "col", "x", "right", "left")
        gather.begin()
        x_row.start()

    @at(1)
    def _():
        gather.first()
        g_core.start()

    for k in range(1, depth):
        moment = attend0 + 1 + (k - 1) * 5 // 2 if depth == 4 else far1 + blocks

        @at(moment)
        def _():
            gather.forward(k)

    @at(attend0)
    def _():
        keep_row = x_row
        keep_row.wait_recv()
        x_col.start()
        g_row.start()

    @at(attend0 + 1)
    def _():
        x_col.wait_recv()
        load_near.start()
        load_far.start()

    @at(far1)
    def _():
        load_near.wait()
        load_far.wait()

    @at(end - 1)
    def _():
        g_row.wait_recv()
        g_col.start()

    @pl.when(now < 2 * blocks)
    def _():
        x_s[:, :wide] = xa[0]
        x_s[:, wide:] = xc[0]

    @pl.when((now >= 2 * blocks) & (now < attend0))
    def _():
        x_s[:, :wide] = xb0[...]
        x_s[:, wide:] = xd0[...]

    for k in range(blocks):
        @at(far1 + k)
        def _():
            x_s[:, :wide] = n_s[k * block : (k + 1) * block]
            x_s[:, wide:] = f_s[k * block : (k + 1) * block]

    project = (now < attend0) | ((now >= far1) & (now < attend1))

    @pl.when(project)
    def _():
        micro = jnp.where(now < blocks, 0, jnp.where(now < 2 * blocks, 1, jnp.where(now < attend0, 0, 1)))
        half = jnp.where(now < 2 * blocks, here, there)
        number = jnp.where(now < attend0, now % blocks, (now - far1) % blocks)
        lane = pl.ds(pl.multiple_of(half * own_tokens + number * block, block), block)
        values = x_s[...].astype(F32)
        center = jnp.sum(values, axis=1, keepdims=True) / width
        spread = jnp.sum(values * values, axis=1, keepdims=True) / width - center * center
        normed = (values - center) * lax.rsqrt(spread + EPSILON)
        first[0, 0] = (normed * vectors[0:1, :] + vectors[1:2, :]).astype(BF16)
        second[0, 0] = (normed * vectors[2:3, :] + vectors[3:4, :]).astype(BF16)
        cos, sin = cosine[:, lane], sine[:, lane]
        for head in range(heads):
            base = head * 3 * HS
            rows = mm(weight[base : base + 3 * HS, :], first[0, 0], NT) + bias[base : base + 3 * HS, :]
            pieces = []
            for which in range(2):
                lo = which * HS
                scale = HS ** (-0.5) if which == 0 else 1.0
                u1, u2 = rows[lo : lo + HALF], rows[lo + HALF : lo + ROT]
                pieces += [(u1 * cos - u2 * sin) * scale, (u2 * cos + u1 * sin) * scale, rows[lo + ROT : lo + HS] * scale]
            pieces.append(rows[2 * HS :])
            q_s[micro, base : base + 3 * HS, lane] = jnp.concatenate(pieces, axis=0).astype(BF16)

    @at(attend0)
    def _():
        keep[0].start()

    @at(attend1)
    def _():
        keep[1].start()

    attending = ((now >= attend0) & (now < far1)) | (now >= attend1)

    @pl.when(attending)
    def _():
        micro = jnp.where(now < far1, 0, 1)
        head = jnp.where(now < far1, now - attend0, now - attend1)
        base = pl.multiple_of(head * 3 * HS, HS)
        query_of = lambda lo, hi: q_s[micro, pl.ds(base, HS), lo:hi]
        keys_of = lambda lo, hi: q_s[micro, pl.ds(pl.multiple_of(base + HS, HS), HS), lo:hi]
        v_s[0:HS, :] = q_s[micro, pl.ds(pl.multiple_of(base + 2 * HS, HS), HS), :]
        extra = lax.broadcasted_iota(jnp.int32, (16, length), 0)
        v_s[HS : HS + 16, :] = jnp.where(extra == 0, 1.0, 0.0).astype(BF16)
        allowed = causal_tile(step)
        for i in range(length // step):
            lo, hi = i * step, (i + 1) * step
            query = query_of(lo, hi)
            diag = jnp.where(allowed, mm(keys_of(lo, hi), query, TN), MASKED)
            highest = jnp.max(diag, axis=0, keepdims=True)
            if i:
                past = mm(keys_of(0, lo), query, TN)
                highest = jnp.maximum(highest, jnp.max(past, axis=0, keepdims=True))
            raised = jnp.exp(diag - highest).astype(BF16)
            result = mm(v_s[:, lo:hi], raised, NN)
            if i:
                raised = jnp.exp(past - highest).astype(BF16)
                result = result + mm(v_s[:, :lo], raised, NN)
            total = result[HS : HS + 1]
            o_s[:, lo:hi] = (result[:HS] / total).astype(BF16)
            logsum[0, 0, :, lo:hi] = highest + jnp.log(total)
        att_own[0] = o_s[:, lanes(here, own_tokens)]
        att_far[0] = o_s[:, lanes(there, own_tokens)]

    @at(end)
    def _():
        gather.finish()
        g_col.wait()
        g_core.wait()
        x_col.wait_send()
        x_row.wait_send()
        g_row.wait_send()
        keep[0].wait()
        keep[1].wait()


def lanes(index, tokens):
    return pl.ds(pl.multiple_of(index * tokens, tokens), tokens)


def forward(residual, xc, xb0, xd0, weight, bias, vectors, cosine, sine, mine, theirs, cotangent, count, block=512, step=512):
    micros, tokens, wide = residual.shape
    width, length = 2 * wide, 2 * tokens
    block, step = min(block, tokens), min(step, length)
    blocks = tokens // block
    rows = weight.shape[0]
    heads = rows // (3 * HS)
    depth = count // 2
    a0, f1, a1 = 3 * blocks, 3 * blocks + heads, 4 * blocks + heads
    steps = a1 + heads
    clip = lambda v, lo, hi: jnp.minimum(jnp.maximum(v, lo), hi)
    own = pl.BlockSpec((1, block, wide), lambda i: (jnp.where(i < blocks, 0, 1), jnp.where(i < 2 * blocks, i % blocks, blocks - 1), 0))
    far = pl.BlockSpec((block, wide), lambda i: (clip(i - 2 * blocks, 0, blocks - 1), 0))

    def place(i):
        late = i >= f1
        micro = jnp.where(i < blocks, 0, jnp.where(i < 2 * blocks, 1, jnp.where(late, 1, 0)))
        half = jnp.where(i < 2 * blocks, 1, 0)
        number = jnp.where(i < 2 * blocks, i % blocks, jnp.where(late, clip(i - f1, 0, blocks - 1), clip(i - 2 * blocks, 0, blocks - 1)))
        return micro, half, number, 0

    def head_of(i):
        late = i >= a1
        return jnp.where(late, 1, 0), jnp.where(late, i - a1, clip(i - a0, 0, heads - 1))

    normal = pl.BlockSpec((1, 1, block, width), place)
    att = pl.BlockSpec((1, HS, tokens), lambda i: (*head_of(i), 0))
    half = jax.ShapeDtypeStruct((tokens, wide), BF16)
    piece = mine.shape[0]
    return pl.pallas_call(
        partial(forward_kernel, block=block, step=step),
        grid=(steps,),
        in_specs=[
            own, own, far, far, whole(weight.shape), whole(bias.shape), whole(vectors.shape),
            whole(cosine.shape), whole(sine.shape), ANYWHERE, ANYWHERE, ANYWHERE, ANYWHERE,
        ],
        out_specs=[
            normal, normal, ANYWHERE, att, att, pl.BlockSpec((1, 1, 1, length), lambda i: (*head_of(i), 0, 0)),
            *[ANYWHERE] * 6,
        ],
        out_shape=[
            jax.ShapeDtypeStruct((micros, 2, tokens, width), BF16),
            jax.ShapeDtypeStruct((micros, 2, tokens, width), BF16),
            jax.ShapeDtypeStruct((micros, rows, length), BF16),
            jax.ShapeDtypeStruct((micros, heads * HS, tokens), BF16),
            jax.ShapeDtypeStruct((micros, heads * HS, tokens), BF16),
            jax.ShapeDtypeStruct((micros, heads, 1, length), F32),
            jax.ShapeDtypeStruct((count, piece, width), BF16),
            half, half, half, jax.ShapeDtypeStruct(cotangent.shape, BF16), half,
        ],
        scratch_shapes=[
            pltpu.VMEM((block, width), BF16),
            pltpu.VMEM((micros, rows, length), BF16),
            pltpu.VMEM((HS + 16, length), BF16),
            pltpu.VMEM((HS, length), BF16),
            pltpu.VMEM((tokens, wide), BF16),
            pltpu.VMEM((tokens, wide), BF16),
            pltpu.SemaphoreType.DMA, Gather.sems(2 * depth), Gather.sems(2 * depth),
            Gather.sems(2), Gather.sems(2), Gather.sems(3), Gather.sems(3), Gather.sems(2), Gather.sems(2),
        ],
        compiler_params=params(collective_id=1, has_side_effects=True),
        cost_estimate=cost(micros * length * width * rows * 2 + micros * heads * length * length * 256 * 2, 40 << 20),
        name="forward",
    )(residual, xc, xb0, xd0, weight, bias, vectors, cosine, sine, mine, theirs, residual, cotangent)
def causal_tile(size):
    keys = lax.broadcasted_iota(jnp.int32, (size, size), 0)
    places = lax.broadcasted_iota(jnp.int32, (size, size), 1)
    return keys <= places


def lanes(index, tokens):
    return pl.ds(pl.multiple_of(index * tokens, tokens), tokens)


POLY = (0.254829592, -0.284496736, 1.421413741, -1.453152027, 1.061405429)


def gelu_pair(value):
    magnitude = jnp.abs(value)
    t = 1.0 / (1.0 + magnitude * (0.3275911 * 0.5**0.5))
    bell = jnp.exp(value * value * -0.5)
    series = POLY[4]
    for term in (POLY[3], POLY[2], POLY[1], POLY[0]):
        series = series * t + term
    tail = 0.5 * series * t * bell
    cumulative = jnp.where(value >= 0.0, 1.0 - tail, tail)
    return value * cumulative, cumulative + value * bell * (1.0 / (2.0 * np.pi) ** 0.5)


def middle_kernel(
    second, ca, cc, cb0, cd0, att_own, att_far, pieces, wo, bias, grads,
    out_near, out_other, heads_own, heads_far, part, tiles, dbias, cb1, cd1,
    w1, w2, dw1, dw2, dwo, n_s, f_s, c_s, a_s, act_s, eg_s, w_sem, l_sem, y_send, y_recv, c_send, c_recv,
    *, block, chunk, out_part,
):
    spot = Spot()
    micro, half, at = pl.program_id(0), pl.program_id(1), pl.program_id(2)
    wide = ca.shape[2]
    count, rows, width = pieces.shape
    hid = w1.shape[0] // count
    heads = wo.shape[0] // HS
    steps = pl.num_programs(2)
    starting = (micro == 0) & (half == 0) & (at == 0)
    moment = micro * 2 * steps + half * steps + at
    g_row = remote(spot, "row", grads.at[1], cb1, y_send, y_recv)
    g_col = remote(spot, "col", cb1, cd1, c_send, c_recv)
    load_near = pltpu.make_async_copy(cb1, n_s, l_sem.at[0])
    load_far = pltpu.make_async_copy(cd1, f_s, l_sem.at[1])

    @pl.when(starting)
    def _():
        spot.greet("row", "col")
        g_row.start()
        lo = heads * out_part
        copies = []
        for p in range(count):
            here = slice(p * hid, (p + 1) * hid)
            copies.append(pltpu.make_async_copy(pieces.at[p, lo : lo + hid], w1.at[here], w_sem.at[2 * p]))
            copies.append(pltpu.make_async_copy(pieces.at[p, lo + hid :], w2.at[here], w_sem.at[2 * p + 1]))
        for copy in copies:
            copy.start()
        dw1[...] = jnp.zeros_like(dw1)
        dw2[...] = jnp.zeros_like(dw2)
        dwo[...] = jnp.zeros_like(dwo)
        dbias[...] = jnp.zeros_like(dbias)
        for copy in copies:
            copy.wait()

    @pl.when(moment == 2 * steps - 2)
    def _():
        g_row.wait_recv()
        g_col.start()

    @pl.when(moment == 2 * steps - 1)
    def _():
        g_col.wait_recv()
        load_near.start()
        load_far.start()

    @pl.when(moment == 2 * steps)
    def _():
        load_near.wait()
        load_far.wait()

    @pl.when((half == 0) & (micro == 0))
    def _():
        c_s[:, :wide] = cb0[...]
        c_s[:, wide:] = cd0[...]

    @pl.when((half == 0) & (micro == 1))
    def _():
        here = pl.ds(pl.multiple_of(at * block, block), block)
        c_s[:, :wide] = n_s[here, :]
        c_s[:, wide:] = f_s[here, :]

    @pl.when(half == 1)
    def _():
        c_s[:, :wide] = ca[0]
        c_s[:, wide:] = cc[0]
        a_s[...] = att_own[0]

    @pl.when(half == 0)
    def _():
        a_s[...] = att_far[0]

    hidden = w1.shape[0]
    for lo in range(0, hidden, chunk):
        hi = lo + chunk
        expanded = mm(second[0, 0], w1[lo:hi, :], NT) + bias[:, lo:hi]
        active, slope = gelu_pair(expanded)
        act_s[:, lo:hi] = active.astype(BF16)
        rounded = (mm(c_s[...], w2[lo:hi, :], NT) * slope).astype(BF16)
        eg_s[:, lo:hi] = rounded
        dbias[:, lo:hi] += jnp.sum(rounded.astype(F32), axis=0, keepdims=True)
    for lo in range(0, hidden, chunk):
        hi = lo + chunk
        dw2[lo:hi, :] += mm(act_s[:, lo:hi], c_s[...], TN)
        dw1[lo:hi, :] += mm(eg_s[:, lo:hi], second[0, 0], TN)
    dwo[...] += mm(a_s[...], c_s[...], NN)
    out_near[0, 0] = (mm(act_s[...], w2[:, :wide], NN) + mm(a_s[...], wo[:, :wide], TN)).astype(BF16)
    out_other[0, 0] = (mm(act_s[...], w2[:, wide:], NN) + mm(a_s[...], wo[:, wide:], TN)).astype(BF16)
    part[0, 0] = mm(eg_s[...], w1[...], NN).astype(BF16)
    heads_grad = mm(wo[...], c_s[...], NT).astype(BF16)

    @pl.when(half == 0)
    def _():
        heads_far[0] = heads_grad

    @pl.when(half == 1)
    def _():
        heads_own[0] = heads_grad

    @pl.when(moment == 4 * steps - 1)
    def _():
        lo = heads * out_part
        for p in range(count):
            here = slice(p * hid, (p + 1) * hid)
            small = [dwo[h * HS + p * out_part : h * HS + (p + 1) * out_part, :] for h in range(heads)]
            tiles[p, :lo] = jnp.concatenate(small, axis=0).astype(BF16)
            tiles[p, lo : lo + hid] = dw1[here, :].astype(BF16)
            tiles[p, lo + hid :] = dw2[here, :].astype(BF16)
        g_row.wait_send()
        g_col.wait_send()


def middle(second, cotangent, cc, cb0, cd0, att_own, att_far, pieces, wo, bias, block=256, chunk=256):
    micros, tokens, wide = cotangent.shape
    count, rows, width = pieces.shape
    block = min(block, tokens)
    steps = tokens // block
    hidden, head_rows = bias.shape[1], wo.shape[0]
    hid = hidden // count
    out_part = (rows - 2 * hid) * HS // head_rows
    end = steps - 1
    both = lambda n: pl.BlockSpec((1, 1, block, n), lambda m, h, i: (m, h, i, 0))
    own_at = lambda m, h, i: (m, h * i)
    far_at = lambda m, h, i: (m, i * (1 - h) + end * h)
    own = pl.BlockSpec((1, block, wide), lambda m, h, i: (*own_at(m, h, i), 0))
    far0 = pl.BlockSpec((block, wide), lambda m, h, i: (jnp.where((m == 0) & (h == 0), i, end), 0))
    cols_own = pl.BlockSpec((1, head_rows, block), lambda m, h, i: (m, 0, h * i))
    cols_far = pl.BlockSpec((1, head_rows, block), lambda m, h, i: (m, 0, i * (1 - h) + end * h))
    halves = jax.ShapeDtypeStruct((tokens, wide), BF16)
    return pl.pallas_call(
        partial(middle_kernel, block=block, chunk=min(chunk, hidden), out_part=out_part),
        grid=(micros, 2, steps),
        in_specs=[
            both(width), own, own, far0, far0, cols_own, cols_far, ANYWHERE, whole(wo.shape), whole(bias.shape), ANYWHERE,
        ],
        out_specs=[
            both(wide), both(wide), cols_own, cols_far, both(width), whole(pieces.shape), whole(bias.shape),
            ANYWHERE, ANYWHERE,
        ],
        out_shape=[
            jax.ShapeDtypeStruct((micros, 2, tokens, wide), BF16),
            jax.ShapeDtypeStruct((micros, 2, tokens, wide), BF16),
            jax.ShapeDtypeStruct((micros, head_rows, tokens), BF16),
            jax.ShapeDtypeStruct((micros, head_rows, tokens), BF16),
            jax.ShapeDtypeStruct((micros, 2, tokens, width), BF16),
            jax.ShapeDtypeStruct(pieces.shape, BF16),
            jax.ShapeDtypeStruct(bias.shape, F32),
            halves, halves,
        ],
        scratch_shapes=[
            pltpu.VMEM((hidden, width), BF16),
            pltpu.VMEM((hidden, width), BF16),
            pltpu.VMEM((hidden, width), F32),
            pltpu.VMEM((hidden, width), F32),
            pltpu.VMEM((head_rows, width), F32),
            pltpu.VMEM((tokens, wide), BF16),
            pltpu.VMEM((tokens, wide), BF16),
            pltpu.VMEM((block, width), BF16),
            pltpu.VMEM((head_rows, block), BF16),
            pltpu.VMEM((block, hidden), BF16),
            pltpu.VMEM((block, hidden), BF16),
            Gather.sems(2 * count), Gather.sems(2),
            pltpu.SemaphoreType.DMA, pltpu.SemaphoreType.DMA, pltpu.SemaphoreType.DMA, pltpu.SemaphoreType.DMA,
        ],
        compiler_params=params(collective_id=2, has_side_effects=True),
        cost_estimate=cost(2 * micros * tokens * 2 * width * (6 * hidden + 3 * head_rows), 80 << 20),
        name="middle",
    )(second, cotangent, cc, cb0, cd0, att_own, att_far, pieces, wo, bias, cotangent)


def attend_back_kernel(
    triple, grad_own, grad_far, att_own, att_far, logsum, cosine, sine,
    out_own, out_far, bias_grad, g_s, delta_s, dq_s, dk_s, dv_s, t_s, *, step,
):
    tokens = grad_own.shape[2]
    length = 2 * tokens
    here = lax.axis_index("row")
    there = 1 - here
    for grad, att, place in ((grad_own, att_own, here), (grad_far, att_far, there)):
        at = lanes(place, tokens)
        g_s[:, at] = grad[0]
        delta_s[:, at] = jnp.sum(grad[0].astype(F32) * att[0].astype(F32), axis=0, keepdims=True)
    q_s, k_s, v_s = (triple.at[0, i * HS : (i + 1) * HS] for i in range(3))
    dk_s[...] = jnp.zeros_like(dk_s)
    dv_s[...] = jnp.zeros_like(dv_s)
    allowed = causal_tile(step)
    for i in range(length // step):
        lo, hi = i * step, (i + 1) * step
        query, grad = q_s[:, lo:hi], g_s[:, lo:hi]
        base, delta = logsum[0, 0, :, lo:hi], delta_s[:, lo:hi]
        query_grad = None
        for begin, end in ((0, lo), (lo, hi)):
            if end == begin:
                continue
            raised = jnp.exp(mm(k_s[:, begin:end], query, TN) - base)
            if begin == lo:
                raised = jnp.where(allowed, raised, 0.0)
            prob_grad = mm(v_s[:, begin:end], grad, TN)
            score_grad = (raised * (prob_grad - delta)).astype(BF16)
            dv_s[:, begin:end] += mm(grad, raised.astype(BF16), NT)
            dk_s[:, begin:end] += mm(query, score_grad, NT)
            term = mm(k_s[:, begin:end], score_grad, NN)
            query_grad = term if query_grad is None else query_grad + term
        dq_s[:, lo:hi] = query_grad * HS ** (-0.5)
    cos, sin = cosine[...], sine[...]
    for which, ref in ((0, dq_s), (1, dk_s)):
        g1, g2 = ref[0:HALF, :], ref[HALF:ROT, :]
        spun = jnp.concatenate([g1 * cos + g2 * sin, g2 * cos - g1 * sin], axis=0)
        t_s[which * HS : which * HS + ROT, :] = spun.astype(BF16)
        t_s[which * HS + ROT : (which + 1) * HS, :] = ref[ROT:HS, :].astype(BF16)
    t_s[2 * HS : 3 * HS, :] = dv_s[...].astype(BF16)
    bias_grad[...] = jnp.sum(t_s[...].astype(F32), axis=1, keepdims=True)
    out_own[...] = t_s[:, lanes(here, tokens)]
    out_far[...] = t_s[:, lanes(there, tokens)]


def attend_back(micro, triple, grad_own, grad_far, att_own, att_far, logsum, cosine, sine, step=256):
    _, rows, length = triple.shape
    tokens = length // 2
    heads = rows // (3 * HS)
    narrow = pl.BlockSpec((1, HS, tokens), lambda h: (micro, h, 0))
    result = pl.BlockSpec((3 * HS, tokens), lambda h: (h, 0))
    table = whole((HALF, length))
    return pl.pallas_call(
        partial(attend_back_kernel, step=min(step, length)),
        grid=(heads,),
        in_specs=[
            pl.BlockSpec((1, 3 * HS, length), lambda h: (micro, h, 0)), narrow, narrow, narrow, narrow,
            pl.BlockSpec((1, 1, 1, length), lambda h: (micro, h, 0, 0)), table, table,
        ],
        out_specs=[result, result, pl.BlockSpec((3 * HS, 1), lambda h: (h, 0))],
        out_shape=[
            jax.ShapeDtypeStruct((rows, tokens), BF16),
            jax.ShapeDtypeStruct((rows, tokens), BF16),
            jax.ShapeDtypeStruct((rows, 1), F32),
        ],
        scratch_shapes=[
            pltpu.VMEM((HS, length), BF16),
            pltpu.VMEM((1, length), F32),
            pltpu.VMEM((HS, length), F32),
            pltpu.VMEM((HS, length), F32),
            pltpu.VMEM((HS, length), F32),
            pltpu.VMEM((3 * HS, length), BF16),
        ],
        compiler_params=params(),
        cost_estimate=cost(heads * length * length * 256 * 5, 16 * rows * tokens),
        name="attend_back",
    )(triple, grad_own, grad_far, att_own, att_far, logsum, cosine, sine)


def last_kernel(
    t_own, t_far, first, part, xa, xb, xc, xd, weight, vectors, before,
    ng_near, ng_other, sums, result, dvec, total, t_s, x_s, *, final, count,
):
    half, at = pl.program_id(0), pl.program_id(1)
    wide = xb.shape[1]
    width = 2 * wide
    steps = pl.num_programs(1)

    @pl.when((half == 0) & (at == 0))
    def _():
        if final:
            total[...] = before[...]
        else:
            total[...] = jnp.zeros_like(total)
        dvec[...] = jnp.zeros_like(dvec)

    @pl.when(half == 0)
    def _():
        t_s[...] = t_far[...]
        x_s[:, :wide] = xb[...]
        x_s[:, wide:] = xd[...]

    @pl.when(half == 1)
    def _():
        t_s[...] = t_own[...]
        x_s[:, :wide] = xa[0]
        x_s[:, wide:] = xc[0]

    total[...] += mm(t_s[...], first[0, 0], NN)
    values = x_s[...].astype(F32)
    center = jnp.sum(values, axis=1, keepdims=True) / width
    spread = jnp.sum(values * values, axis=1, keepdims=True) / width - center * center
    inv = lax.rsqrt(spread + EPSILON)
    first_sum = second_sum = 0.0
    for side, ref in ((0, ng_near), (1, ng_other)):
        cols = slice(side * wide, (side + 1) * wide)
        normed = (x_s[:, cols].astype(F32) - center) * inv
        first_grad = mm(t_s[...], weight[:, cols], TN)
        second_grad = part[0, 0, :, cols].astype(F32)
        dvec[0:1, cols] += jnp.sum(first_grad * normed, axis=0, keepdims=True)
        dvec[1:2, cols] += jnp.sum(first_grad, axis=0, keepdims=True)
        dvec[2:3, cols] += jnp.sum(second_grad * normed, axis=0, keepdims=True)
        dvec[3:4, cols] += jnp.sum(second_grad, axis=0, keepdims=True)
        grad = first_grad * vectors[0:1, cols] + second_grad * vectors[2:3, cols]
        first_sum = first_sum + jnp.sum(grad, axis=1, keepdims=True)
        second_sum = second_sum + jnp.sum(grad * normed, axis=1, keepdims=True)
        ref[0] = grad.astype(BF16)
    column = lax.broadcasted_iota(jnp.int32, (x_s.shape[0], 128), 1)
    both = jnp.where(column == 0, first_sum, jnp.where(column == 1, second_sum, 0.0))
    sums[0] = jnp.transpose(both)[0:8, :]

    @pl.when((half == 1) & (at == steps - 1))
    def _():
        if final:
            heads = total.shape[0] // (3 * HS)
            size = 3 * HS // count
            for p in range(count):
                small = [total[h * 3 * HS + p * size : h * 3 * HS + (p + 1) * size, :] for h in range(heads)]
                result[p] = jnp.concatenate(small, axis=0).astype(BF16)
        else:
            result[...] = total[...]


def last(micro, t_own, t_far, first, part, residual, xb, xc, xd, weight, vectors, before, count, block=256):
    _, tokens, wide = residual.shape
    width = 2 * wide
    block = min(block, tokens)
    steps = tokens // block
    rows = weight.shape[0]
    end = steps - 1
    far_at = lambda h, i: i * (1 - h) + end * h
    own_at = lambda h, i: i * h
    own = pl.BlockSpec((1, block, wide), lambda h, i: (micro, own_at(h, i), 0))
    far = pl.BlockSpec((block, wide), lambda h, i: (far_at(h, i), 0))
    both = lambda n: pl.BlockSpec((1, 1, block, n), lambda h, i: (micro, h, i, 0))
    out = pl.BlockSpec((1, block, wide), lambda h, i: (h, i, 0))
    final = before is not None
    shape = jax.ShapeDtypeStruct((count, rows // count, width), BF16) if final else jax.ShapeDtypeStruct((rows, width), F32)
    before = before if final else jnp.zeros((8, 128), F32)
    return pl.pallas_call(
        partial(last_kernel, final=final, count=count),
        grid=(2, steps),
        in_specs=[
            pl.BlockSpec((rows, block), lambda h, i: (0, own_at(h, i))),
            pl.BlockSpec((rows, block), lambda h, i: (0, far_at(h, i))),
            both(width), both(width), own, far, own, far,
            whole(weight.shape), whole(vectors.shape), whole(before.shape),
        ],
        out_specs=[
            out, out, pl.BlockSpec((1, 8, block), lambda h, i: (h, 0, i)), whole(shape.shape), whole((8, width)),
        ],
        out_shape=[
            jax.ShapeDtypeStruct((2, tokens, wide), BF16),
            jax.ShapeDtypeStruct((2, tokens, wide), BF16),
            jax.ShapeDtypeStruct((2, 8, tokens), F32),
            shape,
            jax.ShapeDtypeStruct((8, width), F32),
        ],
        scratch_shapes=[
            pltpu.VMEM((rows, width), F32),
            pltpu.VMEM((rows, block), BF16),
            pltpu.VMEM((block, width), BF16),
        ],
        compiler_params=params(),
        cost_estimate=cost(2 * tokens * 2 * width * 2 * rows, 2 * tokens * width * 10),
        name="last",
    )(t_own, t_far, first, part, residual, xb, xc, xd, weight, vectors, before)


def total_kernel(value, out, held, arrived, send, recv):
    spot = Spot()
    partners = [{"col": 1 - spot.col}, {"row": 1 - spot.row}, {"dp": spot.z * 2 + (1 - spot.x)}]
    stride = 1
    while stride < spot.depth:
        other = spot.z + stride * (1 - 2 * ((spot.z // stride) % 2))
        partners.append({"dp": other * 2 + spot.x})
        stride *= 2
    barrier = pltpu.get_barrier_semaphore()
    for partner in partners:
        pl.semaphore_signal(barrier, inc=1, device_id=partner, device_id_type=MESH)
    pl.semaphore_wait(barrier, len(partners))
    held[0] = value[...]
    for k, partner in enumerate(partners):
        copy = pltpu.make_async_remote_copy(
            src_ref=held.at[k], dst_ref=arrived.at[k], send_sem=send.at[k], recv_sem=recv.at[k],
            device_id=partner, device_id_type=MESH,
        )
        copy.start()
        copy.wait()
        if k + 1 < len(partners):
            held[k + 1] = held[k] + arrived[k]
        else:
            out[...] = held[k] + arrived[k]


def total_of(value, count):
    hops = 3 + max(count // 2 - 1, 0).bit_length()
    vmem = pl.BlockSpec(memory_space=pltpu.VMEM)
    return pl.pallas_call(
        total_kernel,
        in_specs=[vmem],
        out_specs=vmem,
        out_shape=jax.ShapeDtypeStruct(value.shape, F32),
        scratch_shapes=[
            pltpu.VMEM((hops, *value.shape), F32), pltpu.VMEM((hops, *value.shape), F32),
            Gather.sems(hops), Gather.sems(hops),
        ],
        compiler_params=pltpu.CompilerParams(collective_id=3, has_side_effects=True),
        name="total",
    )(value)


def swap(value, axis):
    return lax.ppermute(value, axis, [(0, 1), (1, 0)])


def across(value, count):
    return lax.ppermute(value, "dp", [(i, i ^ 1) for i in range(count)])


def shifted(value, steps, count):
    return lax.ppermute(value, "dp", [(i, (i + 2 * steps) % count) for i in range(count)])


def pick(value, index, axis=0):
    return lax.dynamic_index_in_dim(value, index, axis, keepdims=False)


def rows_from_cores(mine, col):
    wide = mine.shape[-1] // 2
    other = swap(mine[..., wide:], "col")
    mine = mine[..., :wide]
    return jnp.where(col == 0, jnp.concatenate([mine, other], 0), jnp.concatenate([other, mine], 0))


def body(
    residual, attend_norm_gain, attend_norm_bias, expand_norm_gain, expand_norm_bias,
    attend_weight, attend_bias, output_weight, output_bias, expand_weight, expand_bias,
    shrink_weight, shrink_bias, cotangent,
):
    count = lax.axis_size("dp")
    depth = count // 2
    row, col, dp = lax.axis_index("row"), lax.axis_index("col"), lax.axis_index("dp")
    place_z, place_x = dp // 2, dp % 2
    micros, tokens, wide = residual.shape
    width, length = 2 * wide, 2 * tokens
    heads = attend_weight.shape[1] // 2
    head_part, out_part = attend_weight.shape[2], output_weight.shape[1]
    hid = expand_weight.shape[1] // 2

    def sides(rows):
        return pick(rows, col), pick(rows, 1 - col)

    head_mine, head_theirs = sides(attend_weight.transpose(1, 2, 0).reshape(2, heads * head_part, wide))
    rest_mine, rest_theirs = sides(
        jnp.concatenate(
            [
                output_weight.reshape(2, heads * out_part, wide),
                expand_weight.T.reshape(2, hid, wide),
                shrink_weight.reshape(2, hid, wide),
            ],
            axis=1,
        )
    )
    head_all, xb0, xc, xd0 = enter(head_mine, head_theirs, residual, count)
    wq = head_all.reshape(count, heads, head_part, width).transpose(1, 0, 2, 3).reshape(heads * 3 * HS, width)

    vectors = jnp.stack([attend_norm_gain, attend_norm_bias, expand_norm_gain, expand_norm_bias])
    vectors = jnp.concatenate([jnp.roll(vectors, -col * wide, axis=1), jnp.zeros((4, width), F32)])
    head_begin = row * 2 * heads + col * heads
    bias_q = lax.dynamic_slice_in_dim(attend_bias, head_begin, heads, 0).reshape(-1, 1)
    bias_1 = pick(expand_bias.reshape(count, 4, hid), row * 2 + col, 1).reshape(1, -1)
    out_bias = lax.dynamic_slice_in_dim(output_bias + shrink_bias, col * wide, wide, 0)
    powers = 10000.0 ** (-np.arange(HALF) * (2.0 / ROT))
    angles = powers[:, None] * np.arange(length)[None, :]
    cosine, sine = jnp.asarray(np.cos(angles), F32), jnp.asarray(np.sin(angles), F32)

    first, second, triple, att_own, att_far, logsum, pieces, xb1, xd1, cb0, cc, cd0 = forward(
        residual, xc, xb0, xd0, wq, bias_q, vectors, cosine, sine, rest_mine, rest_theirs, cotangent, count
    )
    lo = heads * out_part
    wo = pieces[:, :lo].reshape(count, heads, out_part, width).transpose(1, 0, 2, 3).reshape(heads * HS, width)
    near, other, heads_own, heads_far, part, tiles, db1, cb1, cd1 = middle(
        second, cotangent, cc, cb0, cd0, att_own, att_far, pieces, wo, bias_1
    )

    crossed = swap(other, "col")
    tiles = tiles.reshape(depth, 2, *tiles.shape[1:])
    tiles_away = pick(tiles, 1 - place_x, 1)
    heads_own, tiles_away = lax.optimization_barrier((heads_own, tiles_away))
    moved = swap((near[:, 0].astype(F32) + crossed[:, 0].astype(F32)).astype(BF16), "row")
    tiles_back = across(tiles_away, count)

    def norm_back(micro, xb, xd, before, heads_own):
        t_own, t_far, bias_grad = attend_back(
            micro, triple, heads_own, heads_far, att_own, att_far, logsum, cosine, sine
        )
        return bias_grad, last(micro, t_own, t_far, first, part, residual, xb, xc, xd, wq, vectors, before, count)

    def input_grad(micro, near, other, sums):
        crossed = swap(other, "col")
        moved = swap((near[0].astype(F32) + crossed[0].astype(F32)).astype(BF16), "row")
        sums = sums + swap(sums, "col")
        sums = sums[1] + swap(sums[0], "row")
        grad = near[1].astype(F32) + crossed[1].astype(F32) + moved.astype(F32)
        near_x, far_x = residual[micro].astype(F32), xc[micro].astype(F32)
        center = (jnp.sum(near_x, 1) + jnp.sum(far_x, 1)) / width
        spread = (jnp.sum(near_x * near_x, 1) + jnp.sum(far_x * far_x, 1)) / width - center * center
        inv = lax.rsqrt(spread + EPSILON)[:, None]
        normed = (near_x - center[:, None]) * inv
        return cotangent[micro].astype(F32) + inv * (
            grad - sums[0][:, None] / width - normed * sums[1][:, None] / width
        )

    def along_z(kept):
        total = pick(kept, place_z)
        for s in range(1, depth):
            total = total + shifted(pick(kept, (place_z + s) % depth).astype(BF16), s, count).astype(F32)
        return total

    bias_0, (near_0, other_0, sums_0, dq, dvec_0) = norm_back(0, xb0, xd0, None, heads_own)
    kept = pick(tiles, place_x, 1).astype(F32) + tiles_back.astype(F32)
    dq, kept = lax.optimization_barrier((dq, kept))
    rest_sum = along_z(kept)
    outputs = (
        residual.astype(F32) + near[:, 1].astype(F32) + crossed[:, 1].astype(F32) + moved.astype(F32) + out_bias
    ).astype(BF16)
    grad_0 = input_grad(0, near_0, other_0, sums_0)
    heads_own, dq = lax.optimization_barrier((heads_own, dq))
    bias_1_, (near_1, other_1, sums_1, dq_tiles, dvec_1) = norm_back(1, xb1, xd1, dq, heads_own)
    grad_1 = input_grad(1, near_1, other_1, sums_1)
    dq_tiles = dq_tiles.reshape(depth, 2, *dq_tiles.shape[1:])
    dq_back = across(pick(dq_tiles, 1 - place_x, 1), count)
    dq_sum = along_z(pick(dq_tiles, place_x, 1).astype(F32) + dq_back.astype(F32))

    attend_weight_grad = rows_from_cores(dq_sum.reshape(heads, head_part, width), col).transpose(2, 0, 1)
    output_weight_grad = rows_from_cores(rest_sum[:lo].reshape(heads, out_part, width), col)
    expand_weight_grad = rows_from_cores(rest_sum[lo : lo + hid], col).T
    shrink_weight_grad = rows_from_cores(rest_sum[lo + hid :], col)

    dvec = jnp.roll((dvec_0 + dvec_1)[:4], col * wide, axis=1)
    dout = jnp.sum(cotangent.astype(F32), axis=(0, 1))
    dout = lax.dynamic_update_slice_in_dim(jnp.zeros((width,), F32), dout, col * wide, 0)
    dbq = (bias_0 + bias_1_).reshape(heads, -1)
    dbq = lax.dynamic_update_slice_in_dim(jnp.zeros(attend_bias.shape, F32), dbq, head_begin, 0)
    db1 = lax.dynamic_update_slice_in_dim(
        jnp.zeros((count, 4, hid), F32), db1.reshape(count, 1, hid), row * 2 + col, 1
    )
    flat = [dvec.reshape(-1), dout, dbq.reshape(-1), db1.reshape(-1)]
    ends = np.cumsum([part.size for part in flat])
    summed = total_of(jnp.concatenate(flat).reshape(-1, 128), count).reshape(-1)
    dvec, dout, dbq, db1 = jnp.split(summed, ends[:-1])
    dvec = dvec.reshape(4, width)
    return (
        outputs, jnp.stack([grad_0, grad_1]), dvec[0], dvec[1], dvec[2], dvec[3],
        attend_weight_grad, dbq.reshape(attend_bias.shape), output_weight_grad, dout, expand_weight_grad, db1,
        shrink_weight_grad, dout,
    )


def solution(mesh):
    tokens = P(None, ("dp", "row"), "col")
    weights = (P("col", "row", "dp"), P("row", "dp", "col"), P("col", ("dp", "row")), P(("dp", "row"), "col"))
    one = P()
    in_specs = (tokens, one, one, one, one, weights[0], one, weights[1], one, weights[2], one, weights[3], one, tokens)
    out_specs = (tokens, tokens, one, one, one, one, weights[0], one, weights[1], one, weights[2], one, weights[3], one)
    return jax.shard_map(body, mesh=mesh, in_specs=in_specs, out_specs=out_specs, check_vma=False)
```

```python
from functools import partial

import jax
import jax.numpy as jnp
import numpy as np
from jax import lax
from jax.experimental import pallas as pl
from jax.experimental.pallas import tpu as pltpu
from jax.sharding import PartitionSpec as P

D = 1024
HS = 64
ROT = 16
HALF = ROT // 2
EPSILON = 1e-05
MASKED = -1e30
NN = (((1,), (0,)), ((), ()))
NT = (((1,), (1,)), ((), ()))
TN = (((0,), (0,)), ((), ()))
VMEM_LIMIT = 56 << 20
F32 = jnp.float32
BF16 = jnp.bfloat16


def mm(a, b, dims):
    return lax.dot_general(a, b, dims, preferred_element_type=F32)


def params(**extra):
    return pltpu.CompilerParams(vmem_limit_bytes=VMEM_LIMIT, **extra)


def cost(flops, nbytes):
    return pl.CostEstimate(flops=int(flops), bytes_accessed=int(nbytes), transcendentals=0)


def whole(shape):
    return pl.BlockSpec(shape, lambda *_: (0,) * len(shape))


MESH = pl.DeviceIdType.MESH
ANYWHERE = pl.BlockSpec(memory_space=pl.ANY)


class Spot:
    def __init__(self):
        self.count = lax.axis_size("dp")
        self.depth = self.count // 2
        self.dp, self.row, self.col = (lax.axis_index(a) for a in ("dp", "row", "col"))
        self.z, self.x = self.dp // 2, self.dp % 2

    def along(self, steps):
        return ((self.z + steps) % self.depth) * 2 + self.x

    def device(self, which):
        return {
            "row": {"row": 1 - self.row},
            "col": {"col": 1 - self.col},
            "x": {"dp": self.z * 2 + (1 - self.x)},
            "right": {"dp": self.along(1)},
            "left": {"dp": self.along(self.depth - 1)},
        }[which]

    def greet(self, *names):
        barrier = pltpu.get_barrier_semaphore()
        for name in names:
            pl.semaphore_signal(barrier, inc=1, device_id=self.device(name), device_id_type=MESH)
        pl.semaphore_wait(barrier, len(names))


def remote(spot, which, source, target, send, recv):
    return pltpu.make_async_remote_copy(
        src_ref=source, dst_ref=target, send_sem=send, recv_sem=recv,
        device_id=spot.device(which), device_id_type=MESH,
    )


class Gather:
    def __init__(self, spot, mine, theirs, all_ref, local, send, recv):
        self.spot, self.all = spot, all_ref
        wide = mine.shape[1]
        here = all_ref.at[spot.dp]
        depth = spot.depth
        self.local = pltpu.make_async_copy(mine, here.at[:, pl.ds(0, wide)], local)
        self.core = remote(spot, "col", theirs, here.at[:, pl.ds(wide, wide)], send.at[0], recv.at[0])
        self.ring, self.cross = [], []
        for k in range(depth):
            slot = all_ref.at[spot.along(depth - k)]
            self.cross.append(remote(spot, "x", slot, slot, send.at[1 + k], recv.at[1 + k]))
            if k < depth - 1:
                at = 1 + depth + k
                self.ring.append(remote(spot, "right", slot, slot, send.at[at], recv.at[at]))

    @staticmethod
    def sems(count):
        return pltpu.SemaphoreType.DMA((count,))

    def begin(self):
        self.local.start()
        self.core.start()

    def first(self):
        self.local.wait()
        self.core.wait_recv()
        self.ring[0].start()
        self.cross[0].start()

    def forward(self, k):
        self.ring[k - 1].wait_recv()
        if k < len(self.ring):
            self.ring[k].start()
        self.cross[k].start()

    def finish(self):
        for copy in self.cross:
            copy.wait_recv()
        for copy in (self.core, *self.ring, *self.cross):
            copy.wait_send()


def enter_kernel(mine, theirs, tokens, all_ref, xb, xc, xd, local, send, recv, y_send, y_recv, c_send, c_recv, *, chunks):
    spot = Spot()
    spot.greet("row", "col", "x", "right", "left")
    gather = Gather(spot, mine, theirs, all_ref, local, send, recv)
    size = xb.shape[0] // chunks
    part = lambda k: pl.ds(k * size, size)
    over_row = [
        remote(spot, "row", tokens.at[0, part(k)], xb.at[part(k)], y_send.at[k], y_recv.at[k]) for k in range(chunks)
    ]
    over_col = [
        remote(spot, "col", xb.at[part(k)], xd.at[part(k)], c_send.at[k], c_recv.at[k]) for k in range(chunks)
    ]
    core = remote(spot, "col", tokens, xc, c_send.at[chunks], c_recv.at[chunks])
    gather.begin()
    for copy in over_row:
        copy.start()
    gather.first()
    core.start()
    depth = spot.depth
    for k in range(max(depth - 1, chunks)):
        if k + 1 < depth:
            gather.forward(k + 1)
        if k < chunks:
            over_row[k].wait_recv()
            over_col[k].start()
    gather.finish()
    core.wait()
    for k in range(chunks):
        over_col[k].wait()
        over_row[k].wait_send()


def enter(mine, theirs, tokens, count, chunks=4):
    rows, wide = mine.shape
    micros, length, _ = tokens.shape
    depth = count // 2
    half = jax.ShapeDtypeStruct((length, wide), BF16)
    return pl.pallas_call(
        partial(enter_kernel, chunks=chunks),
        in_specs=[ANYWHERE] * 3,
        out_specs=[ANYWHERE] * 4,
        out_shape=[
            jax.ShapeDtypeStruct((count, rows, 2 * wide), BF16), half,
            jax.ShapeDtypeStruct(tokens.shape, BF16), half,
        ],
        scratch_shapes=[
            pltpu.SemaphoreType.DMA, Gather.sems(2 * depth), Gather.sems(2 * depth),
            Gather.sems(chunks), Gather.sems(chunks), Gather.sems(chunks + 1), Gather.sems(chunks + 1),
        ],
        compiler_params=pltpu.CompilerParams(collective_id=0, has_side_effects=True),
        name="enter",
    )(mine, theirs, tokens)


def forward_kernel(
    xa, xc, xb0, xd0, weight, bias, vectors, cosine, sine, mine, theirs, tokens, grads,
    plain, second, triple, att_own, att_far, logsum, all_ref, xb1, xd1, cb0, cc, cd0,
    x_s, first, q_s, v_s, o_s, n_s, f_s, local, send, recv, y_send, y_recv, c_send, c_recv, t_sem, l_sem, *, block, step,
):
    spot = Spot()
    now = pl.program_id(0)
    wide = xa.shape[2]
    width = 2 * wide
    own_tokens = tokens.shape[1]
    length = 2 * own_tokens
    blocks = own_tokens // block
    heads = weight.shape[0] // (3 * HS)
    depth = spot.depth
    attend0, far1, attend1 = 3 * blocks, 3 * blocks + heads, 4 * blocks + heads
    end = attend1 + heads - 1
    here, there = spot.row, 1 - spot.row

    gather = Gather(spot, mine, theirs, all_ref, local, send, recv)
    x_row = remote(spot, "row", tokens.at[1], xb1, y_send.at[0], y_recv.at[0])
    x_col = remote(spot, "col", xb1, xd1, c_send.at[0], c_recv.at[0])
    g_row = remote(spot, "row", grads.at[0], cb0, y_send.at[1], y_recv.at[1])
    g_col = remote(spot, "col", cb0, cd0, c_send.at[1], c_recv.at[1])
    g_core = remote(spot, "col", grads, cc, c_send.at[2], c_recv.at[2])
    load_near = pltpu.make_async_copy(xb1, n_s, l_sem.at[0])
    load_far = pltpu.make_async_copy(xd1, f_s, l_sem.at[1])
    keep = [pltpu.make_async_copy(q_s.at[m], triple.at[m], t_sem.at[m]) for m in range(2)]

    at = lambda k: pl.when(now == k)

    @at(0)
    def _():
        spot.greet("row", "col", "x", "right", "left")
        gather.begin()
        x_row.start()

    @at(1)
    def _():
        gather.first()
        g_core.start()

    moments = {1: attend0 + 1, 2: far1, 3: attend1 + 2} if depth == 4 else {}
    for k in range(1, depth):
        moment = moments.get(k, attend1 + 2)

        @at(moment)
        def _():
            gather.forward(k)

    @at(attend0 + 2)
    def _():
        x_row.wait_recv()
        x_col.start()
        g_row.start()

    @at(attend0 + 3)
    def _():
        x_col.wait_recv()
        load_near.start()
        load_far.start()

    @at(far1)
    def _():
        load_near.wait()
        load_far.wait()

    @at(end - 1)
    def _():
        g_row.wait_recv()
        g_col.start()

    @pl.when(now < 2 * blocks)
    def _():
        x_s[:, :wide] = xa[0]
        x_s[:, wide:] = xc[0]

    @pl.when((now >= 2 * blocks) & (now < attend0))
    def _():
        x_s[:, :wide] = xb0[...]
        x_s[:, wide:] = xd0[...]

    for k in range(blocks):
        @at(far1 + k)
        def _():
            x_s[:, :wide] = n_s[k * block : (k + 1) * block]
            x_s[:, wide:] = f_s[k * block : (k + 1) * block]

    project = (now < attend0) | ((now >= far1) & (now < attend1))

    @pl.when(project)
    def _():
        micro = jnp.where(now < blocks, 0, jnp.where(now < 2 * blocks, 1, jnp.where(now < attend0, 0, 1)))
        half = jnp.where(now < 2 * blocks, here, there)
        number = jnp.where(now < attend0, now % blocks, (now - far1) % blocks)
        lane = pl.ds(pl.multiple_of(half * own_tokens + number * block, block), block)
        values = x_s[...].astype(F32)
        center = jnp.sum(values, axis=1, keepdims=True) / width
        spread = jnp.sum(values * values, axis=1, keepdims=True) / width - center * center
        normed = (values - center) * lax.rsqrt(spread + EPSILON)
        plain[0, 0] = normed.astype(BF16)
        first[...] = (normed * vectors[0:1, :] + vectors[1:2, :]).astype(BF16)
        second[0, 0] = (normed * vectors[2:3, :] + vectors[3:4, :]).astype(BF16)
        cos, sin = cosine[:, lane], sine[:, lane]
        for head in range(heads):
            base = head * 3 * HS
            rows = mm(weight[base : base + 3 * HS, :], first[...], NT) + bias[base : base + 3 * HS, :]
            pieces = []
            for which in range(2):
                lo = which * HS
                scale = HS ** (-0.5) if which == 0 else 1.0
                u1, u2 = rows[lo : lo + HALF], rows[lo + HALF : lo + ROT]
                pieces += [(u1 * cos - u2 * sin) * scale, (u2 * cos + u1 * sin) * scale, rows[lo + ROT : lo + HS] * scale]
            pieces.append(rows[2 * HS :])
            q_s[micro, base : base + 3 * HS, lane] = jnp.concatenate(pieces, axis=0).astype(BF16)

    @at(attend0)
    def _():
        keep[0].start()

    @at(attend1)
    def _():
        keep[1].start()

    attending = ((now >= attend0) & (now < far1)) | (now >= attend1)

    @pl.when(attending)
    def _():
        micro = jnp.where(now < far1, 0, 1)
        head = jnp.where(now < far1, now - attend0, now - attend1)
        base = pl.multiple_of(head * 3 * HS, HS)
        query_of = lambda lo, hi: q_s[micro, pl.ds(base, HS), lo:hi]
        keys_of = lambda lo, hi: q_s[micro, pl.ds(pl.multiple_of(base + HS, HS), HS), lo:hi]
        v_s[0:HS, :] = q_s[micro, pl.ds(pl.multiple_of(base + 2 * HS, HS), HS), :]
        extra = lax.broadcasted_iota(jnp.int32, (16, length), 0)
        v_s[HS : HS + 16, :] = jnp.where(extra == 0, 1.0, 0.0).astype(BF16)
        allowed = causal_tile(step)
        for i in range(length // step):
            lo, hi = i * step, (i + 1) * step
            query = query_of(lo, hi)
            diag = jnp.where(allowed, mm(keys_of(lo, hi), query, TN), MASKED)
            highest = jnp.max(diag, axis=0, keepdims=True)
            if i:
                past = mm(keys_of(0, lo), query, TN)
                highest = jnp.maximum(highest, jnp.max(past, axis=0, keepdims=True))
            raised = jnp.exp(diag - highest).astype(BF16)
            result = mm(v_s[:, lo:hi], raised, NN)
            if i:
                raised = jnp.exp(past - highest).astype(BF16)
                result = result + mm(v_s[:, :lo], raised, NN)
            total = result[HS : HS + 1]
            o_s[:, lo:hi] = (result[:HS] / total).astype(BF16)
            logsum[0, 0, :, lo:hi] = highest + jnp.log(total)
        att_own[0] = o_s[:, lanes(here, own_tokens)]
        att_far[0] = o_s[:, lanes(there, own_tokens)]

    @at(end)
    def _():
        gather.finish()
        g_col.wait()
        g_core.wait()
        x_col.wait_send()
        x_row.wait_send()
        g_row.wait_send()
        keep[0].wait()
        keep[1].wait()


def lanes(index, tokens):
    return pl.ds(pl.multiple_of(index * tokens, tokens), tokens)


def forward(residual, xc, xb0, xd0, weight, bias, vectors, cosine, sine, mine, theirs, cotangent, count, block=512, step=512):
    micros, tokens, wide = residual.shape
    width, length = 2 * wide, 2 * tokens
    block, step = min(block, tokens), min(step, length)
    blocks = tokens // block
    rows = weight.shape[0]
    heads = rows // (3 * HS)
    depth = count // 2
    a0, f1, a1 = 3 * blocks, 3 * blocks + heads, 4 * blocks + heads
    steps = a1 + heads
    clip = lambda v, lo, hi: jnp.minimum(jnp.maximum(v, lo), hi)
    own = pl.BlockSpec((1, block, wide), lambda i: (jnp.where(i < blocks, 0, 1), jnp.where(i < 2 * blocks, i % blocks, blocks - 1), 0))
    far = pl.BlockSpec((block, wide), lambda i: (clip(i - 2 * blocks, 0, blocks - 1), 0))

    def place(i):
        late = i >= f1
        micro = jnp.where(i < blocks, 0, jnp.where(i < 2 * blocks, 1, jnp.where(late, 1, 0)))
        half = jnp.where(i < 2 * blocks, 1, 0)
        number = jnp.where(i < 2 * blocks, i % blocks, jnp.where(late, clip(i - f1, 0, blocks - 1), clip(i - 2 * blocks, 0, blocks - 1)))
        return micro, half, number, 0

    def head_of(i):
        late = i >= a1
        return jnp.where(late, 1, 0), jnp.where(late, i - a1, clip(i - a0, 0, heads - 1))

    normal = pl.BlockSpec((1, 1, block, width), place)
    att = pl.BlockSpec((1, HS, tokens), lambda i: (*head_of(i), 0))
    half = jax.ShapeDtypeStruct((tokens, wide), BF16)
    piece = mine.shape[0]
    return pl.pallas_call(
        partial(forward_kernel, block=block, step=step),
        grid=(steps,),
        in_specs=[
            own, own, far, far, whole(weight.shape), whole(bias.shape), whole(vectors.shape),
            whole(cosine.shape), whole(sine.shape), ANYWHERE, ANYWHERE, ANYWHERE, ANYWHERE,
        ],
        out_specs=[
            normal, normal, ANYWHERE, att, att, pl.BlockSpec((1, 1, 1, length), lambda i: (*head_of(i), 0, 0)),
            *[ANYWHERE] * 6,
        ],
        out_shape=[
            jax.ShapeDtypeStruct((micros, 2, tokens, width), BF16),
            jax.ShapeDtypeStruct((micros, 2, tokens, width), BF16),
            jax.ShapeDtypeStruct((micros, rows, length), BF16),
            jax.ShapeDtypeStruct((micros, heads * HS, tokens), BF16),
            jax.ShapeDtypeStruct((micros, heads * HS, tokens), BF16),
            jax.ShapeDtypeStruct((micros, heads, 1, length), F32),
            jax.ShapeDtypeStruct((count, piece, width), BF16),
            half, half, half, jax.ShapeDtypeStruct(cotangent.shape, BF16), half,
        ],
        scratch_shapes=[
            pltpu.VMEM((block, width), BF16),
            pltpu.VMEM((block, width), BF16),
            pltpu.VMEM((micros, rows, length), BF16),
            pltpu.VMEM((HS + 16, length), BF16),
            pltpu.VMEM((HS, length), BF16),
            pltpu.VMEM((tokens, wide), BF16),
            pltpu.VMEM((tokens, wide), BF16),
            pltpu.SemaphoreType.DMA, Gather.sems(2 * depth), Gather.sems(2 * depth),
            Gather.sems(2), Gather.sems(2), Gather.sems(3), Gather.sems(3), Gather.sems(2), Gather.sems(2),
        ],
        compiler_params=params(collective_id=1, has_side_effects=True),
        cost_estimate=cost(micros * length * width * rows * 2 + micros * heads * length * length * 256 * 2, 40 << 20),
        name="forward",
    )(residual, xc, xb0, xd0, weight, bias, vectors, cosine, sine, mine, theirs, residual, cotangent)
def causal_tile(size):
    keys = lax.broadcasted_iota(jnp.int32, (size, size), 0)
    places = lax.broadcasted_iota(jnp.int32, (size, size), 1)
    return keys <= places


def lanes(index, tokens):
    return pl.ds(pl.multiple_of(index * tokens, tokens), tokens)


POLY = (0.254829592, -0.284496736, 1.421413741, -1.453152027, 1.061405429)


def gelu_pair(value):
    magnitude = jnp.abs(value)
    t = 1.0 / (1.0 + magnitude * (0.3275911 * 0.5**0.5))
    bell = jnp.exp(value * value * -0.5)
    series = POLY[4]
    for term in (POLY[3], POLY[2], POLY[1], POLY[0]):
        series = series * t + term
    tail = 0.5 * series * t * bell
    cumulative = jnp.where(value >= 0.0, 1.0 - tail, tail)
    return value * cumulative, cumulative + value * bell * (1.0 / (2.0 * np.pi) ** 0.5)


def column_of(row):
    return jnp.transpose(jnp.broadcast_to(row, (128, row.shape[1])))[:, 0:1]


def middle_kernel(
    second, normed, ca, cc, cb0, cd0, att_own, att_far, pieces, wo, bias, vectors, out_bias, grads, x_fin,
    out, heads_own, heads_far, part, tiles, dvec, dbias, cb1, cd1,
    w1, w2, dw1, dw2, dwo, n_s, f_s, c_s, a_s, act_s, eg_s,
    near_f, near_o, other_f, other_o, cross_f, cross_o, y_s, moved,
    w_sem, l_sem, y_send, y_recv, c_send, c_recv, cf_send, cf_recv, co_send, co_recv, m_send, m_recv,
    *, block, chunk, out_part,
):
    spot = Spot()
    now = pl.program_id(0)
    wide = ca.shape[2]
    count, rows, width = pieces.shape
    hid = w1.shape[0] // count
    heads = wo.shape[0] // HS
    steps = ca_steps = grads.shape[1] // block
    end = 4 * steps
    micro, half, at = now // (2 * steps), (now // steps) % 2, now % steps
    g_row = remote(spot, "row", grads.at[1], cb1, y_send, y_recv)
    g_col = remote(spot, "col", cb1, cd1, c_send, c_recv)
    load_near = pltpu.make_async_copy(cb1, n_s, l_sem.at[0])
    load_far = pltpu.make_async_copy(cd1, f_s, l_sem.at[1])

    def over_core(which, m, i):
        k = m * steps + i
        if which == 0:
            return remote(spot, "col", other_f.at[m, i], cross_f.at[m, i], cf_send.at[k], cf_recv.at[k])
        return remote(spot, "col", other_o.at[m, i], cross_o.at[m, i], co_send.at[k], co_recv.at[k])

    def over_row(m, i):
        k = m * steps + i
        return remote(spot, "row", y_s.at[m, i], moved.at[m, i], m_send.at[k], m_recv.at[k])

    @pl.when(now == 0)
    def _():
        spot.greet("row", "col")
        g_row.start()
        lo = heads * out_part
        copies = []
        for p in range(count):
            here = slice(p * hid, (p + 1) * hid)
            copies.append(pltpu.make_async_copy(pieces.at[p, lo : lo + hid], w1.at[here], w_sem.at[2 * p]))
            copies.append(pltpu.make_async_copy(pieces.at[p, lo + hid :], w2.at[here], w_sem.at[2 * p + 1]))
        for copy in copies:
            copy.start()
        dw1[...] = jnp.zeros_like(dw1)
        dw2[...] = jnp.zeros_like(dw2)
        dwo[...] = jnp.zeros_like(dwo)
        dbias[...] = jnp.zeros_like(dbias)
        for copy in copies:
            copy.wait()

    @pl.when(now == 2 * steps - 2)
    def _():
        g_row.wait_recv()
        g_col.start()

    @pl.when(now == 2 * steps - 1)
    def _():
        g_col.wait_recv()
        load_near.start()
        load_far.start()

    @pl.when(now == 2 * steps)
    def _():
        load_near.wait()
        load_far.wait()

    before = now - 1

    @pl.when((now > 0) & ((before // steps) % 2 == 0) & (now < end))
    def _():
        m, i = before // (2 * steps), before % steps
        over_core(0, m, i).wait_recv()
        y_s[m, i] = (near_f[...] + cross_f[m, i].astype(F32)).astype(BF16)
        over_row(m, i).start()

    def finish(m, i):
        over_row(m, i).wait_recv()
        over_core(1, m, i).wait_recv()
        out[0] = (
            x_fin[0].astype(F32) + near_o[m, i].astype(F32) + cross_o[m, i].astype(F32)
            + moved[m, i].astype(F32) + out_bias[...]
        ).astype(BF16)

    @pl.when((now >= 2 * steps) & (now < 3 * steps))
    def _():
        finish(0, now - 2 * steps)

    @pl.when(now > 3 * steps)
    def _():
        finish(1, now - 3 * steps - 1)

    @pl.when((half == 0) & (now < steps))
    def _():
        c_s[:, :wide] = cb0[...]
        c_s[:, wide:] = cd0[...]

    @pl.when((half == 0) & (now >= 2 * steps) & (now < end))
    def _():
        here = pl.ds(pl.multiple_of(at * block, block), block)
        c_s[:, :wide] = n_s[here, :]
        c_s[:, wide:] = f_s[here, :]

    @pl.when((half == 1) & (now < end))
    def _():
        c_s[:, :wide] = ca[0]
        c_s[:, wide:] = cc[0]
        a_s[...] = att_own[0]

    @pl.when((half == 0) & (now < end))
    def _():
        a_s[...] = att_far[0]

    @pl.when(now < end)
    def _():
        hidden = w1.shape[0]
        for lo in range(0, hidden, chunk):
            hi = lo + chunk
            expanded = mm(second[0, 0], w1[lo:hi, :], NT) + bias[:, lo:hi]
            active, slope = gelu_pair(expanded)
            act_s[:, lo:hi] = active.astype(BF16)
            rounded = (mm(c_s[...], w2[lo:hi, :], NT) * slope).astype(BF16)
            eg_s[:, lo:hi] = rounded
            dbias[:, lo:hi] += jnp.sum(rounded.astype(F32), axis=0, keepdims=True)
        for lo in range(0, hidden, chunk):
            hi = lo + chunk
            dw2[lo:hi, :] += mm(act_s[:, lo:hi], c_s[...], TN)
            dw1[lo:hi, :] += mm(eg_s[:, lo:hi], normed[0, 0], TN)
        dwo[...] += mm(a_s[...], c_s[...], NN)
        near = mm(act_s[...], w2[:, :wide], NN) + mm(a_s[...], wo[:, :wide], TN)
        other = (mm(act_s[...], w2[:, wide:], NN) + mm(a_s[...], wo[:, wide:], TN)).astype(BF16)
        part[0, 0] = (mm(eg_s[...], w1[...], NN) * vectors[2:3, :]).astype(BF16)
        heads_grad = mm(wo[...], c_s[...], NT).astype(BF16)

        @pl.when(half == 0)
        def _():
            heads_far[0] = heads_grad
            near_f[...] = near
            other_f[micro, at] = other
            over_core(0, micro, at).start()

        @pl.when(half == 1)
        def _():
            heads_own[0] = heads_grad
            near_o[micro, at] = near.astype(BF16)
            other_o[micro, at] = other
            over_core(1, micro, at).start()

    @pl.when(now == end)
    def _():
        lo = heads * out_part
        summed = column_of(dbias[...])
        gain_grad = jnp.zeros((1, width), F32)
        bias_grad = jnp.zeros((1, width), F32)
        for p in range(count):
            here = slice(p * hid, (p + 1) * hid)
            small = [dwo[h * HS + p * out_part : h * HS + (p + 1) * out_part, :] for h in range(heads)]
            tiles[p, :lo] = jnp.concatenate(small, axis=0).astype(BF16)
            tiles[p, lo : lo + hid] = (dw1[here, :] * vectors[2:3, :] + summed[here] * vectors[3:4, :]).astype(BF16)
            tiles[p, lo + hid :] = dw2[here, :].astype(BF16)
            weight = w1[here, :].astype(F32)
            gain_grad += jnp.sum(weight * dw1[here, :], axis=0, keepdims=True)
            bias_grad += jnp.sum(weight * summed[here], axis=0, keepdims=True)
        dvec[0:1, :] = gain_grad
        dvec[1:2, :] = bias_grad
        g_row.wait_send()
        g_col.wait_send()
        for m in range(2):
            for i in range(steps):
                over_core(0, m, i).wait_send()
                over_core(1, m, i).wait_send()
                over_row(m, i).wait_send()


def middle(second, normed, residual, cotangent, cc, cb0, cd0, att_own, att_far, pieces, wo, bias, vectors, out_bias, block=256, chunk=256):
    micros, tokens, wide = cotangent.shape
    count, rows, width = pieces.shape
    block = min(block, tokens)
    steps = tokens // block
    hidden, head_rows = bias.shape[1], wo.shape[0]
    hid = hidden // count
    out_part = (rows - 2 * hid) * HS // head_rows
    end, top = steps - 1, 4 * steps - 1

    def place(s):
        s = jnp.minimum(s, top)
        return s // (2 * steps), (s // steps) % 2, s % steps

    def own_at(s):
        m, h, i = place(s)
        return m, h * i

    def far_at(s):
        m, h, i = place(s)
        return m, i * (1 - h) + end * h

    def finished(s):
        late = s > 3 * steps
        number = jnp.where(late, s - 3 * steps - 1, jnp.clip(s - 2 * steps, 0, end))
        return jnp.where(late, 1, 0), number, 0

    both = lambda n: pl.BlockSpec((1, 1, block, n), lambda s: (*place(s), 0))
    own = pl.BlockSpec((1, block, wide), lambda s: (*own_at(s), 0))
    far0 = pl.BlockSpec((block, wide), lambda s: (jnp.minimum(s, end), 0))
    cols_own = pl.BlockSpec((1, head_rows, block), lambda s: (own_at(s)[0], 0, own_at(s)[1]))
    cols_far = pl.BlockSpec((1, head_rows, block), lambda s: (far_at(s)[0], 0, far_at(s)[1]))
    fin = pl.BlockSpec((1, block, wide), finished)
    halves = jax.ShapeDtypeStruct((tokens, wide), BF16)
    stack = lambda dtype: pltpu.VMEM((micros, steps, block, wide), dtype)
    return pl.pallas_call(
        partial(middle_kernel, block=block, chunk=min(chunk, hidden), out_part=out_part),
        grid=(4 * steps + 1,),
        in_specs=[
            both(width), both(width), own, own, far0, far0, cols_own, cols_far, ANYWHERE, whole(wo.shape),
            whole(bias.shape), whole(vectors.shape), whole(out_bias.shape), ANYWHERE, fin,
        ],
        out_specs=[
            fin, cols_own, cols_far, both(width), whole(pieces.shape), whole((8, width)), whole(bias.shape),
            ANYWHERE, ANYWHERE,
        ],
        out_shape=[
            jax.ShapeDtypeStruct((micros, tokens, wide), BF16),
            jax.ShapeDtypeStruct((micros, head_rows, tokens), BF16),
            jax.ShapeDtypeStruct((micros, head_rows, tokens), BF16),
            jax.ShapeDtypeStruct((micros, 2, tokens, width), BF16),
            jax.ShapeDtypeStruct(pieces.shape, BF16),
            jax.ShapeDtypeStruct((8, width), F32),
            jax.ShapeDtypeStruct(bias.shape, F32),
            halves, halves,
        ],
        scratch_shapes=[
            pltpu.VMEM((hidden, width), BF16),
            pltpu.VMEM((hidden, width), BF16),
            pltpu.VMEM((hidden, width), F32),
            pltpu.VMEM((hidden, width), F32),
            pltpu.VMEM((head_rows, width), F32),
            pltpu.VMEM((tokens, wide), BF16),
            pltpu.VMEM((tokens, wide), BF16),
            pltpu.VMEM((block, width), BF16),
            pltpu.VMEM((head_rows, block), BF16),
            pltpu.VMEM((block, hidden), BF16),
            pltpu.VMEM((block, hidden), BF16),
            pltpu.VMEM((block, wide), F32), stack(BF16), stack(BF16), stack(BF16), stack(BF16), stack(BF16),
            stack(BF16), stack(BF16),
            Gather.sems(2 * count), Gather.sems(2),
            pltpu.SemaphoreType.DMA, pltpu.SemaphoreType.DMA, pltpu.SemaphoreType.DMA, pltpu.SemaphoreType.DMA,
            *[Gather.sems(micros * steps) for _ in range(6)],
        ],
        compiler_params=params(collective_id=2, has_side_effects=True),
        cost_estimate=cost(2 * micros * tokens * 2 * width * (6 * hidden + 3 * head_rows), 80 << 20),
        name="middle",
    )(
        second, normed, cotangent, cc, cb0, cd0, att_own, att_far, pieces, wo, bias, vectors, out_bias, cotangent,
        residual,
    )


class Scatter:
    def __init__(self, spot, tiles, own, rx, tx, rz, total, out, x_send, x_recv, z_send, z_recv, c_send, c_recv, local):
        self.spot, self.own, self.rx, self.tx, self.rz, self.total = spot, own, rx, tx, rz, total
        depth, wide = spot.depth, out.shape[2]
        self.order = [*range(1, depth), 0]
        self.cross, self.along = {}, {}
        for s in self.order:
            away = spot.along(s) + 1 - 2 * spot.x
            self.cross[s] = remote(spot, "x", tiles.at[away], rx.at[s], x_send.at[s], x_recv.at[s])
            if s:
                self.along[s] = pltpu.make_async_remote_copy(
                    src_ref=tx.at[s - 1], dst_ref=rz.at[s - 1], send_sem=z_send.at[s], recv_sem=z_recv.at[s],
                    device_id={"dp": spot.along(s)}, device_id_type=MESH,
                )
        self.core = remote(spot, "col", total.at[:, pl.ds(wide, wide)], out.at[spot.col], c_send, c_recv)
        self.keep = pltpu.make_async_copy(total.at[:, pl.ds(0, wide)], out.at[spot.col], local)

    def begin(self):
        for s in self.order:
            self.cross[s].start()

    def fold(self, s):
        self.cross[s].wait_recv()
        added = self.own(s).astype(F32) + self.rx[s].astype(F32)
        if s:
            self.tx[s - 1] = added.astype(BF16)
            self.along[s].start()
        else:
            self.total[...] = added

    def finish(self):
        added = self.total[...]
        for s in self.order[:-1]:
            self.along[s].wait_recv()
            added = added + self.rz[s - 1].astype(F32)
        self.total[...] = added
        self.core.start()
        self.keep.start()

    def close(self):
        self.core.wait()
        self.keep.wait()
        for s in self.order:
            self.cross[s].wait_send()
            if s:
                self.along[s].wait_send()


def back_kernel(
    triple, h_own, h_far, att_own, att_far, logsum, cosine, sine, normed, part, weight, vectors, tiles, early,
    x_fin, xc_fin, g_fin,
    grad_out, rest_out, dq_out, vec_out,
    g_s, delta_s, dq_s, dk_s, dv_s, t_s, total, bias_s,
    near_f, near_o, other_f, other_o, cross_f, cross_o, y_s, moved, sum_s, sum_r, ng_s, norm_s, inv_s,
    a_own, a_rx, a_tx, a_rz, a_total, b_tiles, b_rx, b_tx, b_rz, b_total, held, arrived,
    a_load, a_xs, a_xr, a_zs, a_zr, a_cs, a_cr, a_loc, b_xs, b_xr, b_zs, b_zr, b_cs, b_cr, b_loc,
    v_send, v_recv, cf_send, cf_recv, co_send, co_recv, m_send, m_recv, s_send, s_recv,
    *, block, wider, step,
):
    spot = Spot()
    now = pl.program_id(0)
    tokens, wide = h_own.shape[2], x_fin.shape[2]
    width, length = 2 * wide, 2 * tokens
    heads = weight.shape[0] // (3 * HS)
    steps = tokens // block
    count, depth = spot.count, spot.depth
    slow = length // wider
    d0 = heads
    l0 = d0 + slow
    b1 = l0 + 2 * steps
    d1 = b1 + heads
    l1 = d1 + slow
    e1 = l1 + 2 * steps
    end = e1 + steps
    here, there = spot.row, 1 - spot.row
    at_step = lambda k: pl.when(now == k)

    first_sum = Scatter(
        spot, tiles, lambda s: a_own[s], a_rx, a_tx, a_rz, a_total, rest_out,
        a_xs, a_xr, a_zs, a_zr, a_cs, a_cr, a_loc,
    )
    last_sum = Scatter(
        spot, b_tiles, lambda s: b_tiles[spot.along(s)], b_rx, b_tx, b_rz, b_total, dq_out,
        b_xs, b_xr, b_zs, b_zr, b_cs, b_cr, b_loc,
    )
    loads = [pltpu.make_async_copy(tiles.at[spot.along(s)], a_own.at[s], a_load.at[s]) for s in range(depth)]

    partners = [{"col": 1 - spot.col}, {"row": 1 - spot.row}, {"dp": spot.z * 2 + (1 - spot.x)}]
    stride = 1
    while stride < depth:
        other_z = spot.z + stride * (1 - 2 * ((spot.z // stride) % 2))
        partners.append({"dp": other_z * 2 + spot.x})
        stride *= 2
    hops = [
        pltpu.make_async_remote_copy(
            src_ref=held.at[k], dst_ref=arrived.at[k], send_sem=v_send.at[k], recv_sem=v_recv.at[k],
            device_id=partner, device_id_type=MESH,
        )
        for k, partner in enumerate(partners)
    ]

    def over_core(which, m, i):
        k = m * steps + i
        if which == 0:
            return remote(spot, "col", other_f.at[i], cross_f.at[m, i], cf_send.at[k], cf_recv.at[k])
        return remote(spot, "col", other_o.at[i], cross_o.at[m, i], co_send.at[k], co_recv.at[k])

    def over_row(m, i):
        k = m * steps + i
        return remote(spot, "row", y_s.at[m, i], moved.at[m, i], m_send.at[k], m_recv.at[k])

    def sums_over(m, i):
        k = m * steps + i
        return remote(spot, "col", sum_s.at[m, i], sum_r.at[m, i], s_send.at[k], s_recv.at[k])

    @at_step(0)
    def _():
        barrier = pltpu.get_barrier_semaphore()
        near = [{"col": 1 - spot.col}, {"row": 1 - spot.row}, {"dp": spot.z * 2 + (1 - spot.x)}]
        for device in near + [{"dp": spot.along(s)} for s in range(1, depth)]:
            pl.semaphore_signal(barrier, inc=1, device_id=device, device_id_type=MESH)
        pl.semaphore_wait(barrier, depth + 2)
        first_sum.begin()
        for load in loads:
            load.start()
        bias_s[...] = jnp.zeros_like(bias_s)

    @at_step(1)
    def _():
        for load in loads:
            load.wait()

    moments = {1: 2, 2: d0, 3: l0 + 4, 0: b1 + 1} if depth == 4 else {}
    for s in first_sum.order:
        @at_step(moments.get(s, b1 + 1))
        def _():
            first_sum.fold(s)

    @pl.when((now < d0) | ((now >= b1) & (now < d1)))
    def _():
        head = jnp.where(now < d0, now, now - b1)
        for grad, att, place in ((h_own, att_own, here), (h_far, att_far, there)):
            at = lanes(place, tokens)
            g_s[:, at] = grad[0]
            delta_s[:, at] = jnp.sum(grad[0].astype(F32) * att[0].astype(F32), axis=0, keepdims=True)
        q_s, k_s, v_s = (triple.at[0, i * HS : (i + 1) * HS] for i in range(3))
        dk_s[...] = jnp.zeros_like(dk_s)
        dv_s[...] = jnp.zeros_like(dv_s)
        allowed = causal_tile(step)
        for i in range(length // step):
            lo, hi = i * step, (i + 1) * step
            query, grad = q_s[:, lo:hi], g_s[:, lo:hi]
            base, delta = logsum[0, 0, :, lo:hi], delta_s[:, lo:hi]
            query_grad = None
            for begin, stop in ((0, lo), (lo, hi)):
                if stop == begin:
                    continue
                raised = jnp.exp(mm(k_s[:, begin:stop], query, TN) - base)
                if begin == lo:
                    raised = jnp.where(allowed, raised, 0.0)
                prob_grad = mm(v_s[:, begin:stop], grad, TN)
                score_grad = (raised * (prob_grad - delta)).astype(BF16)
                dv_s[:, begin:stop] += mm(grad, raised.astype(BF16), NT)
                dk_s[:, begin:stop] += mm(query, score_grad, NT)
                term = mm(k_s[:, begin:stop], score_grad, NN)
                query_grad = term if query_grad is None else query_grad + term
            dq_s[:, lo:hi] = query_grad * HS ** (-0.5)
        cos, sin = cosine[...], sine[...]
        pieces = []
        for ref in (dq_s, dk_s):
            g1, g2 = ref[0:HALF, :], ref[HALF:ROT, :]
            pieces += [g1 * cos + g2 * sin, g2 * cos - g1 * sin, ref[ROT:HS, :]]
        pieces.append(dv_s[...])
        rounded = jnp.concatenate(pieces, axis=0).astype(BF16)
        at = pl.ds(pl.multiple_of(head * 3 * HS, HS), 3 * HS)
        t_s[at, :] = rounded
        bias_s[at, :] += jnp.sum(rounded.astype(F32), axis=1, keepdims=True)

    @pl.when(((now >= d0) & (now < l0)) | ((now >= d1) & (now < l1)))
    def _():
        number = jnp.where(now < l0, now - d0, now - d1)
        half, at = number // (slow // 2), number % (slow // 2)
        place = jnp.where(half == 0, there, here)
        lane = pl.ds(pl.multiple_of(place * tokens + at * wider, wider), wider)
        term = mm(t_s[:, lane], normed[0, 0], NN)

        @at_step(d0)
        def _():
            total[...] = term

        @pl.when(now > d0)
        def _():
            total[...] += term

    @at_step(l1 - 1)
    def _():
        size = 3 * HS // count
        gain, shift = vectors[0:1, :], vectors[1:2, :]
        weights = weight[...].astype(F32)
        gain_grad = jnp.sum(weights * total[...], axis=0, keepdims=True)
        shift_grad = jnp.sum(weights * bias_s[...], axis=0, keepdims=True)
        total[...] = total[...] * gain + bias_s[...] * shift
        for p in range(count):
            small = [total[h * 3 * HS + p * size : h * 3 * HS + (p + 1) * size, :] for h in range(heads)]
            b_tiles[p] = jnp.concatenate(small, axis=0).astype(BF16)
        last_sum.begin()
        used = early.shape[0]
        part_rows = width // (2 * held.shape[2])
        lanes_here = held.shape[2]
        held[0] = jnp.zeros_like(held[0])
        held[0, 0:used, :] = early[...]
        at = used
        for vector in (gain_grad, shift_grad):
            for r in range(2 * part_rows):
                mirror = (r + part_rows) % (2 * part_rows)
                plain = vector[:, r * lanes_here : (r + 1) * lanes_here]
                turned = vector[:, mirror * lanes_here : (mirror + 1) * lanes_here]
                held[0, at : at + 1, :] = jnp.where(spot.col == 0, plain, turned)
                at += 1
        line = jnp.transpose(jnp.broadcast_to(bias_s[...], (bias_s.shape[0], 128)))[0:1, :]
        mine = spot.row * 2 + spot.col
        for h in range(4 * heads):
            k = h % heads
            values = line[:, k * 3 * HS : (k + 1) * 3 * HS]
            held[0, at : at + 1, 0 : 3 * HS] = jnp.where(mine == h // heads, values, 0.0)
            at += 1

    for k in range(len(hops) + 1):
        @at_step(l1 + k)
        def _():
            if k:
                hops[k - 1].wait_recv()
            if 0 < k < len(hops):
                held[k] = held[k - 1] + arrived[k - 1]
            if k < len(hops):
                hops[k].start()
            else:
                vec_out[...] = held[k - 1] + arrived[k - 1]

    @at_step(l1)
    def _():
        first_sum.finish()

    moments_b = {1: l1 + 3, 2: l1 + 5, 3: l1 + 7, 0: e1} if depth == 4 else {}
    for s in last_sum.order:
        @at_step(moments_b.get(s, e1))
        def _():
            last_sum.fold(s)

    @at_step(b1)
    def _():
        for i in range(steps):
            over_core(0, 0, i).wait_send()
            over_core(1, 0, i).wait_send()

    later = now >= b1
    lead = jnp.where(later, now - l1, now - l0)

    @pl.when((lead > 0) & (lead <= steps))
    def _():
        m, i = jnp.where(later, 1, 0), lead - 1
        over_core(0, m, i).wait_recv()
        y_s[m, i] = (near_f[...] + cross_f[m, i].astype(F32)).astype(BF16)
        over_row(m, i).start()

    trail = jnp.where(now >= e1, now - e1, now - l1)
    micro = jnp.where(now >= e1, 1, 0)

    @pl.when((trail > 0) & (trail <= steps))
    def _():
        i = trail - 1
        sums_over(micro, i).wait_recv()
        sums = (sum_s[micro, i] + sum_r[micro, i]) / width
        grad_out[0] = g_fin[0].astype(F32) + inv_s[...] * (ng_s[...] - sums[:, 0:1] - norm_s[...] * sums[:, 1:2])

    @pl.when((trail >= 0) & (trail < steps))
    def _():
        over_row(micro, trail).wait_recv()
        over_core(1, micro, trail).wait_recv()
        grad = near_o[trail] + cross_o[micro, trail].astype(F32) + moved[micro, trail].astype(F32)
        near_x, far_x = x_fin[0].astype(F32), xc_fin[0].astype(F32)
        center = jnp.sum(near_x + far_x, axis=1, keepdims=True) / width
        spread = jnp.sum(near_x * near_x + far_x * far_x, axis=1, keepdims=True) / width - center * center
        inv = lax.rsqrt(spread + EPSILON)
        normed_x = (near_x - center) * inv
        ng_s[...] = grad
        norm_s[...] = normed_x
        inv_s[...] = inv
        column = lax.broadcasted_iota(jnp.int32, (block, 128), 1)
        one = jnp.sum(grad, axis=1, keepdims=True)
        two = jnp.sum(grad * normed_x, axis=1, keepdims=True)
        sum_s[micro, trail] = jnp.where(column == 0, one, jnp.where(column == 1, two, 0.0))
        sums_over(micro, trail).start()

    @pl.when((lead >= 0) & (lead < 2 * steps))
    def _():
        m, half, i = jnp.where(later, 1, 0), lead // steps, lead % steps
        place = jnp.where(half == 0, there, here)
        lane = pl.ds(pl.multiple_of(place * tokens + i * block, block), block)
        turned = t_s[:, lane]
        near = mm(turned, weight[:, :wide], TN) * vectors[0:1, :wide] + part[0, 0, :, :wide].astype(F32)
        other = mm(turned, weight[:, wide:], TN) * vectors[0:1, wide:] + part[0, 0, :, wide:].astype(F32)

        @pl.when(half == 0)
        def _():
            near_f[...] = near
            other_f[i] = other.astype(BF16)
            over_core(0, m, i).start()

        @pl.when(half == 1)
        def _():
            near_o[i] = near
            other_o[i] = other.astype(BF16)
            over_core(1, m, i).start()

    @at_step(end)
    def _():
        last_sum.finish()
        first_sum.close()
        for k in hops:
            k.wait_send()
        for i in range(steps):
            over_core(0, 1, i).wait_send()
            over_core(1, 1, i).wait_send()
            for m in range(2):
                over_row(m, i).wait_send()
                sums_over(m, i).wait_send()
        last_sum.close()


def backward(
    triple, h_own, h_far, att_own, att_far, logsum, cosine, sine, normed, part, weight, vectors, tiles, early,
    residual, xc, cotangent, block=256, wider=512, step=256,
):
    micros, rows, length = triple.shape
    tokens, wide = length // 2, residual.shape[2]
    width = 2 * wide
    heads = rows // (3 * HS)
    block, wider, step = min(block, tokens), min(wider, tokens), min(step, length)
    steps, slow = tokens // block, length // wider
    count, piece = tiles.shape[:2]
    depth = count // 2
    small = rows // count
    d0 = heads
    l0 = d0 + slow
    b1 = l0 + 2 * steps
    d1 = b1 + heads
    l1 = d1 + slow
    e1 = l1 + 2 * steps
    head_of = lambda s: (jnp.where(s >= b1, 1, 0), jnp.where(s >= b1, jnp.minimum(s - b1, heads - 1), jnp.minimum(s, heads - 1)))

    def slow_at(s):
        late = s >= b1
        number = jnp.clip(jnp.where(late, s - d1, s - d0), 0, slow - 1)
        return jnp.where(late, 1, 0), number // (slow // 2), number % (slow // 2), 0

    def part_at(s):
        late = s >= b1
        number = jnp.clip(jnp.where(late, s - l1, s - l0), 0, 2 * steps - 1)
        return jnp.where(late, 1, 0), number // steps, number % steps, 0

    def in_at(s):
        late = s > l1 + steps
        return jnp.where(late, 1, 0), jnp.clip(jnp.where(late, s - e1, s - l1), 0, steps - 1), 0

    def out_at(s):
        late = s > l1 + steps
        return jnp.where(late, 1, 0), jnp.clip(jnp.where(late, s - e1 - 1, s - l1 - 1), 0, steps - 1), 0

    narrow = pl.BlockSpec((1, HS, tokens), lambda s: (*head_of(s), 0))
    fin_in = pl.BlockSpec((1, block, wide), in_at)
    fin_out = pl.BlockSpec((1, block, wide), out_at)
    hops = 3 + max(depth - 1, 0).bit_length()
    vec_rows = early.shape[0] + 2 * (width // early.shape[1]) + 4 * heads
    pair = lambda dtype: pltpu.VMEM((micros, steps, block, wide), dtype)
    single = lambda dtype: pltpu.VMEM((steps, block, wide), dtype)
    sems, one = Gather.sems, pltpu.SemaphoreType.DMA
    return pl.pallas_call(
        partial(back_kernel, block=block, wider=wider, step=step),
        grid=(e1 + steps + 1,),
        in_specs=[
            pl.BlockSpec((1, 3 * HS, length), lambda s: (*head_of(s), 0)), narrow, narrow, narrow, narrow,
            pl.BlockSpec((1, 1, 1, length), lambda s: (*head_of(s), 0, 0)), whole(cosine.shape), whole(sine.shape),
            pl.BlockSpec((1, 1, wider, width), slow_at), pl.BlockSpec((1, 1, block, width), part_at),
            whole(weight.shape), whole(vectors.shape), ANYWHERE, whole(early.shape), fin_in, fin_in, fin_out,
        ],
        out_specs=[fin_out, ANYWHERE, ANYWHERE, whole((vec_rows, early.shape[1]))],
        out_shape=[
            jax.ShapeDtypeStruct((micros, tokens, wide), F32),
            jax.ShapeDtypeStruct((2, piece, wide), F32),
            jax.ShapeDtypeStruct((2, small, wide), F32),
            jax.ShapeDtypeStruct((vec_rows, early.shape[1]), F32),
        ],
        scratch_shapes=[
            pltpu.VMEM((HS, length), BF16),
            pltpu.VMEM((1, length), F32),
            pltpu.VMEM((HS, length), F32),
            pltpu.VMEM((HS, length), F32),
            pltpu.VMEM((HS, length), F32),
            pltpu.VMEM((rows, length), BF16),
            pltpu.VMEM((rows, width), F32),
            pltpu.VMEM((rows, 1), F32),
            pltpu.VMEM((block, wide), F32), single(F32), single(BF16), single(BF16), pair(BF16), pair(BF16),
            pair(BF16), pair(BF16),
            pltpu.VMEM((micros, steps, block, 128), F32), pltpu.VMEM((micros, steps, block, 128), F32),
            pltpu.VMEM((block, wide), F32), pltpu.VMEM((block, wide), F32), pltpu.VMEM((block, 1), F32),
            pltpu.VMEM((depth, piece, width), BF16), pltpu.VMEM((depth, piece, width), BF16),
            pltpu.VMEM((depth - 1, piece, width), BF16), pltpu.VMEM((depth - 1, piece, width), BF16),
            pltpu.VMEM((piece, width), F32),
            pltpu.VMEM((count, small, width), BF16), pltpu.VMEM((depth, small, width), BF16),
            pltpu.VMEM((depth - 1, small, width), BF16), pltpu.VMEM((depth - 1, small, width), BF16),
            pltpu.VMEM((small, width), F32),
            pltpu.VMEM((hops, vec_rows, early.shape[1]), F32), pltpu.VMEM((hops, vec_rows, early.shape[1]), F32),
            sems(depth), sems(depth), sems(depth), sems(depth), sems(depth), one, one, one,
            sems(depth), sems(depth), sems(depth), sems(depth), one, one, one,
            sems(hops), sems(hops), *[sems(micros * steps) for _ in range(8)],
        ],
        compiler_params=params(collective_id=3, has_side_effects=True),
        cost_estimate=cost(micros * (heads * length * length * 256 * 5 + length * width * 4 * rows), 100 << 20),
        name="backward",
    )(
        triple, h_own, h_far, att_own, att_far, logsum, cosine, sine, normed, part, weight, vectors, tiles, early,
        residual, xc, cotangent,
    )


def pick(value, index, axis=0):
    return lax.dynamic_index_in_dim(value, index, axis, keepdims=False)


def body(
    residual, attend_norm_gain, attend_norm_bias, expand_norm_gain, expand_norm_bias,
    attend_weight, attend_bias, output_weight, output_bias, expand_weight, expand_bias,
    shrink_weight, shrink_bias, cotangent,
):
    count = lax.axis_size("dp")
    row, col = lax.axis_index("row"), lax.axis_index("col")
    micros, tokens, wide = residual.shape
    width, length = 2 * wide, 2 * tokens
    heads = attend_weight.shape[1] // 2
    head_part, out_part = attend_weight.shape[2], output_weight.shape[1]
    hid = expand_weight.shape[1] // 2

    def sides(rows):
        return pick(rows, col), pick(rows, 1 - col)

    head_mine, head_theirs = sides(attend_weight.transpose(1, 2, 0).reshape(2, heads * head_part, wide))
    rest_mine, rest_theirs = sides(
        jnp.concatenate(
            [
                output_weight.reshape(2, heads * out_part, wide),
                expand_weight.T.reshape(2, hid, wide),
                shrink_weight.reshape(2, hid, wide),
            ],
            axis=1,
        )
    )
    head_all, xb0, xc, xd0 = enter(head_mine, head_theirs, residual, count)
    wq = head_all.reshape(count, heads, head_part, width).transpose(1, 0, 2, 3).reshape(heads * 3 * HS, width)

    vectors = jnp.stack([attend_norm_gain, attend_norm_bias, expand_norm_gain, expand_norm_bias])
    vectors = jnp.concatenate([jnp.roll(vectors, -col * wide, axis=1), jnp.zeros((4, width), F32)])
    head_begin = row * 2 * heads + col * heads
    bias_q = lax.dynamic_slice_in_dim(attend_bias, head_begin, heads, 0).reshape(-1, 1)
    bias_1 = pick(expand_bias.reshape(count, 4, hid), row * 2 + col, 1).reshape(1, -1)
    out_bias = lax.dynamic_slice_in_dim(output_bias + shrink_bias, col * wide, wide, 0).reshape(1, -1)
    powers = 10000.0 ** (-np.arange(HALF) * (2.0 / ROT))
    angles = powers[:, None] * np.arange(length)[None, :]
    cosine, sine = jnp.asarray(np.cos(angles), F32), jnp.asarray(np.sin(angles), F32)

    normed, second, triple, att_own, att_far, logsum, pieces, xb1, xd1, cb0, cc, cd0 = forward(
        residual, xc, xb0, xd0, wq, bias_q, vectors, cosine, sine, rest_mine, rest_theirs, cotangent, count
    )
    lo = heads * out_part
    wo = pieces[:, :lo].reshape(count, heads, out_part, width).transpose(1, 0, 2, 3).reshape(heads * HS, width)
    outputs, h_own, h_far, part, tiles, dvec, db1, _, _ = middle(
        second, normed, residual, cotangent, cc, cb0, cd0, att_own, att_far, pieces, wo, bias_1, vectors, out_bias
    )

    dout = jnp.sum(cotangent.astype(F32), axis=(0, 1))
    dout = lax.dynamic_update_slice_in_dim(jnp.zeros((width,), F32), dout, col * wide, 0)
    dvec = jnp.roll(dvec[:2], col * wide, axis=1)
    db1 = lax.dynamic_update_slice_in_dim(
        jnp.zeros((count, 4, hid), F32), db1.reshape(count, 1, hid), row * 2 + col, 1
    )
    lane = 256
    early = jnp.concatenate([db1.reshape(-1, lane), dout.reshape(-1, lane), dvec.reshape(-1, lane)])
    early = jnp.pad(early, ((0, -early.shape[0] % 8), (0, 0)))

    grads, rest_sum, dq_sum, vec = backward(
        triple, h_own, h_far, att_own, att_far, logsum, cosine, sine, normed, part, wq, vectors, tiles, early,
        residual, xc, cotangent,
    )
    attend_weight_grad = dq_sum.reshape(2 * heads, head_part, wide).transpose(2, 0, 1)
    output_weight_grad = rest_sum[:, :lo].reshape(2 * heads, out_part, wide)
    expand_weight_grad = rest_sum[:, lo : lo + hid].reshape(2 * hid, wide).T
    shrink_weight_grad = rest_sum[:, lo + hid :].reshape(2 * hid, wide)

    n1, nw, ne = db1.size // lane, width // lane, early.shape[0]
    cut = lambda at, rows: vec[at : at + rows].reshape(-1)
    dout = cut(n1, nw)
    return (
        outputs, grads, cut(ne, nw), cut(ne + nw, nw), cut(n1 + nw, nw), cut(n1 + 2 * nw, nw),
        attend_weight_grad, vec[ne + 2 * nw :, : 3 * HS], output_weight_grad, dout, expand_weight_grad, cut(0, n1),
        shrink_weight_grad, dout,
    )


def solution(mesh):
    tokens = P(None, ("dp", "row"), "col")
    weights = (P("col", "row", "dp"), P("row", "dp", "col"), P("col", ("dp", "row")), P(("dp", "row"), "col"))
    one = P()
    in_specs = (tokens, one, one, one, one, weights[0], one, weights[1], one, weights[2], one, weights[3], one, tokens)
    out_specs = (tokens, tokens, one, one, one, one, weights[0], one, weights[1], one, weights[2], one, weights[3], one)
    return jax.shard_map(body, mesh=mesh, in_specs=in_specs, out_specs=out_specs, check_vma=False)
```

```python
from functools import partial

import jax
import jax.numpy as jnp
import numpy as np
from jax import lax
from jax.experimental import pallas as pl
from jax.experimental.pallas import tpu as pltpu
from jax.sharding import PartitionSpec as P

D = 1024
HS = 64
ROT = 16
HALF = ROT // 2
EPSILON = 1e-05
MASKED = -1e30
NN = (((1,), (0,)), ((), ()))
NT = (((1,), (1,)), ((), ()))
TN = (((0,), (0,)), ((), ()))
VMEM_LIMIT = 56 << 20
F32 = jnp.float32
BF16 = jnp.bfloat16


def mm(a, b, dims):
    return lax.dot_general(a, b, dims, preferred_element_type=F32)


def params(**extra):
    return pltpu.CompilerParams(vmem_limit_bytes=VMEM_LIMIT, **extra)


def cost(flops, nbytes):
    return pl.CostEstimate(flops=int(flops), bytes_accessed=int(nbytes), transcendentals=0)


def whole(shape):
    return pl.BlockSpec(shape, lambda *_: (0,) * len(shape))


MESH = pl.DeviceIdType.MESH
ANYWHERE = pl.BlockSpec(memory_space=pl.ANY)


class Spot:
    def __init__(self):
        self.count = lax.axis_size("dp")
        self.depth = self.count // 2
        self.dp, self.row, self.col = (lax.axis_index(a) for a in ("dp", "row", "col"))
        self.z, self.x = self.dp // 2, self.dp % 2

    def along(self, steps):
        return ((self.z + steps) % self.depth) * 2 + self.x

    def device(self, which):
        return {
            "row": {"row": 1 - self.row},
            "col": {"col": 1 - self.col},
            "x": {"dp": self.z * 2 + (1 - self.x)},
            "right": {"dp": self.along(1)},
            "left": {"dp": self.along(self.depth - 1)},
        }[which]

    def greet(self, *names):
        barrier = pltpu.get_barrier_semaphore()
        for name in names:
            pl.semaphore_signal(barrier, inc=1, device_id=self.device(name), device_id_type=MESH)
        pl.semaphore_wait(barrier, len(names))


def remote(spot, which, source, target, send, recv):
    return pltpu.make_async_remote_copy(
        src_ref=source, dst_ref=target, send_sem=send, recv_sem=recv,
        device_id=spot.device(which), device_id_type=MESH,
    )


class Gather:
    def __init__(self, spot, mine, theirs, all_ref, local, send, recv):
        self.spot, self.all = spot, all_ref
        wide = mine.shape[1]
        here = all_ref.at[spot.dp]
        depth = spot.depth
        self.local = pltpu.make_async_copy(mine, here.at[:, pl.ds(0, wide)], local)
        self.core = remote(spot, "col", theirs, here.at[:, pl.ds(wide, wide)], send.at[0], recv.at[0])
        self.ring, self.cross = [], []
        for k in range(depth):
            slot = all_ref.at[spot.along(depth - k)]
            self.cross.append(remote(spot, "x", slot, slot, send.at[1 + k], recv.at[1 + k]))
            if k < depth - 1:
                at = 1 + depth + k
                self.ring.append(remote(spot, "right", slot, slot, send.at[at], recv.at[at]))

    @staticmethod
    def sems(count):
        return pltpu.SemaphoreType.DMA((count,))

    def begin(self):
        self.local.start()
        self.core.start()

    def first(self):
        self.local.wait()
        self.core.wait_recv()
        self.ring[0].start()
        self.cross[0].start()

    def forward(self, k):
        self.ring[k - 1].wait_recv()
        if k < len(self.ring):
            self.ring[k].start()
        self.cross[k].start()

    def arrive(self):
        for copy in self.cross:
            copy.wait_recv()

    def close(self):
        for copy in (self.core, *self.ring, *self.cross):
            copy.wait_send()


def lanes(index, tokens):
    return pl.ds(pl.multiple_of(index * tokens, tokens), tokens)


def forward_kernel(
    xa, bias, vectors, cosine, sine, head_mine, head_theirs, mine, theirs, tokens, grads,
    plain, second, triple, weight_out, att_own, att_far, logsum, all_ref, xc, cb0, cc, cd0,
    x_s, first, q_s, v_s, o_s, xc_s, near_s, far_s, pieces, weight,
    a_local, a_send, a_recv, local, send, recv, y_send, y_recv, c_send, c_recv, t_sem, *, block, step, chunks, rows_at_once,
):
    spot = Spot()
    now = pl.program_id(0)
    wide = xa.shape[2]
    width = 2 * wide
    own_tokens = tokens.shape[1]
    length = 2 * own_tokens
    blocks = own_tokens // block
    heads = weight.shape[0] // (3 * HS)
    depth, count = spot.depth, spot.count
    cast0 = 2 * blocks
    far0 = 2 * cast0
    attend0 = far0 + blocks
    far1 = attend0 + heads
    attend1 = far1 + blocks
    end = attend1 + heads - 1
    here, there = spot.row, 1 - spot.row
    at = lambda k: pl.when(now == k)

    head_gather = Gather(spot, head_mine, head_theirs, pieces, a_local, a_send, a_recv)
    gather = Gather(spot, mine, theirs, all_ref, local, send, recv)
    size = own_tokens // chunks
    part = lambda k: pl.ds(k * size, size)
    x_row = [
        [remote(spot, "row", tokens.at[m, part(k)], near_s.at[m, part(k)], y_send.at[m * chunks + k], y_recv.at[m * chunks + k]) for k in range(chunks)]
        for m in range(2)
    ]
    x_col = [
        [remote(spot, "col", near_s.at[m, part(k)], far_s.at[m, part(k)], c_send.at[m * chunks + k], c_recv.at[m * chunks + k]) for k in range(chunks)]
        for m in range(2)
    ]
    x_core = [remote(spot, "col", tokens.at[m], xc_s.at[m], c_send.at[2 * chunks + m], c_recv.at[2 * chunks + m]) for m in range(2)]
    g_row = remote(spot, "row", grads.at[0], cb0, y_send.at[2 * chunks], y_recv.at[2 * chunks])
    g_col = remote(spot, "col", cb0, cd0, c_send.at[2 * chunks + 2], c_recv.at[2 * chunks + 2])
    g_core = remote(spot, "col", grads, cc, c_send.at[2 * chunks + 3], c_recv.at[2 * chunks + 3])
    keep = [pltpu.make_async_copy(q_s.at[m], triple.at[m], t_sem.at[m]) for m in range(2)]
    keep_weight = pltpu.make_async_copy(weight, weight_out, t_sem.at[2])
    keep_core = pltpu.make_async_copy(xc_s, xc, t_sem.at[3])

    @at(0)
    def _():
        spot.greet("row", "col", "x", "right", "left")
        head_gather.begin()
        for copy in x_row[0]:
            copy.start()
        x_core[0].start()
        gather.begin()
        head_gather.first()
        x_core[1].start()
        x_core[0].wait_recv()

    @at(blocks)
    def _():
        x_core[1].wait_recv()
        keep_core.start()

    @at(2)
    def _():
        head_gather.forward(1)

    @at(cast0)
    def _():
        for k in range(2, depth):
            head_gather.forward(k)
        gather.first()
        for copy in x_row[1]:
            copy.start()
        head_gather.arrive()
        size = weight.shape[0] // (heads * count)
        for h in range(heads):
            small = [pieces[p, h * size : (h + 1) * size, :].astype(F32) for p in range(count)]
            weight[h * 3 * HS : (h + 1) * 3 * HS, :] = jnp.concatenate(small, axis=0).astype(BF16)
        keep_weight.start()

    @at(cast0 + 1)
    def _():
        for k in range(chunks):
            x_row[0][k].wait_recv()
            x_col[0][k].start()

    @at(far0)
    def _():
        for k in range(chunks):
            x_col[0][k].wait_recv()
        g_core.start()

    moments = {1: attend0, 2: attend0 + 3, 3: attend1} if depth == 4 else {}
    for k in range(1, depth):
        @at(moments.get(k, attend1))
        def _():
            gather.forward(k)

    @at(far1 - 1)
    def _():
        for k in range(chunks):
            x_row[1][k].wait_recv()
            x_col[1][k].start()
        g_row.start()

    @at(far1)
    def _():
        for k in range(chunks):
            x_col[1][k].wait_recv()

    norming = (now < cast0) | ((now >= far0) & (now < attend0)) | ((now >= far1) & (now < attend1))

    @pl.when(now < cast0)
    def _():
        lo = pl.multiple_of((now % blocks) * block, block)
        x_s[:, :wide] = xa[0]
        x_s[:, wide:] = xc_s[now // blocks, pl.ds(lo, block), :]

    for begin, m in ((far0, 0), (far1, 1)):
        @pl.when((now >= begin) & (now < begin + blocks))
        def _():
            lo = pl.multiple_of((now - begin) * block, block)
            x_s[:, :wide] = near_s[m, pl.ds(lo, block), :]
            x_s[:, wide:] = far_s[m, pl.ds(lo, block), :]

    slot = jnp.where(now < far0, now % cast0, (now - far0) % blocks)
    slot = jnp.where(now >= far1, now - far1, slot)

    @pl.when(norming)
    def _():
        for lo in range(0, block, rows_at_once):
            rows = slice(lo, lo + rows_at_once)
            values = x_s[rows, :].astype(F32)
            center = jnp.sum(values, axis=1, keepdims=True) / width
            spread = jnp.sum(values * values, axis=1, keepdims=True) / width - center * center
            normed = (values - center) * lax.rsqrt(spread + EPSILON)
            plain[0, 0, rows, :] = normed.astype(BF16)
            first[slot, rows, :] = (normed * vectors[0:1, :] + vectors[1:2, :]).astype(BF16)
            second[0, 0, rows, :] = (normed * vectors[2:3, :] + vectors[3:4, :]).astype(BF16)

    casting = ((now >= cast0) & (now < attend0)) | ((now >= far1) & (now < attend1))

    @pl.when(casting)
    def _():
        number = now - cast0
        micro = jnp.where(now < far0, number // blocks, jnp.where(now < attend0, 0, 1))
        half = jnp.where(now < far0, here, there)
        block_at = jnp.where(now >= far1, now - far1, number % blocks)
        lane = pl.ds(pl.multiple_of(half * own_tokens + block_at * block, block), block)
        cos, sin = cosine[:, lane], sine[:, lane]
        every = mm(weight[...], first[slot], NT) + bias[...]
        for head in range(heads):
            base = head * 3 * HS
            rows = every[base : base + 3 * HS]
            parts = []
            for which in range(2):
                lo = which * HS
                scale = HS ** (-0.5) if which == 0 else 1.0
                u1, u2 = rows[lo : lo + HALF], rows[lo + HALF : lo + ROT]
                parts += [(u1 * cos - u2 * sin) * scale, (u2 * cos + u1 * sin) * scale, rows[lo + ROT : lo + HS] * scale]
            parts.append(rows[2 * HS :])
            q_s[micro, base : base + 3 * HS, lane] = jnp.concatenate(parts, axis=0).astype(BF16)

    @at(attend0)
    def _():
        keep[0].start()

    @at(attend1)
    def _():
        keep[1].start()

    attending = ((now >= attend0) & (now < far1)) | (now >= attend1)

    @pl.when(attending)
    def _():
        micro = jnp.where(now < far1, 0, 1)
        head = jnp.where(now < far1, now - attend0, now - attend1)
        base = pl.multiple_of(head * 3 * HS, HS)
        query_of = lambda lo, hi: q_s[micro, pl.ds(base, HS), lo:hi]
        keys_of = lambda lo, hi: q_s[micro, pl.ds(pl.multiple_of(base + HS, HS), HS), lo:hi]
        v_s[0:HS, :] = q_s[micro, pl.ds(pl.multiple_of(base + 2 * HS, HS), HS), :]
        extra = lax.broadcasted_iota(jnp.int32, (16, length), 0)
        v_s[HS : HS + 16, :] = jnp.where(extra == 0, 1.0, 0.0).astype(BF16)
        allowed = causal_tile(step)
        for i in range(length // step):
            lo, hi = i * step, (i + 1) * step
            query = query_of(lo, hi)
            diag = jnp.where(allowed, mm(keys_of(lo, hi), query, TN), MASKED)
            highest = jnp.max(diag, axis=0, keepdims=True)
            if i:
                past = mm(keys_of(0, lo), query, TN)
                highest = jnp.maximum(highest, jnp.max(past, axis=0, keepdims=True))
            raised = jnp.exp(diag - highest).astype(BF16)
            result = mm(v_s[:, lo:hi], raised, NN)
            if i:
                raised = jnp.exp(past - highest).astype(BF16)
                result = result + mm(v_s[:, :lo], raised, NN)
            total = result[HS : HS + 1]
            o_s[:, lo:hi] = (result[:HS] / total).astype(BF16)
            logsum[0, 0, :, lo:hi] = highest + jnp.log(total)
        att_own[0] = o_s[:, lanes(here, own_tokens)]
        att_far[0] = o_s[:, lanes(there, own_tokens)]

    @at(end)
    def _():
        g_row.wait_recv()
        g_col.start()
        gather.arrive()
        gather.close()
        head_gather.close()
        g_col.wait()
        g_core.wait()
        for m in range(2):
            x_core[m].wait_send()
            for k in range(chunks):
                x_row[m][k].wait_send()
                x_col[m][k].wait_send()
        g_row.wait_send()
        keep[0].wait()
        keep[1].wait()
        keep_weight.wait()
        keep_core.wait()


def forward(residual, bias, vectors, cosine, sine, head_mine, head_theirs, mine, theirs, cotangent, count, block=512, step=512):
    micros, tokens, wide = residual.shape
    width, length = 2 * wide, 2 * tokens
    block, step = min(block, tokens), min(step, length)
    blocks = tokens // block
    rows = bias.shape[0]
    heads = rows // (3 * HS)
    depth = count // 2
    chunks = 4
    cast0 = 2 * blocks
    far0 = 2 * cast0
    a0 = far0 + blocks
    f1 = a0 + heads
    a1 = f1 + blocks
    steps = a1 + heads
    own = pl.BlockSpec((1, block, wide), lambda i: (jnp.minimum(i, cast0 - 1) // blocks, jnp.minimum(i, cast0 - 1) % blocks, 0))

    def place(i):
        early = jnp.minimum(i, cast0 - 1)
        late = i >= f1
        far = i >= far0
        micro = jnp.where(late, 1, jnp.where(far, 0, early // blocks))
        number = jnp.where(late, jnp.minimum(i - f1, blocks - 1), jnp.where(far, jnp.minimum(i - far0, blocks - 1), early % blocks))
        return micro, jnp.where(far, 0, 1), number, 0

    def head_of(i):
        late = i >= a1
        return jnp.where(late, 1, 0), jnp.where(late, i - a1, jnp.clip(i - a0, 0, heads - 1))

    normal = pl.BlockSpec((1, 1, block, width), place)
    att = pl.BlockSpec((1, HS, tokens), lambda i: (*head_of(i), 0))
    half = jax.ShapeDtypeStruct((tokens, wide), BF16)
    piece = mine.shape[0]
    sems, one = Gather.sems, pltpu.SemaphoreType.DMA
    return pl.pallas_call(
        partial(forward_kernel, block=block, step=step, chunks=chunks, rows_at_once=min(64, block)),
        grid=(steps,),
        in_specs=[
            own, whole(bias.shape), whole(vectors.shape), whole(cosine.shape), whole(sine.shape), *[ANYWHERE] * 6,
        ],
        out_specs=[
            normal, normal, ANYWHERE, ANYWHERE, att, att,
            pl.BlockSpec((1, 1, 1, length), lambda i: (*head_of(i), 0, 0)), *[ANYWHERE] * 5,
        ],
        out_shape=[
            jax.ShapeDtypeStruct((micros, 2, tokens, width), BF16),
            jax.ShapeDtypeStruct((micros, 2, tokens, width), BF16),
            jax.ShapeDtypeStruct((micros, rows, length), BF16),
            jax.ShapeDtypeStruct((rows, width), BF16),
            jax.ShapeDtypeStruct((micros, heads * HS, tokens), BF16),
            jax.ShapeDtypeStruct((micros, heads * HS, tokens), BF16),
            jax.ShapeDtypeStruct((micros, heads, 1, length), F32),
            jax.ShapeDtypeStruct((count, piece, width), BF16),
            jax.ShapeDtypeStruct(residual.shape, BF16), half, jax.ShapeDtypeStruct(cotangent.shape, BF16), half,
        ],
        scratch_shapes=[
            pltpu.VMEM((block, width), BF16),
            pltpu.VMEM((cast0, block, width), BF16),
            pltpu.VMEM((micros, rows, length), BF16),
            pltpu.VMEM((HS + 16, length), BF16),
            pltpu.VMEM((HS, length), BF16),
            pltpu.VMEM((micros, tokens, wide), BF16),
            pltpu.VMEM((micros, tokens, wide), BF16),
            pltpu.VMEM((micros, tokens, wide), BF16),
            pltpu.VMEM((count, rows // count, width), BF16),
            pltpu.VMEM((rows, width), BF16),
            one, sems(2 * depth), sems(2 * depth), one, sems(2 * depth), sems(2 * depth),
            sems(2 * chunks + 1), sems(2 * chunks + 1), sems(2 * chunks + 4), sems(2 * chunks + 4), sems(4),
        ],
        compiler_params=params(collective_id=1, has_side_effects=True),
        cost_estimate=cost(micros * length * width * rows * 2 + micros * heads * length * length * 256 * 2, 40 << 20),
        name="forward",
    )(residual, bias, vectors, cosine, sine, head_mine, head_theirs, mine, theirs, residual, cotangent)
def causal_tile(size):
    keys = lax.broadcasted_iota(jnp.int32, (size, size), 0)
    places = lax.broadcasted_iota(jnp.int32, (size, size), 1)
    return keys <= places


def lanes(index, tokens):
    return pl.ds(pl.multiple_of(index * tokens, tokens), tokens)


POLY = (0.254829592, -0.284496736, 1.421413741, -1.453152027, 1.061405429)


def gelu_pair(value):
    magnitude = jnp.abs(value)
    t = 1.0 / (1.0 + magnitude * (0.3275911 * 0.5**0.5))
    bell = jnp.exp(value * value * -0.5)
    series = POLY[4]
    for term in (POLY[3], POLY[2], POLY[1], POLY[0]):
        series = series * t + term
    tail = 0.5 * series * t * bell
    cumulative = jnp.where(value >= 0.0, 1.0 - tail, tail)
    return value * cumulative, cumulative + value * bell * (1.0 / (2.0 * np.pi) ** 0.5)


def column_of(row):
    return jnp.transpose(jnp.broadcast_to(row, (128, row.shape[1])))[:, 0:1]


def middle_kernel(
    second, normed, ca, cc, cb0, cd0, att_own, att_far, pieces, wo, bias, vectors, out_bias, grads, x_fin,
    out, heads_own, heads_far, part, tiles, dvec, dbias, cb1, cd1,
    w1, w2, dw1, dw2, dwo, n_s, f_s, c_s, a_s, act_s, eg_s,
    near_f, near_o, other_f, other_o, cross_f, cross_o, y_s, moved,
    w_sem, l_sem, y_send, y_recv, c_send, c_recv, cf_send, cf_recv, co_send, co_recv, m_send, m_recv,
    *, block, chunk, out_part,
):
    spot = Spot()
    now = pl.program_id(0)
    wide = ca.shape[2]
    count, rows, width = pieces.shape
    hid = w1.shape[0] // count
    heads = wo.shape[0] // HS
    steps = ca_steps = grads.shape[1] // block
    end = 4 * steps
    micro, half, at = now // (2 * steps), (now // steps) % 2, now % steps
    g_row = remote(spot, "row", grads.at[1], cb1, y_send, y_recv)
    g_col = remote(spot, "col", cb1, cd1, c_send, c_recv)
    load_near = pltpu.make_async_copy(cb1, n_s, l_sem.at[0])
    load_far = pltpu.make_async_copy(cd1, f_s, l_sem.at[1])

    def over_core(which, m, i):
        k = m * steps + i
        if which == 0:
            return remote(spot, "col", other_f.at[m, i], cross_f.at[m, i], cf_send.at[k], cf_recv.at[k])
        return remote(spot, "col", other_o.at[m, i], cross_o.at[m, i], co_send.at[k], co_recv.at[k])

    def over_row(m, i):
        k = m * steps + i
        return remote(spot, "row", y_s.at[m, i], moved.at[m, i], m_send.at[k], m_recv.at[k])

    @pl.when(now == 0)
    def _():
        spot.greet("row", "col")
        g_row.start()
        lo = heads * out_part
        copies = []
        for p in range(count):
            here = slice(p * hid, (p + 1) * hid)
            copies.append(pltpu.make_async_copy(pieces.at[p, lo : lo + hid], w1.at[here], w_sem.at[2 * p]))
            copies.append(pltpu.make_async_copy(pieces.at[p, lo + hid :], w2.at[here], w_sem.at[2 * p + 1]))
        for copy in copies:
            copy.start()
        dw1[...] = jnp.zeros_like(dw1)
        dw2[...] = jnp.zeros_like(dw2)
        dwo[...] = jnp.zeros_like(dwo)
        dbias[...] = jnp.zeros_like(dbias)
        for copy in copies:
            copy.wait()

    @pl.when(now == 2 * steps - 2)
    def _():
        g_row.wait_recv()
        g_col.start()

    @pl.when(now == 2 * steps - 1)
    def _():
        g_col.wait_recv()
        load_near.start()
        load_far.start()

    @pl.when(now == 2 * steps)
    def _():
        load_near.wait()
        load_far.wait()

    before = now - 1

    @pl.when((now > 0) & ((before // steps) % 2 == 0) & (now < end))
    def _():
        m, i = before // (2 * steps), before % steps
        over_core(0, m, i).wait_recv()
        y_s[m, i] = (near_f[...] + cross_f[m, i].astype(F32)).astype(BF16)
        over_row(m, i).start()

    def finish(m, i):
        over_row(m, i).wait_recv()
        over_core(1, m, i).wait_recv()
        out[0] = (
            x_fin[0].astype(F32) + near_o[m, i].astype(F32) + cross_o[m, i].astype(F32)
            + moved[m, i].astype(F32) + out_bias[...]
        ).astype(BF16)

    @pl.when((now >= 2 * steps) & (now < 3 * steps))
    def _():
        finish(0, now - 2 * steps)

    @pl.when(now > 3 * steps)
    def _():
        finish(1, now - 3 * steps - 1)

    @pl.when((half == 0) & (now < steps))
    def _():
        c_s[:, :wide] = cb0[...]
        c_s[:, wide:] = cd0[...]

    @pl.when((half == 0) & (now >= 2 * steps) & (now < end))
    def _():
        here = pl.ds(pl.multiple_of(at * block, block), block)
        c_s[:, :wide] = n_s[here, :]
        c_s[:, wide:] = f_s[here, :]

    @pl.when((half == 1) & (now < end))
    def _():
        c_s[:, :wide] = ca[0]
        c_s[:, wide:] = cc[0]
        a_s[...] = att_own[0]

    @pl.when((half == 0) & (now < end))
    def _():
        a_s[...] = att_far[0]

    @pl.when(now < end)
    def _():
        hidden = w1.shape[0]
        for lo in range(0, hidden, chunk):
            hi = lo + chunk
            expanded = mm(second[0, 0], w1[lo:hi, :], NT) + bias[:, lo:hi]
            active, slope = gelu_pair(expanded)
            act_s[:, lo:hi] = active.astype(BF16)
            rounded = (mm(c_s[...], w2[lo:hi, :], NT) * slope).astype(BF16)
            eg_s[:, lo:hi] = rounded
            dbias[:, lo:hi] += jnp.sum(rounded.astype(F32), axis=0, keepdims=True)
        for lo in range(0, hidden, chunk):
            hi = lo + chunk
            dw2[lo:hi, :] += mm(act_s[:, lo:hi], c_s[...], TN)
            dw1[lo:hi, :] += mm(eg_s[:, lo:hi], normed[0, 0], TN)
        dwo[...] += mm(a_s[...], c_s[...], NN)
        near = mm(act_s[...], w2[:, :wide], NN) + mm(a_s[...], wo[:, :wide], TN)
        other = (mm(act_s[...], w2[:, wide:], NN) + mm(a_s[...], wo[:, wide:], TN)).astype(BF16)
        part[0, 0] = (mm(eg_s[...], w1[...], NN) * vectors[2:3, :]).astype(BF16)
        heads_grad = mm(wo[...], c_s[...], NT).astype(BF16)

        @pl.when(half == 0)
        def _():
            heads_far[0] = heads_grad
            near_f[...] = near
            other_f[micro, at] = other
            over_core(0, micro, at).start()

        @pl.when(half == 1)
        def _():
            heads_own[0] = heads_grad
            near_o[micro, at] = near.astype(BF16)
            other_o[micro, at] = other
            over_core(1, micro, at).start()

    @pl.when(now == end)
    def _():
        lo = heads * out_part
        summed = column_of(dbias[...])
        gain_grad = jnp.zeros((1, width), F32)
        bias_grad = jnp.zeros((1, width), F32)
        for p in range(count):
            here = slice(p * hid, (p + 1) * hid)
            small = [dwo[h * HS + p * out_part : h * HS + (p + 1) * out_part, :] for h in range(heads)]
            tiles[p, :lo] = jnp.concatenate(small, axis=0).astype(BF16)
            tiles[p, lo : lo + hid] = (dw1[here, :] * vectors[2:3, :] + summed[here] * vectors[3:4, :]).astype(BF16)
            tiles[p, lo + hid :] = dw2[here, :].astype(BF16)
            weight = w1[here, :].astype(F32)
            gain_grad += jnp.sum(weight * dw1[here, :], axis=0, keepdims=True)
            bias_grad += jnp.sum(weight * summed[here], axis=0, keepdims=True)
        dvec[0:1, :] = gain_grad
        dvec[1:2, :] = bias_grad
        g_row.wait_send()
        g_col.wait_send()
        for m in range(2):
            for i in range(steps):
                over_core(0, m, i).wait_send()
                over_core(1, m, i).wait_send()
                over_row(m, i).wait_send()


def middle(second, normed, residual, cotangent, cc, cb0, cd0, att_own, att_far, pieces, wo, bias, vectors, out_bias, block=256, chunk=256):
    micros, tokens, wide = cotangent.shape
    count, rows, width = pieces.shape
    block = min(block, tokens)
    steps = tokens // block
    hidden, head_rows = bias.shape[1], wo.shape[0]
    hid = hidden // count
    out_part = (rows - 2 * hid) * HS // head_rows
    end, top = steps - 1, 4 * steps - 1

    def place(s):
        s = jnp.minimum(s, top)
        return s // (2 * steps), (s // steps) % 2, s % steps

    def own_at(s):
        m, h, i = place(s)
        return m, h * i

    def far_at(s):
        m, h, i = place(s)
        return m, i * (1 - h) + end * h

    def finished(s):
        late = s > 3 * steps
        number = jnp.where(late, s - 3 * steps - 1, jnp.clip(s - 2 * steps, 0, end))
        return jnp.where(late, 1, 0), number, 0

    both = lambda n: pl.BlockSpec((1, 1, block, n), lambda s: (*place(s), 0))
    own = pl.BlockSpec((1, block, wide), lambda s: (*own_at(s), 0))
    far0 = pl.BlockSpec((block, wide), lambda s: (jnp.minimum(s, end), 0))
    cols_own = pl.BlockSpec((1, head_rows, block), lambda s: (own_at(s)[0], 0, own_at(s)[1]))
    cols_far = pl.BlockSpec((1, head_rows, block), lambda s: (far_at(s)[0], 0, far_at(s)[1]))
    fin = pl.BlockSpec((1, block, wide), finished)
    halves = jax.ShapeDtypeStruct((tokens, wide), BF16)
    stack = lambda dtype: pltpu.VMEM((micros, steps, block, wide), dtype)
    return pl.pallas_call(
        partial(middle_kernel, block=block, chunk=min(chunk, hidden), out_part=out_part),
        grid=(4 * steps + 1,),
        in_specs=[
            both(width), both(width), own, own, far0, far0, cols_own, cols_far, ANYWHERE, whole(wo.shape),
            whole(bias.shape), whole(vectors.shape), whole(out_bias.shape), ANYWHERE, fin,
        ],
        out_specs=[
            fin, cols_own, cols_far, both(width), whole(pieces.shape), whole((8, width)), whole(bias.shape),
            ANYWHERE, ANYWHERE,
        ],
        out_shape=[
            jax.ShapeDtypeStruct((micros, tokens, wide), BF16),
            jax.ShapeDtypeStruct((micros, head_rows, tokens), BF16),
            jax.ShapeDtypeStruct((micros, head_rows, tokens), BF16),
            jax.ShapeDtypeStruct((micros, 2, tokens, width), BF16),
            jax.ShapeDtypeStruct(pieces.shape, BF16),
            jax.ShapeDtypeStruct((8, width), F32),
            jax.ShapeDtypeStruct(bias.shape, F32),
            halves, halves,
        ],
        scratch_shapes=[
            pltpu.VMEM((hidden, width), BF16),
            pltpu.VMEM((hidden, width), BF16),
            pltpu.VMEM((hidden, width), F32),
            pltpu.VMEM((hidden, width), F32),
            pltpu.VMEM((head_rows, width), F32),
            pltpu.VMEM((tokens, wide), BF16),
            pltpu.VMEM((tokens, wide), BF16),
            pltpu.VMEM((block, width), BF16),
            pltpu.VMEM((head_rows, block), BF16),
            pltpu.VMEM((block, hidden), BF16),
            pltpu.VMEM((block, hidden), BF16),
            pltpu.VMEM((block, wide), F32), stack(BF16), stack(BF16), stack(BF16), stack(BF16), stack(BF16),
            stack(BF16), stack(BF16),
            Gather.sems(2 * count), Gather.sems(2),
            pltpu.SemaphoreType.DMA, pltpu.SemaphoreType.DMA, pltpu.SemaphoreType.DMA, pltpu.SemaphoreType.DMA,
            *[Gather.sems(micros * steps) for _ in range(6)],
        ],
        compiler_params=params(collective_id=2, has_side_effects=True),
        cost_estimate=cost(2 * micros * tokens * 2 * width * (6 * hidden + 3 * head_rows), 80 << 20),
        name="middle",
    )(
        second, normed, cotangent, cc, cb0, cd0, att_own, att_far, pieces, wo, bias, vectors, out_bias, cotangent,
        residual,
    )


class Scatter:
    def __init__(self, spot, tiles, own, rx, rz, x_sems, z_sems):
        self.spot, self.own, self.rx, self.rz = spot, own, rx, rz
        self.order = [*range(1, spot.depth), 0]
        self.cross, self.along = {}, {}
        for s in self.order:
            away = spot.along(s) + 1 - 2 * spot.x
            self.cross[s] = remote(spot, "x", tiles(away), rx(s), x_sems[0](s), x_sems[1](s))
            if s:
                self.along[s] = pltpu.make_async_remote_copy(
                    src_ref=rx(s), dst_ref=rz(s - 1), send_sem=z_sems[0](s), recv_sem=z_sems[1](s),
                    device_id={"dp": spot.along(s)}, device_id_type=MESH,
                )

    def begin(self):
        for s in self.order:
            self.cross[s].start()

    def fold(self, s):
        self.cross[s].wait_recv()
        rx = self.rx(s)
        if s:
            rx[...] = (self.own(s)[...].astype(F32) + rx[...].astype(F32)).astype(BF16)
            self.along[s].start()

    def total(self):
        added = self.own(0)[...].astype(F32) + self.rx(0)[...].astype(F32)
        for s in self.order[:-1]:
            self.along[s].wait_recv()
            added = added + self.rz(s - 1)[...].astype(F32)
        return added

    def close(self):
        for s in self.order:
            self.cross[s].wait_send()
            if s:
                self.along[s].wait_send()


def back_kernel(
    triple, h_own, h_far, att_own, att_far, logsum, cosine, sine, part, weight, vectors, early, normed, tiles,
    x_fin, xc_fin, g_fin,
    grad_out, rest_out, dq_out, vec_out,
    g_s, delta_s, dq_s, dk_s, dv_s, t_s, norm_in, total, bias_s, gain_s, shift_s,
    near_f, near_o, other_f, other_o, cross_f, cross_o, moved, sum_s, sum_r, ng_s, norm_s, inv_s,
    a_own, a_rx, a_rz, a_total, b_tiles, b_rx, b_rz, b_total, held, arrived,
    n_load, a_load, a_xs, a_xr, a_zs, a_zr, b_xs, b_xr, b_zs, b_zr, k_send, k_recv, k_loc,
    v_send, v_recv, cf_send, cf_recv, co_send, co_recv, m_send, m_recv, s_send, s_recv,
    *, block, wider, step,
):
    spot = Spot()
    now = pl.program_id(0)
    tokens, wide = h_own.shape[2], x_fin.shape[2]
    width, length = 2 * wide, 2 * tokens
    heads = weight.shape[0] // (3 * HS)
    steps = tokens // block
    group = wider // block
    slow = tokens // wider
    count, depth = spot.count, spot.depth
    size = 3 * HS // count
    l0 = heads
    b1 = l0 + 2 * slow
    l1 = b1 + heads
    e0 = l1 + 2 * slow
    end = e0 + 2 * steps
    here, there = spot.row, 1 - spot.row
    at_step = lambda k: pl.when(now == k)

    sem = lambda ref, base=0: (lambda s: ref.at[base + s])
    first_sum = Scatter(
        spot, lambda p: tiles.at[p], lambda s: a_own.at[s], lambda s: a_rx.at[s], lambda s: a_rz.at[s],
        (sem(a_xs), sem(a_xr)), (sem(a_zs), sem(a_zr)),
    )

    def head_sum(h):
        return Scatter(
            spot, lambda p: b_tiles.at[p, h], lambda s: b_tiles.at[spot.along(s), h], lambda s: b_rx.at[h, s],
            lambda s: b_rz.at[h, s], (sem(b_xs, h * depth), sem(b_xr, h * depth)), (sem(b_zs, h * depth), sem(b_zr, h * depth)),
        )

    loads = [pltpu.make_async_copy(tiles.at[spot.along(s)], a_own.at[s], a_load.at[s]) for s in range(depth)]
    load_norm = [pltpu.make_async_copy(normed.at[m], norm_in, n_load.at[m]) for m in range(2)]

    def to_core(k, source, out):
        return (
            remote(spot, "col", source.at[:, pl.ds(wide, wide)], out.at[spot.col], k_send.at[k], k_recv.at[k]),
            pltpu.make_async_copy(source.at[:, pl.ds(0, wide)], out.at[spot.col], k_loc.at[k]),
        )

    a_core, b_core = to_core(0, a_total, rest_out), to_core(1, b_total, dq_out)

    partners = [{"col": 1 - spot.col}, {"row": 1 - spot.row}, {"dp": spot.z * 2 + (1 - spot.x)}]
    stride = 1
    while stride < depth:
        other_z = spot.z + stride * (1 - 2 * ((spot.z // stride) % 2))
        partners.append({"dp": other_z * 2 + spot.x})
        stride *= 2
    hops = [
        pltpu.make_async_remote_copy(
            src_ref=held.at[k], dst_ref=arrived.at[k], send_sem=v_send.at[k], recv_sem=v_recv.at[k],
            device_id=partner, device_id_type=MESH,
        )
        for k, partner in enumerate(partners)
    ]

    def over_core(which, m, i):
        k = m * steps + i
        if which == 0:
            return remote(spot, "col", other_f.at[i], cross_f.at[m, i], cf_send.at[k], cf_recv.at[k])
        return remote(spot, "col", other_o.at[i], cross_o.at[m, i], co_send.at[k], co_recv.at[k])

    def over_row(m, i):
        k = m * steps + i
        return remote(spot, "row", cross_f.at[m, i], moved.at[m, i], m_send.at[k], m_recv.at[k])

    def sums_over(m, i):
        k = m * steps + i
        return remote(spot, "col", sum_s.at[m, i], sum_r.at[m, i], s_send.at[k], s_recv.at[k])

    @at_step(0)
    def _():
        barrier = pltpu.get_barrier_semaphore()
        near = [{"col": 1 - spot.col}, {"row": 1 - spot.row}, {"dp": spot.z * 2 + (1 - spot.x)}]
        for device in near + [{"dp": spot.along(s)} for s in range(1, depth)]:
            pl.semaphore_signal(barrier, inc=1, device_id=device, device_id_type=MESH)
        load_norm[0].start()
        for load in loads:
            load.start()
        bias_s[...] = jnp.zeros_like(bias_s)
        gain_s[...] = jnp.zeros_like(gain_s)
        shift_s[...] = jnp.zeros_like(shift_s)
        pl.semaphore_wait(barrier, depth + 2)
        first_sum.begin()
        load_norm[0].wait()

    @at_step(1)
    def _():
        for load in loads:
            load.wait()

    @at_step(l0)
    def _():
        load_norm[1].start()

    @at_step(b1)
    def _():
        load_norm[1].wait()
        for i in range(steps):
            over_core(0, 0, i).wait_send()
            over_core(1, 0, i).wait_send()

    @pl.when((now < l0) | ((now >= b1) & (now < l1)))
    def _():
        head = jnp.where(now < l0, now, now - b1)
        for grad, att, place in ((h_own, att_own, here), (h_far, att_far, there)):
            at = lanes(place, tokens)
            g_s[:, at] = grad[0]
            delta_s[:, at] = jnp.sum(grad[0].astype(F32) * att[0].astype(F32), axis=0, keepdims=True)
        q_s, k_s, v_s = (triple.at[0, i * HS : (i + 1) * HS] for i in range(3))
        dk_s[...] = jnp.zeros_like(dk_s)
        dv_s[...] = jnp.zeros_like(dv_s)
        allowed = causal_tile(step)
        for i in range(length // step):
            lo, hi = i * step, (i + 1) * step
            query, grad = q_s[:, lo:hi], g_s[:, lo:hi]
            base, delta = logsum[0, 0, :, lo:hi], delta_s[:, lo:hi]
            query_grad = None
            for begin, stop in ((0, lo), (lo, hi)):
                if stop == begin:
                    continue
                raised = jnp.exp(mm(k_s[:, begin:stop], query, TN) - base)
                if begin == lo:
                    raised = jnp.where(allowed, raised, 0.0)
                prob_grad = mm(v_s[:, begin:stop], grad, TN)
                raised = raised.astype(BF16)
                score_grad = raised * (prob_grad - delta).astype(BF16)
                dv_s[:, begin:stop] += mm(grad, raised, NT)
                dk_s[:, begin:stop] += mm(query, score_grad, NT)
                term = mm(k_s[:, begin:stop], score_grad, NN)
                query_grad = term if query_grad is None else query_grad + term
            dq_s[:, lo:hi] = query_grad * HS ** (-0.5)
        cos, sin = cosine[...], sine[...]
        pieces = []
        for ref in (dq_s, dk_s):
            g1, g2 = ref[0:HALF, :], ref[HALF:ROT, :]
            pieces += [g1 * cos + g2 * sin, g2 * cos - g1 * sin, ref[ROT:HS, :]]
        pieces.append(dv_s[...])
        rounded = jnp.concatenate(pieces, axis=0).astype(BF16)
        at = pl.ds(pl.multiple_of(head * 3 * HS, HS), 3 * HS)
        t_s[at, :] = rounded
        bias_s[at, :] += jnp.sum(rounded.astype(F32), axis=1, keepdims=True)
        term = mm(t_s[at, lanes(there, tokens)], norm_in[0], NN) + mm(t_s[at, lanes(here, tokens)], norm_in[1], NN)

        @pl.when(now < l0)
        def _():
            total[head] = term

        @pl.when(now >= b1)
        def _():
            gain, shift = vectors[0:1, :], vectors[1:2, :]
            every = total[head] + term
            weights = weight[at, :].astype(F32)
            summed = bias_s[at, :]
            gain_s[...] += jnp.sum(weights * every, axis=0, keepdims=True)
            shift_s[...] += jnp.sum(weights * summed, axis=0, keepdims=True)
            every = every * gain + summed * shift
            for p in range(count):
                b_tiles[p, head] = every[p * size : (p + 1) * size].astype(BF16)
            head_sum(head).begin()

    moments = {1: 2, 2: l0, 3: b1, 0: b1 + 2} if depth == 4 else {}
    for s in first_sum.order:
        @at_step(moments.get(s, b1 + 2))
        def _():
            first_sum.fold(s)

    @pl.when((now > b1) & (now < l1))
    def _():
        before = head_sum(now - 1 - b1)
        for s in before.order:
            before.fold(s)

    @at_step(l1 + 1)
    def _():
        used = early.shape[0]
        lanes_here = held.shape[2]
        part_rows = width // (2 * lanes_here)
        held[0] = jnp.zeros_like(held[0])
        held[0, 0:used, :] = early[...]
        at = used
        for vector in (gain_s, shift_s):
            for r in range(2 * part_rows):
                mirror = (r + part_rows) % (2 * part_rows)
                plain = vector[:, r * lanes_here : (r + 1) * lanes_here]
                turned = vector[:, mirror * lanes_here : (mirror + 1) * lanes_here]
                held[0, at : at + 1, :] = jnp.where(spot.col == 0, plain, turned)
                at += 1
        line = jnp.transpose(jnp.broadcast_to(bias_s[...], (bias_s.shape[0], 128)))[0:1, :]
        mine = spot.row * 2 + spot.col
        for h in range(4 * heads):
            k = h % heads
            values = line[:, k * 3 * HS : (k + 1) * 3 * HS]
            held[0, at : at + 1, 0 : 3 * HS] = jnp.where(mine == h // heads, values, 0.0)
            at += 1

    later = now >= b1
    lead = jnp.where(later, now - l1, now - l0)

    @pl.when((lead >= 0) & (lead < 2 * slow))
    def _():
        m, half, at = jnp.where(later, 1, 0), lead // slow, lead % slow
        place = jnp.where(half == 0, there, here)
        blocks = [(j, at * group + j, slice(j * block, (j + 1) * block)) for j in range(group)]
        turned = lambda i: t_s[:, pl.ds(pl.multiple_of(place * tokens + i * block, block), block)]
        for j, i, rows in blocks:
            other = (mm(turned(i), weight[:, wide:], TN) * vectors[0:1, wide:] + part[0, 0, rows, wide:].astype(F32)).astype(BF16)

            @pl.when(half == 0)
            def _():
                other_f[i] = other
                over_core(0, m, i).start()

            @pl.when(half == 1)
            def _():
                other_o[i] = other
                over_core(1, m, i).start()

        for j, i, rows in blocks:
            near = mm(turned(i), weight[:, :wide], TN) * vectors[0:1, :wide] + part[0, 0, rows, :wide].astype(F32)

            @pl.when(half == 0)
            def _():
                near_f[j] = near

            @pl.when(half == 1)
            def _():
                near_o[m, i] = near.astype(BF16)

        @pl.when(half == 0)
        def _():
            for j, i, rows in blocks:
                over_core(0, m, i).wait_recv()
                cross_f[m, i] = (near_f[j] + cross_f[m, i].astype(F32)).astype(BF16)
                over_row(m, i).start()

    @at_step(l1 + 2)
    def _():
        before = head_sum(heads - 1)
        for s in before.order:
            before.fold(s)

    for k in range(len(hops) + 1):
        @at_step(l1 + 1 + k)
        def _():
            if k:
                hops[k - 1].wait_recv()
            if 0 < k < len(hops):
                held[k] = held[k - 1] + arrived[k - 1]
            if k < len(hops):
                hops[k].start()
            else:
                vec_out[...] = held[k - 1] + arrived[k - 1]

    @at_step(e0)
    def _():
        a_total[...] = first_sum.total()
        for copy in a_core:
            copy.start()

    trail = now - e0

    @at_step(e0 + steps - 1)
    def _():
        for h in range(heads):
            b_total[h * size : (h + 1) * size, :] = head_sum(h).total()
        for copy in b_core:
            copy.start()

    @pl.when((trail >= 0) & (trail < 2 * steps))
    def _():
        m, i, slot = trail // steps, trail % steps, trail % 2
        over_row(m, i).wait_recv()
        over_core(1, m, i).wait_recv()
        grad = near_o[m, i].astype(F32) + cross_o[m, i].astype(F32) + moved[m, i].astype(F32)
        near_x, far_x = x_fin[0].astype(F32), xc_fin[0].astype(F32)
        center = jnp.sum(near_x + far_x, axis=1, keepdims=True) / width
        spread = jnp.sum(near_x * near_x + far_x * far_x, axis=1, keepdims=True) / width - center * center
        inv = lax.rsqrt(spread + EPSILON)
        normed_x = (near_x - center) * inv
        ng_s[slot] = grad
        norm_s[slot] = normed_x
        inv_s[slot] = inv
        column = lax.broadcasted_iota(jnp.int32, (block, 128), 1)
        one = jnp.sum(grad, axis=1, keepdims=True)
        two = jnp.sum(grad * normed_x, axis=1, keepdims=True)
        sum_s[m, i] = jnp.where(column == 0, one, jnp.where(column == 1, two, 0.0))
        sums_over(m, i).start()

    @pl.when(trail > 0)
    def _():
        m, i, slot = (trail - 1) // steps, (trail - 1) % steps, (trail - 1) % 2
        sums_over(m, i).wait_recv()
        sums = (sum_s[m, i] + sum_r[m, i]) / width
        grad_out[0] = g_fin[0].astype(F32) + inv_s[slot] * (ng_s[slot] - sums[:, 0:1] - norm_s[slot] * sums[:, 1:2])

    @at_step(end)
    def _():
        for copy in (*a_core, *b_core):
            copy.wait()
        first_sum.close()
        for h in range(heads):
            head_sum(h).close()
        for k in hops:
            k.wait_send()
        for i in range(steps):
            over_core(0, 1, i).wait_send()
            over_core(1, 1, i).wait_send()
            for m in range(2):
                over_row(m, i).wait_send()
                sums_over(m, i).wait_send()


def backward(
    triple, h_own, h_far, att_own, att_far, logsum, cosine, sine, normed, part, weight, vectors, tiles, early,
    residual, xc, cotangent, block=256, wider=512, step=256,
):
    micros, rows, length = triple.shape
    tokens, wide = length // 2, residual.shape[2]
    width = 2 * wide
    heads = rows // (3 * HS)
    block, wider, step = min(block, tokens), min(wider, tokens), min(step, length)
    steps, slow = tokens // block, tokens // wider
    count, piece = tiles.shape[:2]
    depth = count // 2
    small = rows // count
    l0 = heads
    b1 = l0 + 2 * slow
    l1 = b1 + heads
    e0 = l1 + 2 * slow

    def head_of(s):
        late = s >= b1
        return jnp.where(late, 1, 0), jnp.minimum(jnp.where(late, s - b1, s), heads - 1)

    def part_at(s):
        late = s >= b1
        number = jnp.clip(jnp.where(late, s - l1, s - l0), 0, 2 * slow - 1)
        return jnp.where(late, 1, 0), number // slow, number % slow, 0

    def in_at(s):
        number = jnp.clip(s - e0, 0, 2 * steps - 1)
        return number // steps, number % steps, 0

    def out_at(s):
        number = jnp.clip(s - e0 - 1, 0, 2 * steps - 1)
        return number // steps, number % steps, 0

    narrow = pl.BlockSpec((1, HS, tokens), lambda s: (*head_of(s), 0))
    fin_in = pl.BlockSpec((1, block, wide), in_at)
    fin_out = pl.BlockSpec((1, block, wide), out_at)
    hops = 3 + max(depth - 1, 0).bit_length()
    vec_rows = early.shape[0] + 2 * (width // early.shape[1]) + 4 * heads
    pair = lambda dtype: pltpu.VMEM((micros, steps, block, wide), dtype)
    single = lambda dtype: pltpu.VMEM((steps, block, wide), dtype)
    sems = Gather.sems
    return pl.pallas_call(
        partial(back_kernel, block=block, wider=wider, step=step),
        grid=(e0 + 2 * steps + 1,),
        in_specs=[
            pl.BlockSpec((1, 3 * HS, length), lambda s: (*head_of(s), 0)), narrow, narrow, narrow, narrow,
            pl.BlockSpec((1, 1, 1, length), lambda s: (*head_of(s), 0, 0)), whole(cosine.shape), whole(sine.shape),
            pl.BlockSpec((1, 1, wider, width), part_at),
            whole(weight.shape), whole(vectors.shape), whole(early.shape), ANYWHERE, ANYWHERE, fin_in, fin_in, fin_out,
        ],
        out_specs=[fin_out, ANYWHERE, ANYWHERE, whole((vec_rows, early.shape[1]))],
        out_shape=[
            jax.ShapeDtypeStruct((micros, tokens, wide), F32),
            jax.ShapeDtypeStruct((2, piece, wide), F32),
            jax.ShapeDtypeStruct((2, small, wide), F32),
            jax.ShapeDtypeStruct((vec_rows, early.shape[1]), F32),
        ],
        scratch_shapes=[
            pltpu.VMEM((HS, length), BF16),
            pltpu.VMEM((1, length), F32),
            pltpu.VMEM((HS, length), F32),
            pltpu.VMEM((HS, length), F32),
            pltpu.VMEM((HS, length), F32),
            pltpu.VMEM((rows, length), BF16),
            pltpu.VMEM((2, tokens, width), BF16),
            pltpu.VMEM((heads, 3 * HS, width), F32),
            pltpu.VMEM((rows, 1), F32),
            pltpu.VMEM((1, width), F32), pltpu.VMEM((1, width), F32),
            pltpu.VMEM((wider // block, block, wide), F32), pair(BF16), single(BF16), single(BF16), pair(BF16), pair(BF16),
            pair(BF16),
            pltpu.VMEM((micros, steps, block, 128), F32), pltpu.VMEM((micros, steps, block, 128), F32),
            pltpu.VMEM((2, block, wide), F32), pltpu.VMEM((2, block, wide), F32), pltpu.VMEM((2, block, 1), F32),
            pltpu.VMEM((depth, piece, width), BF16), pltpu.VMEM((depth, piece, width), BF16),
            pltpu.VMEM((depth - 1, piece, width), BF16), pltpu.VMEM((piece, width), F32),
            pltpu.VMEM((count, heads, small // heads, width), BF16),
            pltpu.VMEM((heads, depth, small // heads, width), BF16),
            pltpu.VMEM((heads, depth - 1, small // heads, width), BF16),
            pltpu.VMEM((small, width), F32),
            pltpu.VMEM((hops, vec_rows, early.shape[1]), F32), pltpu.VMEM((hops, vec_rows, early.shape[1]), F32),
            sems(2), sems(depth), sems(depth), sems(depth), sems(depth), sems(depth),
            *[sems(depth * heads) for _ in range(4)], sems(2), sems(2), sems(2),
            sems(hops), sems(hops), *[sems(micros * steps) for _ in range(8)],
        ],
        compiler_params=params(collective_id=3, has_side_effects=True),
        cost_estimate=cost(micros * (heads * length * length * 256 * 5 + length * width * 4 * rows), 100 << 20),
        name="backward",
    )(
        triple, h_own, h_far, att_own, att_far, logsum, cosine, sine, part, weight, vectors, early, normed, tiles,
        residual, xc, cotangent,
    )


def pick(value, index, axis=0):
    return lax.dynamic_index_in_dim(value, index, axis, keepdims=False)


def body(
    residual, attend_norm_gain, attend_norm_bias, expand_norm_gain, expand_norm_bias,
    attend_weight, attend_bias, output_weight, output_bias, expand_weight, expand_bias,
    shrink_weight, shrink_bias, cotangent,
):
    count = lax.axis_size("dp")
    row, col = lax.axis_index("row"), lax.axis_index("col")
    micros, tokens, wide = residual.shape
    width, length = 2 * wide, 2 * tokens
    heads = attend_weight.shape[1] // 2
    head_part, out_part = attend_weight.shape[2], output_weight.shape[1]
    hid = expand_weight.shape[1] // 2

    def sides(rows):
        return pick(rows, col), pick(rows, 1 - col)

    head_mine, head_theirs = sides(attend_weight.transpose(1, 2, 0).reshape(2, heads * head_part, wide))
    rest_mine, rest_theirs = sides(
        jnp.concatenate(
            [
                output_weight.reshape(2, heads * out_part, wide),
                expand_weight.T.reshape(2, hid, wide),
                shrink_weight.reshape(2, hid, wide),
            ],
            axis=1,
        )
    )

    vectors = jnp.stack([attend_norm_gain, attend_norm_bias, expand_norm_gain, expand_norm_bias])
    vectors = jnp.concatenate([jnp.roll(vectors, -col * wide, axis=1), jnp.zeros((4, width), F32)])
    head_begin = row * 2 * heads + col * heads
    bias_q = lax.dynamic_slice_in_dim(attend_bias, head_begin, heads, 0).reshape(-1, 1)
    bias_1 = pick(expand_bias.reshape(count, 4, hid), row * 2 + col, 1).reshape(1, -1)
    out_bias = lax.dynamic_slice_in_dim(output_bias + shrink_bias, col * wide, wide, 0).reshape(1, -1)
    powers = 10000.0 ** (-np.arange(HALF) * (2.0 / ROT))
    angles = powers[:, None] * np.arange(length)[None, :]
    cosine, sine = jnp.asarray(np.cos(angles), F32), jnp.asarray(np.sin(angles), F32)

    normed, second, triple, wq, att_own, att_far, logsum, pieces, xc, cb0, cc, cd0 = forward(
        residual, bias_q, vectors, cosine, sine, head_mine, head_theirs, rest_mine, rest_theirs, cotangent, count
    )
    lo = heads * out_part
    wo = pieces[:, :lo].reshape(count, heads, out_part, width).transpose(1, 0, 2, 3).reshape(heads * HS, width)
    outputs, h_own, h_far, part, tiles, dvec, db1, _, _ = middle(
        second, normed, residual, cotangent, cc, cb0, cd0, att_own, att_far, pieces, wo, bias_1, vectors, out_bias
    )

    dout = jnp.sum(cotangent.astype(F32), axis=(0, 1))
    dout = lax.dynamic_update_slice_in_dim(jnp.zeros((width,), F32), dout, col * wide, 0)
    dvec = jnp.roll(dvec[:2], col * wide, axis=1)
    db1 = lax.dynamic_update_slice_in_dim(
        jnp.zeros((count, 4, hid), F32), db1.reshape(count, 1, hid), row * 2 + col, 1
    )
    lane = 256
    early = jnp.concatenate([db1.reshape(-1, lane), dout.reshape(-1, lane), dvec.reshape(-1, lane)])
    early = jnp.pad(early, ((0, -early.shape[0] % 8), (0, 0)))

    grads, rest_sum, dq_sum, vec = backward(
        triple, h_own, h_far, att_own, att_far, logsum, cosine, sine, normed, part, wq, vectors, tiles, early,
        residual, xc, cotangent,
    )
    attend_weight_grad = dq_sum.reshape(2 * heads, head_part, wide).transpose(2, 0, 1)
    output_weight_grad = rest_sum[:, :lo].reshape(2 * heads, out_part, wide)
    expand_weight_grad = rest_sum[:, lo : lo + hid].reshape(2 * hid, wide).T
    shrink_weight_grad = rest_sum[:, lo + hid :].reshape(2 * hid, wide)

    n1, nw, ne = db1.size // lane, width // lane, early.shape[0]
    cut = lambda at, rows: vec[at : at + rows].reshape(-1)
    dout = cut(n1, nw)
    return (
        outputs, grads, cut(ne, nw), cut(ne + nw, nw), cut(n1 + nw, nw), cut(n1 + 2 * nw, nw),
        attend_weight_grad, vec[ne + 2 * nw :, : 3 * HS], output_weight_grad, dout, expand_weight_grad, cut(0, n1),
        shrink_weight_grad, dout,
    )


def solution(mesh):
    tokens = P(None, ("dp", "row"), "col")
    weights = (P("col", "row", "dp"), P("row", "dp", "col"), P("col", ("dp", "row")), P(("dp", "row"), "col"))
    one = P()
    in_specs = (tokens, one, one, one, one, weights[0], one, weights[1], one, weights[2], one, weights[3], one, tokens)
    out_specs = (tokens, tokens, one, one, one, one, weights[0], one, weights[1], one, weights[2], one, weights[3], one)
    return jax.shard_map(body, mesh=mesh, in_specs=in_specs, out_specs=out_specs, check_vma=False)
```

```python
from functools import partial

import jax
import jax.numpy as jnp
import numpy as np
from jax import lax
from jax.experimental import pallas as pl
from jax.experimental.pallas import tpu as pltpu
from jax.sharding import PartitionSpec as P

D = 1024
HS = 64
ROT = 16
HALF = ROT // 2
EPSILON = 1e-05
MASKED = -1e30
NN = (((1,), (0,)), ((), ()))
NT = (((1,), (1,)), ((), ()))
TN = (((0,), (0,)), ((), ()))
VMEM_LIMIT = 60 << 20
F32 = jnp.float32
BF16 = jnp.bfloat16


def mm(a, b, dims):
    return lax.dot_general(a, b, dims, preferred_element_type=F32)


def params(**extra):
    return pltpu.CompilerParams(vmem_limit_bytes=VMEM_LIMIT, **extra)


def cost(flops, nbytes):
    return pl.CostEstimate(flops=int(flops), bytes_accessed=int(nbytes), transcendentals=0)


def whole(shape):
    return pl.BlockSpec(shape, lambda *_: (0,) * len(shape))


MESH = pl.DeviceIdType.MESH
ANYWHERE = pl.BlockSpec(memory_space=pl.ANY)


class Spot:
    def __init__(self):
        self.count = lax.axis_size("dp")
        self.depth = self.count // 2
        self.dp, self.row, self.col = (lax.axis_index(a) for a in ("dp", "row", "col"))
        self.z, self.x = self.dp // 2, self.dp % 2

    def along(self, steps):
        return ((self.z + steps) % self.depth) * 2 + self.x

    def device(self, which):
        return {
            "row": {"row": 1 - self.row},
            "col": {"col": 1 - self.col},
            "x": {"dp": self.z * 2 + (1 - self.x)},
            "right": {"dp": self.along(1)},
            "left": {"dp": self.along(self.depth - 1)},
        }[which]

    def greet(self, *names):
        barrier = pltpu.get_barrier_semaphore()
        for name in names:
            pl.semaphore_signal(barrier, inc=1, device_id=self.device(name), device_id_type=MESH)
        pl.semaphore_wait(barrier, len(names))


def remote(spot, which, source, target, send, recv):
    return pltpu.make_async_remote_copy(
        src_ref=source, dst_ref=target, send_sem=send, recv_sem=recv,
        device_id=spot.device(which), device_id_type=MESH,
    )


class Gather:
    def __init__(self, spot, mine, theirs, all_ref, local, send, recv):
        self.spot, self.all = spot, all_ref
        wide = mine.shape[1]
        here = all_ref.at[spot.dp]
        depth = spot.depth
        self.local = pltpu.make_async_copy(mine, here.at[:, pl.ds(0, wide)], local)
        self.core = remote(spot, "col", theirs, here.at[:, pl.ds(wide, wide)], send.at[0], recv.at[0])
        self.ring, self.cross = [], []
        for k in range(depth):
            slot = all_ref.at[spot.along(depth - k)]
            self.cross.append(remote(spot, "x", slot, slot, send.at[1 + k], recv.at[1 + k]))
            if k < depth - 1:
                at = 1 + depth + k
                self.ring.append(remote(spot, "right", slot, slot, send.at[at], recv.at[at]))

    @staticmethod
    def sems(count):
        return pltpu.SemaphoreType.DMA((count,))

    @staticmethod
    def parts(spot, mine, theirs, all_ref, local, send, recv):
        rows = mine.shape[0]
        cuts = 2 if rows % 32 == 0 else 1
        size, slots = rows // cuts, send.shape[0] // 2
        found = []
        for c in range(cuts):
            part, sems = pl.ds(c * size, size), pl.ds(c * slots, slots)
            found.append(
                Gather(
                    spot, mine.at[part], theirs.at[part], all_ref.at[:, part], local.at[c], send.at[sems], recv.at[sems]
                )
            )
        return found

    def begin(self):
        self.local.start()
        self.core.start()

    def first(self):
        self.local.wait()
        self.core.wait_recv()
        self.ring[0].start()
        self.cross[0].start()

    def forward(self, k):
        self.ring[k - 1].wait_recv()
        if k < len(self.ring):
            self.ring[k].start()
        self.cross[k].start()

    def arrive(self):
        for copy in self.cross:
            copy.wait_recv()

    def close(self):
        for copy in (self.core, *self.ring, *self.cross):
            copy.wait_send()


def lanes(index, tokens):
    return pl.ds(pl.multiple_of(index * tokens, tokens), tokens)


def forward_kernel(
    xa, bias, vectors, cosine, sine, head_mine, head_theirs, mine, theirs, tokens, grads,
    plain, second, triple, weight_out, att_own, att_far, logsum, all_ref, xc, cb0, cc, cd0,
    x_s, first, q_s, v_s, o_s, xc_s, near_s, far_s, pieces, weight,
    a_local, a_send, a_recv, local, send, recv, y_send, y_recv, c_send, c_recv, t_sem, *, block, step, chunks, rows_at_once,
):
    spot = Spot()
    now = pl.program_id(0)
    wide = xa.shape[2]
    width = 2 * wide
    own_tokens = tokens.shape[1]
    length = 2 * own_tokens
    blocks = own_tokens // block
    heads = weight.shape[0] // (3 * HS)
    depth, count = spot.depth, spot.count
    cast0 = 2 * blocks
    far0 = 2 * cast0
    attend0 = far0 + blocks
    far1 = attend0 + heads
    attend1 = far1 + blocks
    end = attend1 + heads - 1
    here, there = spot.row, 1 - spot.row
    at = lambda k: pl.when(now == k)

    head_parts = Gather.parts(spot, head_mine, head_theirs, pieces, a_local, a_send, a_recv)
    rest_parts = Gather.parts(spot, mine, theirs, all_ref, local, send, recv)
    size = own_tokens // chunks
    part = lambda k: pl.ds(k * size, size)
    x_row = [
        [remote(spot, "row", tokens.at[m, part(k)], near_s.at[m, part(k)], y_send.at[m * chunks + k], y_recv.at[m * chunks + k]) for k in range(chunks)]
        for m in range(2)
    ]
    x_col = [
        [remote(spot, "col", near_s.at[m, part(k)], far_s.at[m, part(k)], c_send.at[m * chunks + k], c_recv.at[m * chunks + k]) for k in range(chunks)]
        for m in range(2)
    ]
    x_core = [remote(spot, "col", tokens.at[m], xc_s.at[m], c_send.at[2 * chunks + m], c_recv.at[2 * chunks + m]) for m in range(2)]
    g_row = remote(spot, "row", grads.at[0], cb0, y_send.at[2 * chunks], y_recv.at[2 * chunks])
    g_col = remote(spot, "col", cb0, cd0, c_send.at[2 * chunks + 2], c_recv.at[2 * chunks + 2])
    g_core = remote(spot, "col", grads, cc, c_send.at[2 * chunks + 3], c_recv.at[2 * chunks + 3])
    keep = [pltpu.make_async_copy(q_s.at[m], triple.at[m], t_sem.at[m]) for m in range(2)]
    keep_weight = pltpu.make_async_copy(weight, weight_out, t_sem.at[2])
    keep_core = pltpu.make_async_copy(xc_s, xc, t_sem.at[3])

    @at(0)
    def _():
        spot.greet("row", "col", "x", "right", "left")
        for gather in head_parts:
            gather.begin()
        for copy in x_row[0]:
            copy.start()
        x_core[0].start()
        for gather in rest_parts:
            gather.begin()
        for gather in head_parts:
            gather.first()
        x_core[1].start()
        x_core[0].wait_recv()

    @at(1)
    def _():
        head_parts[0].forward(1)

    @at(blocks)
    def _():
        for gather in head_parts[1:]:
            gather.forward(1)
        x_core[1].wait_recv()
        keep_core.start()

    @at(cast0)
    def _():
        for k in range(2, depth):
            for gather in head_parts:
                gather.forward(k)
        for gather in rest_parts:
            gather.first()
        for gather in head_parts:
            gather.arrive()
        for copy in x_row[1]:
            copy.start()
        size = weight.shape[0] // (heads * count)
        for h in range(heads):
            small = [pieces[p, h * size : (h + 1) * size, :].astype(F32) for p in range(count)]
            weight[h * 3 * HS : (h + 1) * 3 * HS, :] = jnp.concatenate(small, axis=0).astype(BF16)
        keep_weight.start()

    @at(cast0 + 1)
    def _():
        for k in range(chunks):
            x_row[0][k].wait_recv()
            x_col[0][k].start()

    @at(far0)
    def _():
        for k in range(chunks):
            x_col[0][k].wait_recv()
        g_core.start()

    moments = {(1, 0): cast0 + 3, (1, 1): far0, (2, 0): attend0 + 1, (2, 1): attend0 + 2, (3, 0): far1, (3, 1): attend1}
    for k in range(1, depth):
        for c, gather in enumerate(rest_parts):
            @at(moments.get((k, c), attend1) if depth == 4 else attend1)
            def _():
                gather.forward(k)

    @at(far1 - 2)
    def _():
        for k in range(chunks):
            x_row[1][k].wait_recv()
            x_col[1][k].start()
        g_row.start()

    @at(far1)
    def _():
        for k in range(chunks):
            x_col[1][k].wait_recv()

    norming = (now < cast0) | ((now >= far0) & (now < attend0)) | ((now >= far1) & (now < attend1))

    @pl.when(now < cast0)
    def _():
        lo = pl.multiple_of((now % blocks) * block, block)
        x_s[:, :wide] = xa[0]
        x_s[:, wide:] = xc_s[now // blocks, pl.ds(lo, block), :]

    for begin, m in ((far0, 0), (far1, 1)):
        @pl.when((now >= begin) & (now < begin + blocks))
        def _():
            lo = pl.multiple_of((now - begin) * block, block)
            x_s[:, :wide] = near_s[m, pl.ds(lo, block), :]
            x_s[:, wide:] = far_s[m, pl.ds(lo, block), :]

    slot = jnp.where(now < far0, now % cast0, (now - far0) % blocks)
    slot = jnp.where(now >= far1, now - far1, slot)

    @pl.when(norming)
    def _():
        for lo in range(0, block, rows_at_once):
            rows = slice(lo, lo + rows_at_once)
            values = x_s[rows, :].astype(F32)
            center = jnp.sum(values, axis=1, keepdims=True) / width
            spread = jnp.sum(values * values, axis=1, keepdims=True) / width - center * center
            normed = (values - center) * lax.rsqrt(spread + EPSILON)
            plain[0, 0, rows, :] = normed.astype(BF16)
            first[slot, rows, :] = (normed * vectors[0:1, :] + vectors[1:2, :]).astype(BF16)
            second[0, 0, rows, :] = (normed * vectors[2:3, :] + vectors[3:4, :]).astype(BF16)

    casting = ((now >= cast0) & (now < attend0)) | ((now >= far1) & (now < attend1))

    @pl.when(casting)
    def _():
        number = now - cast0
        micro = jnp.where(now < far0, number // blocks, jnp.where(now < attend0, 0, 1))
        half = jnp.where(now < far0, here, there)
        block_at = jnp.where(now >= far1, now - far1, number % blocks)
        lane = pl.ds(pl.multiple_of(half * own_tokens + block_at * block, block), block)
        cos, sin = cosine[:, lane], sine[:, lane]
        every = mm(weight[...], first[slot], NT) + bias[...]
        for head in range(heads):
            base = head * 3 * HS
            rows = every[base : base + 3 * HS]
            parts = []
            for which in range(2):
                lo = which * HS
                scale = HS ** (-0.5) if which == 0 else 1.0
                u1, u2 = rows[lo : lo + HALF], rows[lo + HALF : lo + ROT]
                parts += [(u1 * cos - u2 * sin) * scale, (u2 * cos + u1 * sin) * scale, rows[lo + ROT : lo + HS] * scale]
            parts.append(rows[2 * HS :])
            q_s[micro, base : base + 3 * HS, lane] = jnp.concatenate(parts, axis=0).astype(BF16)

    @at(attend0)
    def _():
        keep[0].start()

    @at(attend1)
    def _():
        keep[1].start()

    attending = ((now >= attend0) & (now < far1)) | (now >= attend1)

    @pl.when(attending)
    def _():
        micro = jnp.where(now < far1, 0, 1)
        head = jnp.where(now < far1, now - attend0, now - attend1)
        base = pl.multiple_of(head * 3 * HS, HS)
        query_of = lambda lo, hi: q_s[micro, pl.ds(base, HS), lo:hi]
        keys_of = lambda lo, hi: q_s[micro, pl.ds(pl.multiple_of(base + HS, HS), HS), lo:hi]
        v_s[0:HS, :] = q_s[micro, pl.ds(pl.multiple_of(base + 2 * HS, HS), HS), :]
        extra = lax.broadcasted_iota(jnp.int32, (16, length), 0)
        v_s[HS : HS + 16, :] = jnp.where(extra == 0, 1.0, 0.0).astype(BF16)
        allowed = causal_tile(step)
        for i in range(length // step):
            lo, hi = i * step, (i + 1) * step
            query = query_of(lo, hi)
            diag = jnp.where(allowed, mm(keys_of(lo, hi), query, TN), MASKED)
            highest = jnp.max(diag, axis=0, keepdims=True)
            if i:
                past = mm(keys_of(0, lo), query, TN)
                highest = jnp.maximum(highest, jnp.max(past, axis=0, keepdims=True))
            raised = jnp.exp(diag - highest).astype(BF16)
            result = mm(v_s[:, lo:hi], raised, NN)
            if i:
                raised = jnp.exp(past - highest).astype(BF16)
                result = result + mm(v_s[:, :lo], raised, NN)
            total = result[HS : HS + 1]
            o_s[:, lo:hi] = (result[:HS] / total).astype(BF16)
            logsum[0, 0, :, lo:hi] = highest + jnp.log(total)
        att_own[0] = o_s[:, lanes(here, own_tokens)]
        att_far[0] = o_s[:, lanes(there, own_tokens)]

    @at(end)
    def _():
        g_row.wait_recv()
        g_col.start()
        for gather in rest_parts:
            gather.arrive()
        for gather in (*rest_parts, *head_parts):
            gather.close()
        g_col.wait()
        g_core.wait()
        for m in range(2):
            x_core[m].wait_send()
            for k in range(chunks):
                x_row[m][k].wait_send()
                x_col[m][k].wait_send()
        g_row.wait_send()
        keep[0].wait()
        keep[1].wait()
        keep_weight.wait()
        keep_core.wait()


def forward(residual, bias, vectors, cosine, sine, head_mine, head_theirs, mine, theirs, cotangent, count, block=512, step=512):
    micros, tokens, wide = residual.shape
    width, length = 2 * wide, 2 * tokens
    block, step = min(block, tokens), min(step, length)
    blocks = tokens // block
    rows = bias.shape[0]
    heads = rows // (3 * HS)
    depth = count // 2
    chunks = 4
    cast0 = 2 * blocks
    far0 = 2 * cast0
    a0 = far0 + blocks
    f1 = a0 + heads
    a1 = f1 + blocks
    steps = a1 + heads
    own = pl.BlockSpec((1, block, wide), lambda i: (jnp.minimum(i, cast0 - 1) // blocks, jnp.minimum(i, cast0 - 1) % blocks, 0))

    def place(i):
        early = jnp.minimum(i, cast0 - 1)
        late = i >= f1
        far = i >= far0
        micro = jnp.where(late, 1, jnp.where(far, 0, early // blocks))
        number = jnp.where(late, jnp.minimum(i - f1, blocks - 1), jnp.where(far, jnp.minimum(i - far0, blocks - 1), early % blocks))
        return micro, jnp.where(far, 0, 1), number, 0

    def head_of(i):
        late = i >= a1
        return jnp.where(late, 1, 0), jnp.where(late, i - a1, jnp.clip(i - a0, 0, heads - 1))

    normal = pl.BlockSpec((1, 1, block, width), place)
    att = pl.BlockSpec((1, HS, tokens), lambda i: (*head_of(i), 0))
    half = jax.ShapeDtypeStruct((tokens, wide), BF16)
    piece = mine.shape[0]
    sems = Gather.sems
    return pl.pallas_call(
        partial(forward_kernel, block=block, step=step, chunks=chunks, rows_at_once=min(64, block)),
        grid=(steps,),
        in_specs=[
            own, whole(bias.shape), whole(vectors.shape), whole(cosine.shape), whole(sine.shape), *[ANYWHERE] * 6,
        ],
        out_specs=[
            normal, normal, ANYWHERE, ANYWHERE, att, att,
            pl.BlockSpec((1, 1, 1, length), lambda i: (*head_of(i), 0, 0)), *[ANYWHERE] * 5,
        ],
        out_shape=[
            jax.ShapeDtypeStruct((micros, 2, tokens, width), BF16),
            jax.ShapeDtypeStruct((micros, 2, tokens, width), BF16),
            jax.ShapeDtypeStruct((micros, rows, length), BF16),
            jax.ShapeDtypeStruct((rows, width), BF16),
            jax.ShapeDtypeStruct((micros, heads * HS, tokens), BF16),
            jax.ShapeDtypeStruct((micros, heads * HS, tokens), BF16),
            jax.ShapeDtypeStruct((micros, heads, 1, length), F32),
            jax.ShapeDtypeStruct((count, piece, width), BF16),
            jax.ShapeDtypeStruct(residual.shape, BF16), half, jax.ShapeDtypeStruct(cotangent.shape, BF16), half,
        ],
        scratch_shapes=[
            pltpu.VMEM((block, width), BF16),
            pltpu.VMEM((cast0, block, width), BF16),
            pltpu.VMEM((micros, rows, length), BF16),
            pltpu.VMEM((HS + 16, length), BF16),
            pltpu.VMEM((HS, length), BF16),
            pltpu.VMEM((micros, tokens, wide), BF16),
            pltpu.VMEM((micros, tokens, wide), BF16),
            pltpu.VMEM((micros, tokens, wide), BF16),
            pltpu.VMEM((count, rows // count, width), BF16),
            pltpu.VMEM((rows, width), BF16),
            sems(2), sems(4 * depth), sems(4 * depth), sems(2), sems(4 * depth), sems(4 * depth),
            sems(2 * chunks + 1), sems(2 * chunks + 1), sems(2 * chunks + 4), sems(2 * chunks + 4), sems(4),
        ],
        compiler_params=params(collective_id=1, has_side_effects=True),
        cost_estimate=cost(micros * length * width * rows * 2 + micros * heads * length * length * 256 * 2, 40 << 20),
        name="forward",
    )(residual, bias, vectors, cosine, sine, head_mine, head_theirs, mine, theirs, residual, cotangent)
def causal_tile(size):
    keys = lax.broadcasted_iota(jnp.int32, (size, size), 0)
    places = lax.broadcasted_iota(jnp.int32, (size, size), 1)
    return keys <= places


def lanes(index, tokens):
    return pl.ds(pl.multiple_of(index * tokens, tokens), tokens)


POLY = (0.254829592, -0.284496736, 1.421413741, -1.453152027, 1.061405429)


def gelu_pair(value):
    magnitude = jnp.abs(value)
    t = 1.0 / (1.0 + magnitude * (0.3275911 * 0.5**0.5))
    bell = jnp.exp(value * value * -0.5)
    series = POLY[4]
    for term in (POLY[3], POLY[2], POLY[1], POLY[0]):
        series = series * t + term
    tail = 0.5 * series * t * bell
    cumulative = jnp.where(value >= 0.0, 1.0 - tail, tail)
    return value * cumulative, cumulative + value * bell * (1.0 / (2.0 * np.pi) ** 0.5)


def column_of(row):
    return jnp.transpose(jnp.broadcast_to(row, (128, row.shape[1])))[:, 0:1]


def middle_kernel(
    second, normed, ca, cc, cb0, cd0, att_own, att_far, pieces, wo, bias, vectors, out_bias, grads, x_fin,
    out, heads_own, heads_far, part, tiles, dvec, dbias, cb1, cd1,
    w1, w2, dw1, dw2, dwo, n_s, f_s, c_s, a_s, act_s, eg_s,
    near_f, near_o, other_f, other_o, cross_f, cross_o, y_s, moved,
    w_sem, l_sem, y_send, y_recv, c_send, c_recv, cf_send, cf_recv, co_send, co_recv, m_send, m_recv,
    *, block, chunk, out_part,
):
    spot = Spot()
    now = pl.program_id(0)
    wide = ca.shape[2]
    count, rows, width = pieces.shape
    hid = w1.shape[0] // count
    heads = wo.shape[0] // HS
    steps = ca_steps = grads.shape[1] // block
    end = 4 * steps
    micro, half, at = now // (2 * steps), (now // steps) % 2, now % steps
    g_row = remote(spot, "row", grads.at[1], cb1, y_send, y_recv)
    g_col = remote(spot, "col", cb1, cd1, c_send, c_recv)
    load_near = pltpu.make_async_copy(cb1, n_s, l_sem.at[0])
    load_far = pltpu.make_async_copy(cd1, f_s, l_sem.at[1])

    def over_core(which, m, i):
        k = m * steps + i
        if which == 0:
            return remote(spot, "col", other_f.at[m, i], cross_f.at[m, i], cf_send.at[k], cf_recv.at[k])
        return remote(spot, "col", other_o.at[m, i], cross_o.at[m, i], co_send.at[k], co_recv.at[k])

    def over_row(m, i):
        k = m * steps + i
        return remote(spot, "row", y_s.at[m, i], moved.at[m, i], m_send.at[k], m_recv.at[k])

    @pl.when(now == 0)
    def _():
        spot.greet("row", "col")
        g_row.start()
        lo = heads * out_part
        copies = []
        for p in range(count):
            here = slice(p * hid, (p + 1) * hid)
            copies.append(pltpu.make_async_copy(pieces.at[p, lo : lo + hid], w1.at[here], w_sem.at[2 * p]))
            copies.append(pltpu.make_async_copy(pieces.at[p, lo + hid :], w2.at[here], w_sem.at[2 * p + 1]))
        for copy in copies:
            copy.start()
        dw1[...] = jnp.zeros_like(dw1)
        dw2[...] = jnp.zeros_like(dw2)
        dwo[...] = jnp.zeros_like(dwo)
        dbias[...] = jnp.zeros_like(dbias)
        for copy in copies:
            copy.wait()

    @pl.when(now == 2 * steps)
    def _():
        load_near.wait()
        load_far.wait()

    before = now - 1

    @pl.when((now > 0) & ((before // steps) % 2 == 0) & (now < end))
    def _():
        m, i = before // (2 * steps), before % steps
        over_core(0, m, i).wait_recv()
        y_s[m, i] = (near_f[...] + cross_f[m, i].astype(F32)).astype(BF16)
        over_row(m, i).start()

    def finish(m, i):
        over_row(m, i).wait_recv()
        over_core(1, m, i).wait_recv()
        out[0] = (
            x_fin[0].astype(F32) + near_o[m, i].astype(F32) + cross_o[m, i].astype(F32)
            + moved[m, i].astype(F32) + out_bias[...]
        ).astype(BF16)

    @pl.when((now >= 2 * steps) & (now < 3 * steps))
    def _():
        finish(0, now - 2 * steps)

    @pl.when(now > 3 * steps)
    def _():
        finish(1, now - 3 * steps - 1)

    @pl.when((half == 0) & (now < steps))
    def _():
        c_s[:, :wide] = cb0[...]
        c_s[:, wide:] = cd0[...]

    @pl.when((half == 0) & (now >= 2 * steps) & (now < end))
    def _():
        here = pl.ds(pl.multiple_of(at * block, block), block)
        c_s[:, :wide] = n_s[here, :]
        c_s[:, wide:] = f_s[here, :]

    @pl.when((half == 1) & (now < end))
    def _():
        c_s[:, :wide] = ca[0]
        c_s[:, wide:] = cc[0]
        a_s[...] = att_own[0]

    @pl.when((half == 0) & (now < end))
    def _():
        a_s[...] = att_far[0]

    @pl.when(now < end)
    def _():
        hidden = w1.shape[0]
        for lo in range(0, hidden, chunk):
            hi = lo + chunk
            expanded = mm(second[0, 0], w1[lo:hi, :], NT) + bias[:, lo:hi]
            active, slope = gelu_pair(expanded)
            act_s[:, lo:hi] = active.astype(BF16)
            rounded = (mm(c_s[...], w2[lo:hi, :], NT) * slope).astype(BF16)
            eg_s[:, lo:hi] = rounded
            dbias[:, lo:hi] += jnp.sum(rounded.astype(F32), axis=0, keepdims=True)
        for lo in range(0, hidden, chunk):
            hi = lo + chunk
            dw2[lo:hi, :] += mm(act_s[:, lo:hi], c_s[...], TN)
            dw1[lo:hi, :] += mm(eg_s[:, lo:hi], normed[0, 0], TN)
        dwo[...] += mm(a_s[...], c_s[...], NN)
        near = mm(act_s[...], w2[:, :wide], NN) + mm(a_s[...], wo[:, :wide], TN)
        other = (mm(act_s[...], w2[:, wide:], NN) + mm(a_s[...], wo[:, wide:], TN)).astype(BF16)
        part[0, 0] = (mm(eg_s[...], w1[...], NN) * vectors[2:3, :]).astype(BF16)
        heads_grad = mm(wo[...], c_s[...], NT).astype(BF16)

        @pl.when(half == 0)
        def _():
            heads_far[0] = heads_grad
            near_f[...] = near
            other_f[micro, at] = other
            over_core(0, micro, at).start()

        @pl.when(half == 1)
        def _():
            heads_own[0] = heads_grad
            near_o[micro, at] = near.astype(BF16)
            other_o[micro, at] = other
            over_core(1, micro, at).start()

    @pl.when(now == 2 * steps - 2)
    def _():
        g_row.wait_recv()
        g_col.start()

    @pl.when(now == 2 * steps - 1)
    def _():
        g_col.wait_recv()
        load_near.start()
        load_far.start()

    @pl.when(now == end)
    def _():
        lo = heads * out_part
        summed = column_of(dbias[...])
        gain_grad = jnp.zeros((1, width), F32)
        bias_grad = jnp.zeros((1, width), F32)
        for p in range(count):
            here = slice(p * hid, (p + 1) * hid)
            small = [dwo[h * HS + p * out_part : h * HS + (p + 1) * out_part, :] for h in range(heads)]
            tiles[p, :lo] = jnp.concatenate(small, axis=0).astype(BF16)
            tiles[p, lo : lo + hid] = (dw1[here, :] * vectors[2:3, :] + summed[here] * vectors[3:4, :]).astype(BF16)
            tiles[p, lo + hid :] = dw2[here, :].astype(BF16)
            weight = w1[here, :].astype(F32)
            gain_grad += jnp.sum(weight * dw1[here, :], axis=0, keepdims=True)
            bias_grad += jnp.sum(weight * summed[here], axis=0, keepdims=True)
        dvec[0:1, :] = gain_grad
        dvec[1:2, :] = bias_grad
        g_row.wait_send()
        g_col.wait_send()
        for m in range(2):
            for i in range(steps):
                over_core(0, m, i).wait_send()
                over_core(1, m, i).wait_send()
                over_row(m, i).wait_send()


def middle(second, normed, residual, cotangent, cc, cb0, cd0, att_own, att_far, pieces, wo, bias, vectors, out_bias, block=512, chunk=1024):
    micros, tokens, wide = cotangent.shape
    count, rows, width = pieces.shape
    block = min(block, tokens)
    steps = tokens // block
    hidden, head_rows = bias.shape[1], wo.shape[0]
    hid = hidden // count
    out_part = (rows - 2 * hid) * HS // head_rows
    end, top = steps - 1, 4 * steps - 1

    def place(s):
        s = jnp.minimum(s, top)
        return s // (2 * steps), (s // steps) % 2, s % steps

    def own_at(s):
        m, h, i = place(s)
        return m, h * i

    def far_at(s):
        m, h, i = place(s)
        return m, i * (1 - h) + end * h

    def finished(s):
        late = s > 3 * steps
        number = jnp.where(late, s - 3 * steps - 1, jnp.clip(s - 2 * steps, 0, end))
        return jnp.where(late, 1, 0), number, 0

    both = lambda n: pl.BlockSpec((1, 1, block, n), lambda s: (*place(s), 0))
    own = pl.BlockSpec((1, block, wide), lambda s: (*own_at(s), 0))
    far0 = pl.BlockSpec((block, wide), lambda s: (jnp.minimum(s, end), 0))
    cols_own = pl.BlockSpec((1, head_rows, block), lambda s: (own_at(s)[0], 0, own_at(s)[1]))
    cols_far = pl.BlockSpec((1, head_rows, block), lambda s: (far_at(s)[0], 0, far_at(s)[1]))
    fin = pl.BlockSpec((1, block, wide), finished)
    halves = jax.ShapeDtypeStruct((tokens, wide), BF16)
    stack = lambda dtype: pltpu.VMEM((micros, steps, block, wide), dtype)
    return pl.pallas_call(
        partial(middle_kernel, block=block, chunk=min(chunk, hidden), out_part=out_part),
        grid=(4 * steps + 1,),
        in_specs=[
            both(width), both(width), own, own, far0, far0, cols_own, cols_far, ANYWHERE, whole(wo.shape),
            whole(bias.shape), whole(vectors.shape), whole(out_bias.shape), ANYWHERE, fin,
        ],
        out_specs=[
            fin, cols_own, cols_far, both(width), whole(pieces.shape), whole((8, width)), whole(bias.shape),
            ANYWHERE, ANYWHERE,
        ],
        out_shape=[
            jax.ShapeDtypeStruct((micros, tokens, wide), BF16),
            jax.ShapeDtypeStruct((micros, head_rows, tokens), BF16),
            jax.ShapeDtypeStruct((micros, head_rows, tokens), BF16),
            jax.ShapeDtypeStruct((micros, 2, tokens, width), BF16),
            jax.ShapeDtypeStruct(pieces.shape, BF16),
            jax.ShapeDtypeStruct((8, width), F32),
            jax.ShapeDtypeStruct(bias.shape, F32),
            halves, halves,
        ],
        scratch_shapes=[
            pltpu.VMEM((hidden, width), BF16),
            pltpu.VMEM((hidden, width), BF16),
            pltpu.VMEM((hidden, width), F32),
            pltpu.VMEM((hidden, width), F32),
            pltpu.VMEM((head_rows, width), F32),
            pltpu.VMEM((tokens, wide), BF16),
            pltpu.VMEM((tokens, wide), BF16),
            pltpu.VMEM((block, width), BF16),
            pltpu.VMEM((head_rows, block), BF16),
            pltpu.VMEM((block, hidden), BF16),
            pltpu.VMEM((block, hidden), BF16),
            pltpu.VMEM((block, wide), F32), stack(BF16), stack(BF16), stack(BF16), stack(BF16), stack(BF16),
            stack(BF16), stack(BF16),
            Gather.sems(2 * count), Gather.sems(2),
            pltpu.SemaphoreType.DMA, pltpu.SemaphoreType.DMA, pltpu.SemaphoreType.DMA, pltpu.SemaphoreType.DMA,
            *[Gather.sems(micros * steps) for _ in range(6)],
        ],
        compiler_params=params(collective_id=2, has_side_effects=True),
        cost_estimate=cost(2 * micros * tokens * 2 * width * (6 * hidden + 3 * head_rows), 80 << 20),
        name="middle",
    )(
        second, normed, cotangent, cc, cb0, cd0, att_own, att_far, pieces, wo, bias, vectors, out_bias, cotangent,
        residual,
    )


class Scatter:
    def __init__(self, spot, tiles, own, rx, rz, x_sems, z_sems):
        self.spot, self.own, self.rx, self.rz = spot, own, rx, rz
        self.order = [*range(1, spot.depth), 0]
        self.cross, self.along = {}, {}
        for s in self.order:
            away = spot.along(s) + 1 - 2 * spot.x
            self.cross[s] = remote(spot, "x", tiles(away), rx(s), x_sems[0](s), x_sems[1](s))
            if s:
                self.along[s] = pltpu.make_async_remote_copy(
                    src_ref=rx(s), dst_ref=rz(s - 1), send_sem=z_sems[0](s), recv_sem=z_sems[1](s),
                    device_id={"dp": spot.along(s)}, device_id_type=MESH,
                )

    def begin(self):
        for s in self.order:
            self.cross[s].start()

    def fold(self, s):
        self.cross[s].wait_recv()
        rx = self.rx(s)
        if s:
            rx[...] = (self.own(s)[...].astype(F32) + rx[...].astype(F32)).astype(BF16)
            self.along[s].start()

    def total(self):
        added = self.own(0)[...].astype(F32) + self.rx(0)[...].astype(F32)
        for s in self.order[:-1]:
            self.along[s].wait_recv()
            added = added + self.rz(s - 1)[...].astype(F32)
        return added

    def close(self):
        for s in self.order:
            self.cross[s].wait_send()
            if s:
                self.along[s].wait_send()


def back_kernel(
    triple, h_own, h_far, att_own, att_far, logsum, cosine, sine, part, weight, vectors, early, normed, tiles,
    x_fin, xc_fin, g_fin,
    grad_out, rest_out, dq_out, vec_out,
    g_s, delta_s, dq_s, dk_s, dv_s, t_s, norm_in, total, bias_s, gain_s, shift_s,
    near_f, near_o, other_f, other_o, cross_f, cross_o, moved, sum_s, sum_r, ng_s, norm_s, inv_s,
    a_own, a_rx, a_rz, a_total, b_tiles, b_rx, b_rz, b_total, held, arrived,
    n_load, a_load, a_xs, a_xr, a_zs, a_zr, b_xs, b_xr, b_zs, b_zr, k_send, k_recv, k_loc,
    v_send, v_recv, cf_send, cf_recv, co_send, co_recv, m_send, m_recv, s_send, s_recv,
    *, block, wider, step,
):
    spot = Spot()
    now = pl.program_id(0)
    tokens, wide = h_own.shape[2], x_fin.shape[2]
    width, length = 2 * wide, 2 * tokens
    heads = weight.shape[0] // (3 * HS)
    steps = tokens // block
    group = wider // block
    slow = tokens // wider
    count, depth = spot.count, spot.depth
    size = 3 * HS // count
    l0 = heads
    b1 = l0 + 2 * slow
    l1 = b1 + heads
    e0 = l1 + 2 * slow
    end = e0 + 2 * steps
    here, there = spot.row, 1 - spot.row
    at_step = lambda k: pl.when(now == k)

    sem = lambda ref, base=0: (lambda s: ref.at[base + s])
    first_sum = Scatter(
        spot, lambda p: tiles.at[p], lambda s: a_own.at[s], lambda s: a_rx.at[s], lambda s: a_rz.at[s],
        (sem(a_xs), sem(a_xr)), (sem(a_zs), sem(a_zr)),
    )

    def head_sum(h):
        return Scatter(
            spot, lambda p: b_tiles.at[p, h], lambda s: b_tiles.at[spot.along(s), h], lambda s: b_rx.at[h, s],
            lambda s: b_rz.at[h, s], (sem(b_xs, h * depth), sem(b_xr, h * depth)), (sem(b_zs, h * depth), sem(b_zr, h * depth)),
        )

    loads = [pltpu.make_async_copy(tiles.at[spot.along(s)], a_own.at[s], a_load.at[s]) for s in range(depth)]
    load_norm = [pltpu.make_async_copy(normed.at[m], norm_in, n_load.at[m]) for m in range(2)]

    def to_core(k, source, out):
        return (
            remote(spot, "col", source.at[:, pl.ds(wide, wide)], out.at[spot.col], k_send.at[k], k_recv.at[k]),
            pltpu.make_async_copy(source.at[:, pl.ds(0, wide)], out.at[spot.col], k_loc.at[k]),
        )

    a_core, b_core = to_core(0, a_total, rest_out), to_core(1, b_total, dq_out)

    partners = [{"col": 1 - spot.col}, {"row": 1 - spot.row}, {"dp": spot.z * 2 + (1 - spot.x)}]
    stride = 1
    while stride < depth:
        other_z = spot.z + stride * (1 - 2 * ((spot.z // stride) % 2))
        partners.append({"dp": other_z * 2 + spot.x})
        stride *= 2
    hops = [
        pltpu.make_async_remote_copy(
            src_ref=held.at[k], dst_ref=arrived.at[k], send_sem=v_send.at[k], recv_sem=v_recv.at[k],
            device_id=partner, device_id_type=MESH,
        )
        for k, partner in enumerate(partners)
    ]

    def over_core(which, m, i):
        k = m * steps + i
        if which == 0:
            return remote(spot, "col", other_f.at[i], cross_f.at[m, i], cf_send.at[k], cf_recv.at[k])
        return remote(spot, "col", other_o.at[i], cross_o.at[m, i], co_send.at[k], co_recv.at[k])

    def over_row(m, i):
        k = m * steps + i
        return remote(spot, "row", cross_f.at[m, i], moved.at[m, i], m_send.at[k], m_recv.at[k])

    def sums_over(m, i):
        k = m * steps + i
        return remote(spot, "col", sum_s.at[m, i], sum_r.at[m, i], s_send.at[k], s_recv.at[k])

    @at_step(0)
    def _():
        barrier = pltpu.get_barrier_semaphore()
        near = [{"col": 1 - spot.col}, {"row": 1 - spot.row}, {"dp": spot.z * 2 + (1 - spot.x)}]
        for device in near + [{"dp": spot.along(s)} for s in range(1, depth)]:
            pl.semaphore_signal(barrier, inc=1, device_id=device, device_id_type=MESH)
        load_norm[0].start()
        for load in loads:
            load.start()
        bias_s[...] = jnp.zeros_like(bias_s)
        gain_s[...] = jnp.zeros_like(gain_s)
        shift_s[...] = jnp.zeros_like(shift_s)
        pl.semaphore_wait(barrier, depth + 2)
        first_sum.begin()
        load_norm[0].wait()

    @at_step(1)
    def _():
        for load in loads:
            load.wait()

    @at_step(l0)
    def _():
        load_norm[1].start()

    @at_step(b1)
    def _():
        load_norm[1].wait()
        for i in range(steps):
            over_core(0, 0, i).wait_send()
            over_core(1, 0, i).wait_send()

    @pl.when((now < l0) | ((now >= b1) & (now < l1)))
    def _():
        head = jnp.where(now < l0, now, now - b1)
        for grad, att, place in ((h_own, att_own, here), (h_far, att_far, there)):
            at = lanes(place, tokens)
            g_s[:, at] = grad[0]
            delta_s[:, at] = jnp.sum(grad[0].astype(F32) * att[0].astype(F32), axis=0, keepdims=True)
        q_s, k_s, v_s = (triple.at[0, i * HS : (i + 1) * HS] for i in range(3))
        dk_s[...] = jnp.zeros_like(dk_s)
        dv_s[...] = jnp.zeros_like(dv_s)
        allowed = causal_tile(step)
        for i in range(length // step):
            lo, hi = i * step, (i + 1) * step
            query, grad = q_s[:, lo:hi], g_s[:, lo:hi]
            base, delta = logsum[0, 0, :, lo:hi], delta_s[:, lo:hi]
            query_grad = None
            cuts = [*range(0, lo, 512), lo, hi]
            for begin, stop in zip(cuts[:-1], cuts[1:]):
                if stop == begin:
                    continue
                raised = jnp.exp(mm(k_s[:, begin:stop], query, TN) - base)
                if begin == lo:
                    raised = jnp.where(allowed, raised, 0.0)
                prob_grad = mm(v_s[:, begin:stop], grad, TN)
                raised = raised.astype(BF16)
                score_grad = raised * (prob_grad - delta).astype(BF16)
                dv_s[:, begin:stop] += mm(grad, raised, NT)
                dk_s[:, begin:stop] += mm(query, score_grad, NT)
                term = mm(k_s[:, begin:stop], score_grad, NN)
                query_grad = term if query_grad is None else query_grad + term
            dq_s[:, lo:hi] = query_grad * HS ** (-0.5)
        cos, sin = cosine[...], sine[...]
        pieces = []
        for ref in (dq_s, dk_s):
            g1, g2 = ref[0:HALF, :], ref[HALF:ROT, :]
            pieces += [g1 * cos + g2 * sin, g2 * cos - g1 * sin, ref[ROT:HS, :]]
        pieces.append(dv_s[...])
        rounded = jnp.concatenate(pieces, axis=0).astype(BF16)
        at = pl.ds(pl.multiple_of(head * 3 * HS, HS), 3 * HS)
        t_s[at, :] = rounded
        bias_s[at, :] += jnp.sum(rounded.astype(F32), axis=1, keepdims=True)
        term = mm(t_s[at, lanes(there, tokens)], norm_in[0], NN) + mm(t_s[at, lanes(here, tokens)], norm_in[1], NN)

        @pl.when(now < l0)
        def _():
            total[head] = term

        @pl.when(now >= b1)
        def _():
            gain, shift = vectors[0:1, :], vectors[1:2, :]
            every = total[head] + term
            weights = weight[at, :].astype(F32)
            summed = bias_s[at, :]
            gain_s[...] += jnp.sum(weights * every, axis=0, keepdims=True)
            shift_s[...] += jnp.sum(weights * summed, axis=0, keepdims=True)
            every = every * gain + summed * shift
            for p in range(count):
                b_tiles[p, head] = every[p * size : (p + 1) * size].astype(BF16)
            head_sum(head).begin()

    moments = {1: 2, 2: l0, 3: b1, 0: b1 + 2} if depth == 4 else {}
    for s in first_sum.order:
        @at_step(moments.get(s, b1 + 2))
        def _():
            first_sum.fold(s)

    @pl.when((now > b1) & (now < l1))
    def _():
        before = head_sum(now - 1 - b1)
        for s in before.order:
            before.fold(s)

    @at_step(l1 + 1)
    def _():
        used = early.shape[0]
        lanes_here = held.shape[2]
        part_rows = width // (2 * lanes_here)
        held[0] = jnp.zeros_like(held[0])
        held[0, 0:used, :] = early[...]
        at = used
        for vector in (gain_s, shift_s):
            for r in range(2 * part_rows):
                mirror = (r + part_rows) % (2 * part_rows)
                plain = vector[:, r * lanes_here : (r + 1) * lanes_here]
                turned = vector[:, mirror * lanes_here : (mirror + 1) * lanes_here]
                held[0, at : at + 1, :] = jnp.where(spot.col == 0, plain, turned)
                at += 1
        line = jnp.transpose(jnp.broadcast_to(bias_s[...], (bias_s.shape[0], 128)))[0:1, :]
        mine = spot.row * 2 + spot.col
        for h in range(4 * heads):
            k = h % heads
            values = line[:, k * 3 * HS : (k + 1) * 3 * HS]
            held[0, at : at + 1, 0 : 3 * HS] = jnp.where(mine == h // heads, values, 0.0)
            at += 1

    later = now >= b1
    lead = jnp.where(later, now - l1, now - l0)

    @pl.when((lead >= 0) & (lead < 2 * slow))
    def _():
        m, half, at = jnp.where(later, 1, 0), lead // slow, lead % slow
        place = jnp.where(half == 0, there, here)
        blocks = [(j, at * group + j, slice(j * block, (j + 1) * block)) for j in range(group)]
        turned = lambda i: t_s[:, pl.ds(pl.multiple_of(place * tokens + i * block, block), block)]
        for j, i, rows in blocks:
            other = (mm(turned(i), weight[:, wide:], TN) * vectors[0:1, wide:] + part[0, 0, rows, wide:].astype(F32)).astype(BF16)

            @pl.when(half == 0)
            def _():
                other_f[i] = other
                over_core(0, m, i).start()

            @pl.when(half == 1)
            def _():
                other_o[i] = other
                over_core(1, m, i).start()

        for j, i, rows in blocks:
            near = mm(turned(i), weight[:, :wide], TN) * vectors[0:1, :wide] + part[0, 0, rows, :wide].astype(F32)

            @pl.when(half == 0)
            def _():
                near_f[j] = near

            @pl.when(half == 1)
            def _():
                near_o[m, i] = near.astype(BF16)

        @pl.when(half == 0)
        def _():
            for j, i, rows in blocks:
                over_core(0, m, i).wait_recv()
                cross_f[m, i] = (near_f[j] + cross_f[m, i].astype(F32)).astype(BF16)
                over_row(m, i).start()

    @at_step(l1 + 2)
    def _():
        before = head_sum(heads - 1)
        for s in before.order:
            before.fold(s)

    for k in range(len(hops) + 1):
        @at_step(l1 + 1 + k)
        def _():
            if k:
                hops[k - 1].wait_recv()
            if 0 < k < len(hops):
                held[k] = held[k - 1] + arrived[k - 1]
            if k < len(hops):
                hops[k].start()
            else:
                vec_out[...] = held[k - 1] + arrived[k - 1]

    @at_step(e0)
    def _():
        a_total[...] = first_sum.total()
        for copy in a_core:
            copy.start()

    @at_step(e0 + steps)
    def _():
        first_sum.close()
        for h in range(heads):
            head_sum(h).close()
        for i in range(steps):
            over_core(0, 1, i).wait_send()
            over_core(1, 1, i).wait_send()
            over_row(0, i).wait_send()

    trail = now - e0

    @at_step(e0 + steps - 1)
    def _():
        for h in range(heads):
            b_total[h * size : (h + 1) * size, :] = head_sum(h).total()
        for copy in b_core:
            copy.start()

    @pl.when((trail >= 0) & (trail < 2 * steps))
    def _():
        m, i, slot = trail // steps, trail % steps, trail % 2
        over_row(m, i).wait_recv()
        over_core(1, m, i).wait_recv()
        grad = near_o[m, i].astype(F32) + cross_o[m, i].astype(F32) + moved[m, i].astype(F32)
        near_x, far_x = x_fin[0].astype(F32), xc_fin[0].astype(F32)
        center = jnp.sum(near_x + far_x, axis=1, keepdims=True) / width
        spread = jnp.sum(near_x * near_x + far_x * far_x, axis=1, keepdims=True) / width - center * center
        inv = lax.rsqrt(spread + EPSILON)
        normed_x = (near_x - center) * inv
        ng_s[slot] = grad
        norm_s[slot] = normed_x
        inv_s[slot] = inv
        column = lax.broadcasted_iota(jnp.int32, (block, 128), 1)
        one = jnp.sum(grad, axis=1, keepdims=True)
        two = jnp.sum(grad * normed_x, axis=1, keepdims=True)
        sum_s[m, i] = jnp.where(column == 0, one, jnp.where(column == 1, two, 0.0))
        sums_over(m, i).start()

    @pl.when(trail > 0)
    def _():
        m, i, slot = (trail - 1) // steps, (trail - 1) % steps, (trail - 1) % 2
        sums_over(m, i).wait_recv()
        sums = (sum_s[m, i] + sum_r[m, i]) / width
        grad_out[0] = g_fin[0].astype(F32) + inv_s[slot] * (ng_s[slot] - sums[:, 0:1] - norm_s[slot] * sums[:, 1:2])

    @at_step(end)
    def _():
        for copy in (*a_core, *b_core):
            copy.wait()
        for k in hops:
            k.wait_send()
        for i in range(steps):
            over_row(1, i).wait_send()
            for m in range(2):
                sums_over(m, i).wait_send()


def backward(
    triple, h_own, h_far, att_own, att_far, logsum, cosine, sine, normed, part, weight, vectors, tiles, early,
    residual, xc, cotangent, block=512, wider=512, step=512,
):
    micros, rows, length = triple.shape
    tokens, wide = length // 2, residual.shape[2]
    width = 2 * wide
    heads = rows // (3 * HS)
    block, wider, step = min(block, tokens), min(wider, tokens), min(step, length)
    steps, slow = tokens // block, tokens // wider
    count, piece = tiles.shape[:2]
    depth = count // 2
    small = rows // count
    l0 = heads
    b1 = l0 + 2 * slow
    l1 = b1 + heads
    e0 = l1 + 2 * slow

    def head_of(s):
        late = s >= b1
        return jnp.where(late, 1, 0), jnp.minimum(jnp.where(late, s - b1, s), heads - 1)

    def part_at(s):
        late = s >= b1
        number = jnp.clip(jnp.where(late, s - l1, s - l0), 0, 2 * slow - 1)
        return jnp.where(late, 1, 0), number // slow, number % slow, 0

    def in_at(s):
        number = jnp.clip(s - e0, 0, 2 * steps - 1)
        return number // steps, number % steps, 0

    def out_at(s):
        number = jnp.clip(s - e0 - 1, 0, 2 * steps - 1)
        return number // steps, number % steps, 0

    narrow = pl.BlockSpec((1, HS, tokens), lambda s: (*head_of(s), 0))
    fin_in = pl.BlockSpec((1, block, wide), in_at)
    fin_out = pl.BlockSpec((1, block, wide), out_at)
    hops = 3 + max(depth - 1, 0).bit_length()
    vec_rows = early.shape[0] + 2 * (width // early.shape[1]) + 4 * heads
    pair = lambda dtype: pltpu.VMEM((micros, steps, block, wide), dtype)
    single = lambda dtype: pltpu.VMEM((steps, block, wide), dtype)
    sems = Gather.sems
    return pl.pallas_call(
        partial(back_kernel, block=block, wider=wider, step=step),
        grid=(e0 + 2 * steps + 1,),
        in_specs=[
            pl.BlockSpec((1, 3 * HS, length), lambda s: (*head_of(s), 0)), narrow, narrow, narrow, narrow,
            pl.BlockSpec((1, 1, 1, length), lambda s: (*head_of(s), 0, 0)), whole(cosine.shape), whole(sine.shape),
            pl.BlockSpec((1, 1, wider, width), part_at),
            whole(weight.shape), whole(vectors.shape), whole(early.shape), ANYWHERE, ANYWHERE, fin_in, fin_in, fin_out,
        ],
        out_specs=[fin_out, ANYWHERE, ANYWHERE, whole((vec_rows, early.shape[1]))],
        out_shape=[
            jax.ShapeDtypeStruct((micros, tokens, wide), F32),
            jax.ShapeDtypeStruct((2, piece, wide), F32),
            jax.ShapeDtypeStruct((2, small, wide), F32),
            jax.ShapeDtypeStruct((vec_rows, early.shape[1]), F32),
        ],
        scratch_shapes=[
            pltpu.VMEM((HS, length), BF16),
            pltpu.VMEM((1, length), F32),
            pltpu.VMEM((HS, length), F32),
            pltpu.VMEM((HS, length), F32),
            pltpu.VMEM((HS, length), F32),
            pltpu.VMEM((rows, length), BF16),
            pltpu.VMEM((2, tokens, width), BF16),
            pltpu.VMEM((heads, 3 * HS, width), F32),
            pltpu.VMEM((rows, 1), F32),
            pltpu.VMEM((1, width), F32), pltpu.VMEM((1, width), F32),
            pltpu.VMEM((wider // block, block, wide), F32), pair(BF16), single(BF16), single(BF16), pair(BF16), pair(BF16),
            pair(BF16),
            pltpu.VMEM((micros, steps, block, 128), F32), pltpu.VMEM((micros, steps, block, 128), F32),
            pltpu.VMEM((2, block, wide), F32), pltpu.VMEM((2, block, wide), F32), pltpu.VMEM((2, block, 1), F32),
            pltpu.VMEM((depth, piece, width), BF16), pltpu.VMEM((depth, piece, width), BF16),
            pltpu.VMEM((depth - 1, piece, width), BF16), pltpu.VMEM((piece, width), F32),
            pltpu.VMEM((count, heads, small // heads, width), BF16),
            pltpu.VMEM((heads, depth, small // heads, width), BF16),
            pltpu.VMEM((heads, depth - 1, small // heads, width), BF16),
            pltpu.VMEM((small, width), F32),
            pltpu.VMEM((hops, vec_rows, early.shape[1]), F32), pltpu.VMEM((hops, vec_rows, early.shape[1]), F32),
            sems(2), sems(depth), sems(depth), sems(depth), sems(depth), sems(depth),
            *[sems(depth * heads) for _ in range(4)], sems(2), sems(2), sems(2),
            sems(hops), sems(hops), *[sems(micros * steps) for _ in range(8)],
        ],
        compiler_params=params(collective_id=3, has_side_effects=True),
        cost_estimate=cost(micros * (heads * length * length * 256 * 5 + length * width * 4 * rows), 100 << 20),
        name="backward",
    )(
        triple, h_own, h_far, att_own, att_far, logsum, cosine, sine, part, weight, vectors, early, normed, tiles,
        residual, xc, cotangent,
    )


def pick(value, index, axis=0):
    return lax.dynamic_index_in_dim(value, index, axis, keepdims=False)


def body(
    residual, attend_norm_gain, attend_norm_bias, expand_norm_gain, expand_norm_bias,
    attend_weight, attend_bias, output_weight, output_bias, expand_weight, expand_bias,
    shrink_weight, shrink_bias, cotangent,
):
    count = lax.axis_size("dp")
    row, col = lax.axis_index("row"), lax.axis_index("col")
    micros, tokens, wide = residual.shape
    width, length = 2 * wide, 2 * tokens
    heads = attend_weight.shape[1] // 2
    head_part, out_part = attend_weight.shape[2], output_weight.shape[1]
    hid = expand_weight.shape[1] // 2

    def sides(rows):
        return pick(rows, col), pick(rows, 1 - col)

    head_mine, head_theirs = sides(attend_weight.transpose(1, 2, 0).reshape(2, heads * head_part, wide))
    rest_mine, rest_theirs = sides(
        jnp.concatenate(
            [
                output_weight.reshape(2, heads * out_part, wide),
                expand_weight.T.reshape(2, hid, wide),
                shrink_weight.reshape(2, hid, wide),
            ],
            axis=1,
        )
    )

    vectors = jnp.stack([attend_norm_gain, attend_norm_bias, expand_norm_gain, expand_norm_bias])
    vectors = jnp.concatenate([jnp.roll(vectors, -col * wide, axis=1), jnp.zeros((4, width), F32)])
    head_begin = row * 2 * heads + col * heads
    bias_q = lax.dynamic_slice_in_dim(attend_bias, head_begin, heads, 0).reshape(-1, 1)
    bias_1 = pick(expand_bias.reshape(count, 4, hid), row * 2 + col, 1).reshape(1, -1)
    out_bias = lax.dynamic_slice_in_dim(output_bias + shrink_bias, col * wide, wide, 0).reshape(1, -1)
    powers = 10000.0 ** (-np.arange(HALF) * (2.0 / ROT))
    angles = powers[:, None] * np.arange(length)[None, :]
    cosine, sine = jnp.asarray(np.cos(angles), F32), jnp.asarray(np.sin(angles), F32)

    normed, second, triple, wq, att_own, att_far, logsum, pieces, xc, cb0, cc, cd0 = forward(
        residual, bias_q, vectors, cosine, sine, head_mine, head_theirs, rest_mine, rest_theirs, cotangent, count
    )
    lo = heads * out_part
    wo = pieces[:, :lo].reshape(count, heads, out_part, width).transpose(1, 0, 2, 3).reshape(heads * HS, width)
    outputs, h_own, h_far, part, tiles, dvec, db1, _, _ = middle(
        second, normed, residual, cotangent, cc, cb0, cd0, att_own, att_far, pieces, wo, bias_1, vectors, out_bias
    )

    dout = jnp.sum(cotangent.astype(F32), axis=(0, 1))
    dout = lax.dynamic_update_slice_in_dim(jnp.zeros((width,), F32), dout, col * wide, 0)
    dvec = jnp.roll(dvec[:2], col * wide, axis=1)
    db1 = lax.dynamic_update_slice_in_dim(
        jnp.zeros((count, 4, hid), F32), db1.reshape(count, 1, hid), row * 2 + col, 1
    )
    lane = 256
    early = jnp.concatenate([db1.reshape(-1, lane), dout.reshape(-1, lane), dvec.reshape(-1, lane)])
    early = jnp.pad(early, ((0, -early.shape[0] % 8), (0, 0)))

    grads, rest_sum, dq_sum, vec = backward(
        triple, h_own, h_far, att_own, att_far, logsum, cosine, sine, normed, part, wq, vectors, tiles, early,
        residual, xc, cotangent,
    )
    attend_weight_grad = dq_sum.reshape(2 * heads, head_part, wide).transpose(2, 0, 1)
    output_weight_grad = rest_sum[:, :lo].reshape(2 * heads, out_part, wide)
    expand_weight_grad = rest_sum[:, lo : lo + hid].reshape(2 * hid, wide).T
    shrink_weight_grad = rest_sum[:, lo + hid :].reshape(2 * hid, wide)

    n1, nw, ne = db1.size // lane, width // lane, early.shape[0]
    cut = lambda at, rows: vec[at : at + rows].reshape(-1)
    dout = cut(n1, nw)
    return (
        outputs, grads, cut(ne, nw), cut(ne + nw, nw), cut(n1 + nw, nw), cut(n1 + 2 * nw, nw),
        attend_weight_grad, vec[ne + 2 * nw :, : 3 * HS], output_weight_grad, dout, expand_weight_grad, cut(0, n1),
        shrink_weight_grad, dout,
    )


def solution(mesh):
    tokens = P(None, ("dp", "row"), "col")
    weights = (P("col", "row", "dp"), P("row", "dp", "col"), P("col", ("dp", "row")), P(("dp", "row"), "col"))
    one = P()
    in_specs = (tokens, one, one, one, one, weights[0], one, weights[1], one, weights[2], one, weights[3], one, tokens)
    out_specs = (tokens, tokens, one, one, one, one, weights[0], one, weights[1], one, weights[2], one, weights[3], one)
    return jax.shard_map(body, mesh=mesh, in_specs=in_specs, out_specs=out_specs, check_vma=False)
```

```python
from functools import partial

import jax
import jax.numpy as jnp
import numpy as np
from jax import lax
from jax.experimental import pallas as pl
from jax.experimental.pallas import tpu as pltpu
from jax.sharding import PartitionSpec as P

D = 1024
HS = 64
ROT = 16
HALF = ROT // 2
EPSILON = 1e-05
MASKED = -1e30
NN = (((1,), (0,)), ((), ()))
NT = (((1,), (1,)), ((), ()))
TN = (((0,), (0,)), ((), ()))
VMEM_LIMIT = 60 << 20
F32 = jnp.float32
BF16 = jnp.bfloat16


def mm(a, b, dims):
    return lax.dot_general(a, b, dims, preferred_element_type=F32)


def params(**extra):
    return pltpu.CompilerParams(vmem_limit_bytes=VMEM_LIMIT, **extra)


def cost(flops, nbytes):
    return pl.CostEstimate(flops=int(flops), bytes_accessed=int(nbytes), transcendentals=0)


def whole(shape):
    return pl.BlockSpec(shape, lambda *_: (0,) * len(shape))


MESH = pl.DeviceIdType.MESH
ANYWHERE = pl.BlockSpec(memory_space=pl.ANY)


class Spot:
    def __init__(self):
        self.count = lax.axis_size("dp")
        self.depth = self.count // 2
        self.dp, self.row, self.col = (lax.axis_index(a) for a in ("dp", "row", "col"))
        self.z, self.x = self.dp // 2, self.dp % 2

    def along(self, steps):
        return ((self.z + steps) % self.depth) * 2 + self.x

    def device(self, which):
        return {
            "row": {"row": 1 - self.row},
            "col": {"col": 1 - self.col},
            "x": {"dp": self.z * 2 + (1 - self.x)},
            "right": {"dp": self.along(1)},
            "left": {"dp": self.along(self.depth - 1)},
        }[which]

    def greet(self, *names):
        barrier = pltpu.get_barrier_semaphore()
        for name in names:
            pl.semaphore_signal(barrier, inc=1, device_id=self.device(name), device_id_type=MESH)
        pl.semaphore_wait(barrier, len(names))


def remote(spot, which, source, target, send, recv):
    return pltpu.make_async_remote_copy(
        src_ref=source, dst_ref=target, send_sem=send, recv_sem=recv,
        device_id=spot.device(which), device_id_type=MESH,
    )


class Gather:
    def __init__(self, spot, mine, theirs, all_ref, local, send, recv):
        self.spot, self.all = spot, all_ref
        wide = mine.shape[1]
        here = all_ref.at[spot.dp]
        depth = spot.depth
        self.local = pltpu.make_async_copy(mine, here.at[:, pl.ds(0, wide)], local)
        self.core = remote(spot, "col", theirs, here.at[:, pl.ds(wide, wide)], send.at[0], recv.at[0])
        self.ring, self.cross = [], []
        for k in range(depth):
            slot = all_ref.at[spot.along(depth - k)]
            self.cross.append(remote(spot, "x", slot, slot, send.at[1 + k], recv.at[1 + k]))
            if k < depth - 1:
                at = 1 + depth + k
                self.ring.append(remote(spot, "right", slot, slot, send.at[at], recv.at[at]))

    @staticmethod
    def sems(count):
        return pltpu.SemaphoreType.DMA((count,))

    @staticmethod
    def parts(spot, mine, theirs, all_ref, local, send, recv):
        rows = mine.shape[0]
        cuts = 2 if rows % 32 == 0 else 1
        size, slots = rows // cuts, send.shape[0] // 2
        found = []
        for c in range(cuts):
            part, sems = pl.ds(c * size, size), pl.ds(c * slots, slots)
            found.append(
                Gather(
                    spot, mine.at[part], theirs.at[part], all_ref.at[:, part], local.at[c], send.at[sems], recv.at[sems]
                )
            )
        return found

    def begin(self):
        self.local.start()
        self.core.start()

    def first(self):
        self.local.wait()
        self.core.wait_recv()
        self.ring[0].start()
        self.cross[0].start()

    def forward(self, k):
        self.ring[k - 1].wait_recv()
        if k < len(self.ring):
            self.ring[k].start()
        self.cross[k].start()

    def arrive(self):
        for copy in self.cross:
            copy.wait_recv()

    def close(self):
        for copy in (self.core, *self.ring, *self.cross):
            copy.wait_send()


def lanes(index, tokens):
    return pl.ds(pl.multiple_of(index * tokens, tokens), tokens)


def forward_kernel(
    xa, bias, vectors, cosine, sine, head_mine, head_theirs, mine, theirs, tokens, grads,
    plain, second, triple, weight_out, att_own, att_far, logsum, all_ref, xc, cb0, cc, cd0,
    x_s, first, q_s, v_s, o_s, xc_s, near_s, far_s, pieces, weight,
    a_local, a_send, a_recv, local, send, recv, y_send, y_recv, c_send, c_recv, t_sem, *, block, step, chunks, rows_at_once,
):
    spot = Spot()
    now = pl.program_id(0)
    wide = xa.shape[2]
    width = 2 * wide
    own_tokens = tokens.shape[1]
    length = 2 * own_tokens
    blocks = own_tokens // block
    heads = weight.shape[0] // (3 * HS)
    depth, count = spot.depth, spot.count
    cast0 = 2 * blocks
    far0 = 2 * cast0
    attend0 = far0 + blocks
    far1 = attend0 + heads
    attend1 = far1 + blocks
    end = attend1 + heads - 1
    here, there = spot.row, 1 - spot.row
    at = lambda k: pl.when(now == k)

    head_parts = Gather.parts(spot, head_mine, head_theirs, pieces, a_local, a_send, a_recv)
    rest_parts = Gather.parts(spot, mine, theirs, all_ref, local, send, recv)
    size = own_tokens // chunks
    part = lambda k: pl.ds(k * size, size)
    x_row = [
        [remote(spot, "row", tokens.at[m, part(k)], near_s.at[m, part(k)], y_send.at[m * chunks + k], y_recv.at[m * chunks + k]) for k in range(chunks)]
        for m in range(2)
    ]
    x_col = [
        [remote(spot, "col", near_s.at[m, part(k)], far_s.at[m, part(k)], c_send.at[m * chunks + k], c_recv.at[m * chunks + k]) for k in range(chunks)]
        for m in range(2)
    ]
    x_core = [remote(spot, "col", tokens.at[m], xc_s.at[m], c_send.at[2 * chunks + m], c_recv.at[2 * chunks + m]) for m in range(2)]
    g_row = remote(spot, "row", grads.at[0], cb0, y_send.at[2 * chunks], y_recv.at[2 * chunks])
    g_col = remote(spot, "col", cb0, cd0, c_send.at[2 * chunks + 2], c_recv.at[2 * chunks + 2])
    g_core = remote(spot, "col", grads, cc, c_send.at[2 * chunks + 3], c_recv.at[2 * chunks + 3])
    keep = [pltpu.make_async_copy(q_s.at[m], triple.at[m], t_sem.at[m]) for m in range(2)]
    keep_weight = pltpu.make_async_copy(weight, weight_out, t_sem.at[2])
    keep_core = pltpu.make_async_copy(xc_s, xc, t_sem.at[3])

    @at(0)
    def _():
        spot.greet("row", "col", "x", "right", "left")
        for gather in head_parts:
            gather.begin()
        for copy in x_row[0]:
            copy.start()
        x_core[0].start()
        for gather in rest_parts:
            gather.begin()
        for gather in head_parts:
            gather.first()
        x_core[1].start()
        x_core[0].wait_recv()

    @at(1)
    def _():
        head_parts[0].forward(1)

    @at(blocks)
    def _():
        for gather in head_parts[1:]:
            gather.forward(1)
        x_core[1].wait_recv()
        keep_core.start()

    @at(cast0)
    def _():
        for k in range(2, depth):
            for gather in head_parts:
                gather.forward(k)
        for gather in rest_parts:
            gather.first()
        for gather in head_parts:
            gather.arrive()
        for copy in x_row[1]:
            copy.start()
        size = weight.shape[0] // (heads * count)
        for h in range(heads):
            small = [pieces[p, h * size : (h + 1) * size, :].astype(F32) for p in range(count)]
            weight[h * 3 * HS : (h + 1) * 3 * HS, :] = jnp.concatenate(small, axis=0).astype(BF16)
        keep_weight.start()

    @at(cast0 + 1)
    def _():
        for k in range(chunks):
            x_row[0][k].wait_recv()
            x_col[0][k].start()

    @at(far0)
    def _():
        for k in range(chunks):
            x_col[0][k].wait_recv()
        g_core.start()

    moments = {(1, 0): cast0 + 3, (1, 1): far0, (2, 0): attend0 + 1, (2, 1): attend0 + 2, (3, 0): far1, (3, 1): attend1}
    for k in range(1, depth):
        for c, gather in enumerate(rest_parts):
            @at(moments.get((k, c), attend1) if depth == 4 else attend1)
            def _():
                gather.forward(k)

    @at(far1 - 2)
    def _():
        for k in range(chunks):
            x_row[1][k].wait_recv()
            x_col[1][k].start()
        g_row.start()

    @at(far1)
    def _():
        for k in range(chunks):
            x_col[1][k].wait_recv()

    norming = (now < cast0) | ((now >= far0) & (now < attend0)) | ((now >= far1) & (now < attend1))

    @pl.when(now < cast0)
    def _():
        lo = pl.multiple_of((now % blocks) * block, block)
        x_s[:, :wide] = xa[0]
        x_s[:, wide:] = xc_s[now // blocks, pl.ds(lo, block), :]

    for begin, m in ((far0, 0), (far1, 1)):
        @pl.when((now >= begin) & (now < begin + blocks))
        def _():
            lo = pl.multiple_of((now - begin) * block, block)
            x_s[:, :wide] = near_s[m, pl.ds(lo, block), :]
            x_s[:, wide:] = far_s[m, pl.ds(lo, block), :]

    slot = jnp.where(now < far0, now % cast0, (now - far0) % blocks)
    slot = jnp.where(now >= far1, now - far1, slot)

    @pl.when(norming)
    def _():
        for lo in range(0, block, rows_at_once):
            rows = slice(lo, lo + rows_at_once)
            values = x_s[rows, :].astype(F32)
            center = jnp.sum(values, axis=1, keepdims=True) / width
            spread = jnp.sum(values * values, axis=1, keepdims=True) / width - center * center
            normed = (values - center) * lax.rsqrt(spread + EPSILON)
            plain[0, 0, rows, :] = normed.astype(BF16)
            first[slot, rows, :] = (normed * vectors[0:1, :] + vectors[1:2, :]).astype(BF16)
            second[0, 0, rows, :] = (normed * vectors[2:3, :] + vectors[3:4, :]).astype(BF16)

    casting = ((now >= cast0) & (now < attend0)) | ((now >= far1) & (now < attend1))

    @pl.when(casting)
    def _():
        number = now - cast0
        micro = jnp.where(now < far0, number // blocks, jnp.where(now < attend0, 0, 1))
        half = jnp.where(now < far0, here, there)
        block_at = jnp.where(now >= far1, now - far1, number % blocks)
        lane = pl.ds(pl.multiple_of(half * own_tokens + block_at * block, block), block)
        cos, sin = cosine[:, lane], sine[:, lane]
        every = mm(weight[...], first[slot], NT) + bias[...]
        for head in range(heads):
            base = head * 3 * HS
            rows = every[base : base + 3 * HS]
            parts = []
            for which in range(2):
                lo = which * HS
                scale = HS ** (-0.5) if which == 0 else 1.0
                u1, u2 = rows[lo : lo + HALF], rows[lo + HALF : lo + ROT]
                parts += [(u1 * cos - u2 * sin) * scale, (u2 * cos + u1 * sin) * scale, rows[lo + ROT : lo + HS] * scale]
            parts.append(rows[2 * HS :])
            q_s[micro, base : base + 3 * HS, lane] = jnp.concatenate(parts, axis=0).astype(BF16)

    @at(attend0)
    def _():
        keep[0].start()

    @at(attend1)
    def _():
        keep[1].start()

    attending = ((now >= attend0) & (now < far1)) | (now >= attend1)

    @pl.when(attending)
    def _():
        micro = jnp.where(now < far1, 0, 1)
        head = jnp.where(now < far1, now - attend0, now - attend1)
        base = pl.multiple_of(head * 3 * HS, HS)
        query_of = lambda lo, hi: q_s[micro, pl.ds(base, HS), lo:hi]
        keys_of = lambda lo, hi: q_s[micro, pl.ds(pl.multiple_of(base + HS, HS), HS), lo:hi]
        v_s[0:HS, :] = q_s[micro, pl.ds(pl.multiple_of(base + 2 * HS, HS), HS), :]
        extra = lax.broadcasted_iota(jnp.int32, (16, length), 0)
        v_s[HS : HS + 16, :] = jnp.where(extra == 0, 1.0, 0.0).astype(BF16)
        allowed = causal_tile(step)
        for i in range(length // step):
            lo, hi = i * step, (i + 1) * step
            query = query_of(lo, hi)
            diag = jnp.where(allowed, mm(keys_of(lo, hi), query, TN), MASKED)
            highest = jnp.max(diag, axis=0, keepdims=True)
            if i:
                past = mm(keys_of(0, lo), query, TN)
                highest = jnp.maximum(highest, jnp.max(past, axis=0, keepdims=True))
            raised = jnp.exp(diag - highest).astype(BF16)
            result = mm(v_s[:, lo:hi], raised, NN)
            if i:
                raised = jnp.exp(past - highest).astype(BF16)
                result = result + mm(v_s[:, :lo], raised, NN)
            total = result[HS : HS + 1]
            o_s[:, lo:hi] = (result[:HS] / total).astype(BF16)
            logsum[0, 0, :, lo:hi] = highest + jnp.log(total)
        att_own[0] = o_s[:, lanes(here, own_tokens)]
        att_far[0] = o_s[:, lanes(there, own_tokens)]

    @at(end)
    def _():
        g_row.wait_recv()
        g_col.start()
        for gather in rest_parts:
            gather.arrive()
        for gather in (*rest_parts, *head_parts):
            gather.close()
        g_col.wait()
        g_core.wait()
        for m in range(2):
            x_core[m].wait_send()
            for k in range(chunks):
                x_row[m][k].wait_send()
                x_col[m][k].wait_send()
        g_row.wait_send()
        keep[0].wait()
        keep[1].wait()
        keep_weight.wait()
        keep_core.wait()


def forward(residual, bias, vectors, cosine, sine, head_mine, head_theirs, mine, theirs, cotangent, count, block=512, step=512):
    micros, tokens, wide = residual.shape
    width, length = 2 * wide, 2 * tokens
    block, step = min(block, tokens), min(step, length)
    blocks = tokens // block
    rows = bias.shape[0]
    heads = rows // (3 * HS)
    depth = count // 2
    chunks = 2
    cast0 = 2 * blocks
    far0 = 2 * cast0
    a0 = far0 + blocks
    f1 = a0 + heads
    a1 = f1 + blocks
    steps = a1 + heads
    own = pl.BlockSpec((1, block, wide), lambda i: (jnp.minimum(i, cast0 - 1) // blocks, jnp.minimum(i, cast0 - 1) % blocks, 0))

    def place(i):
        early = jnp.minimum(i, cast0 - 1)
        late = i >= f1
        far = i >= far0
        micro = jnp.where(late, 1, jnp.where(far, 0, early // blocks))
        number = jnp.where(late, jnp.minimum(i - f1, blocks - 1), jnp.where(far, jnp.minimum(i - far0, blocks - 1), early % blocks))
        return micro, jnp.where(far, 0, 1), number, 0

    def head_of(i):
        late = i >= a1
        return jnp.where(late, 1, 0), jnp.where(late, i - a1, jnp.clip(i - a0, 0, heads - 1))

    normal = pl.BlockSpec((1, 1, block, width), place)
    att = pl.BlockSpec((1, HS, tokens), lambda i: (*head_of(i), 0))
    half = jax.ShapeDtypeStruct((tokens, wide), BF16)
    piece = mine.shape[0]
    sems = Gather.sems
    return pl.pallas_call(
        partial(forward_kernel, block=block, step=step, chunks=chunks, rows_at_once=min(64, block)),
        grid=(steps,),
        in_specs=[
            own, whole(bias.shape), whole(vectors.shape), whole(cosine.shape), whole(sine.shape), *[ANYWHERE] * 6,
        ],
        out_specs=[
            normal, normal, ANYWHERE, ANYWHERE, att, att,
            pl.BlockSpec((1, 1, 1, length), lambda i: (*head_of(i), 0, 0)), *[ANYWHERE] * 5,
        ],
        out_shape=[
            jax.ShapeDtypeStruct((micros, 2, tokens, width), BF16),
            jax.ShapeDtypeStruct((micros, 2, tokens, width), BF16),
            jax.ShapeDtypeStruct((micros, rows, length), BF16),
            jax.ShapeDtypeStruct((rows, width), BF16),
            jax.ShapeDtypeStruct((micros, heads * HS, tokens), BF16),
            jax.ShapeDtypeStruct((micros, heads * HS, tokens), BF16),
            jax.ShapeDtypeStruct((micros, heads, 1, length), F32),
            jax.ShapeDtypeStruct((count, piece, width), BF16),
            jax.ShapeDtypeStruct(residual.shape, BF16), half, jax.ShapeDtypeStruct(cotangent.shape, BF16), half,
        ],
        scratch_shapes=[
            pltpu.VMEM((block, width), BF16),
            pltpu.VMEM((cast0, block, width), BF16),
            pltpu.VMEM((micros, rows, length), BF16),
            pltpu.VMEM((HS + 16, length), BF16),
            pltpu.VMEM((HS, length), BF16),
            pltpu.VMEM((micros, tokens, wide), BF16),
            pltpu.VMEM((micros, tokens, wide), BF16),
            pltpu.VMEM((micros, tokens, wide), BF16),
            pltpu.VMEM((count, rows // count, width), BF16),
            pltpu.VMEM((rows, width), BF16),
            sems(2), sems(4 * depth), sems(4 * depth), sems(2), sems(4 * depth), sems(4 * depth),
            sems(2 * chunks + 1), sems(2 * chunks + 1), sems(2 * chunks + 4), sems(2 * chunks + 4), sems(4),
        ],
        compiler_params=params(collective_id=1, has_side_effects=True),
        cost_estimate=cost(micros * length * width * rows * 2 + micros * heads * length * length * 256 * 2, 40 << 20),
        name="forward",
    )(residual, bias, vectors, cosine, sine, head_mine, head_theirs, mine, theirs, residual, cotangent)
def causal_tile(size):
    keys = lax.broadcasted_iota(jnp.int32, (size, size), 0)
    places = lax.broadcasted_iota(jnp.int32, (size, size), 1)
    return keys <= places


def lanes(index, tokens):
    return pl.ds(pl.multiple_of(index * tokens, tokens), tokens)


POLY = (0.254829592, -0.284496736, 1.421413741, -1.453152027, 1.061405429)


def gelu_pair(value):
    magnitude = jnp.abs(value)
    t = 1.0 / (1.0 + magnitude * (0.3275911 * 0.5**0.5))
    bell = jnp.exp(value * value * -0.5)
    series = POLY[4]
    for term in (POLY[3], POLY[2], POLY[1], POLY[0]):
        series = series * t + term
    tail = 0.5 * series * t * bell
    cumulative = jnp.where(value >= 0.0, 1.0 - tail, tail)
    return value * cumulative, cumulative + value * bell * (1.0 / (2.0 * np.pi) ** 0.5)


def column_of(row):
    return jnp.transpose(jnp.broadcast_to(row, (128, row.shape[1])))[:, 0:1]


def middle_kernel(
    second, normed, ca, cc, cb0, cd0, att_own, att_far, pieces, wo, bias, vectors, out_bias, grads, x_fin,
    out, heads_own, heads_far, part, tiles, dvec, dbias, cb1, cd1,
    w1, w2, dw1, dw2, dwo, n_s, f_s, c_s, a_s, act_s, eg_s,
    near_f, near_o, other_f, other_o, cross_f, cross_o, y_s, moved,
    w_sem, l_sem, y_send, y_recv, c_send, c_recv, cf_send, cf_recv, co_send, co_recv, m_send, m_recv,
    *, block, chunk, out_part,
):
    spot = Spot()
    now = pl.program_id(0)
    wide = ca.shape[2]
    count, rows, width = pieces.shape
    hid = w1.shape[0] // count
    heads = wo.shape[0] // HS
    steps = ca_steps = grads.shape[1] // block
    end = 4 * steps
    micro, half, at = now // (2 * steps), (now // steps) % 2, now % steps
    g_row = remote(spot, "row", grads.at[1], cb1, y_send, y_recv)
    g_col = remote(spot, "col", cb1, cd1, c_send, c_recv)
    load_near = pltpu.make_async_copy(cb1, n_s, l_sem.at[0])
    load_far = pltpu.make_async_copy(cd1, f_s, l_sem.at[1])

    def over_core(which, m, i):
        k = m * steps + i
        if which == 0:
            return remote(spot, "col", other_f.at[m, i], cross_f.at[m, i], cf_send.at[k], cf_recv.at[k])
        return remote(spot, "col", other_o.at[m, i], cross_o.at[m, i], co_send.at[k], co_recv.at[k])

    def over_row(m, i):
        k = m * steps + i
        return remote(spot, "row", y_s.at[m, i], moved.at[m, i], m_send.at[k], m_recv.at[k])

    @pl.when(now == 0)
    def _():
        spot.greet("row", "col")
        g_row.start()
        lo = heads * out_part
        copies = []
        for p in range(count):
            here = slice(p * hid, (p + 1) * hid)
            copies.append(pltpu.make_async_copy(pieces.at[p, lo : lo + hid], w1.at[here], w_sem.at[2 * p]))
            copies.append(pltpu.make_async_copy(pieces.at[p, lo + hid :], w2.at[here], w_sem.at[2 * p + 1]))
        for copy in copies:
            copy.start()
        dw1[...] = jnp.zeros_like(dw1)
        dw2[...] = jnp.zeros_like(dw2)
        dwo[...] = jnp.zeros_like(dwo)
        dbias[...] = jnp.zeros_like(dbias)
        for copy in copies:
            copy.wait()

    @pl.when(now == 2 * steps)
    def _():
        load_near.wait()
        load_far.wait()

    before = now - 1

    @pl.when((now > 0) & ((before // steps) % 2 == 0) & (now < end))
    def _():
        m, i = before // (2 * steps), before % steps
        over_core(0, m, i).wait_recv()
        y_s[m, i] = (near_f[...] + cross_f[m, i].astype(F32)).astype(BF16)
        over_row(m, i).start()

    def finish(m, i):
        over_row(m, i).wait_recv()
        over_core(1, m, i).wait_recv()
        out[0] = (
            x_fin[0].astype(F32) + near_o[m, i].astype(F32) + cross_o[m, i].astype(F32)
            + moved[m, i].astype(F32) + out_bias[...]
        ).astype(BF16)

    @pl.when((now >= 2 * steps) & (now < 3 * steps))
    def _():
        finish(0, now - 2 * steps)

    @pl.when(now > 3 * steps)
    def _():
        finish(1, now - 3 * steps - 1)

    @pl.when((half == 0) & (now < steps))
    def _():
        c_s[:, :wide] = cb0[...]
        c_s[:, wide:] = cd0[...]

    @pl.when((half == 0) & (now >= 2 * steps) & (now < end))
    def _():
        here = pl.ds(pl.multiple_of(at * block, block), block)
        c_s[:, :wide] = n_s[here, :]
        c_s[:, wide:] = f_s[here, :]

    @pl.when((half == 1) & (now < end))
    def _():
        c_s[:, :wide] = ca[0]
        c_s[:, wide:] = cc[0]
        a_s[...] = att_own[0]

    @pl.when((half == 0) & (now < end))
    def _():
        a_s[...] = att_far[0]

    @pl.when(now < end)
    def _():
        hidden = w1.shape[0]
        for lo in range(0, hidden, chunk):
            hi = lo + chunk
            expanded = mm(second[0, 0], w1[lo:hi, :], NT) + bias[:, lo:hi]
            active, slope = gelu_pair(expanded)
            act_s[:, lo:hi] = active.astype(BF16)
            rounded = (mm(c_s[...], w2[lo:hi, :], NT) * slope).astype(BF16)
            eg_s[:, lo:hi] = rounded
            dbias[:, lo:hi] += jnp.sum(rounded.astype(F32), axis=0, keepdims=True)
        for lo in range(0, hidden, chunk):
            hi = lo + chunk
            dw2[lo:hi, :] += mm(act_s[:, lo:hi], c_s[...], TN)
            dw1[lo:hi, :] += mm(eg_s[:, lo:hi], normed[0, 0], TN)
        dwo[...] += mm(a_s[...], c_s[...], NN)
        near = mm(act_s[...], w2[:, :wide], NN) + mm(a_s[...], wo[:, :wide], TN)
        other = (mm(act_s[...], w2[:, wide:], NN) + mm(a_s[...], wo[:, wide:], TN)).astype(BF16)
        part[0, 0] = (mm(eg_s[...], w1[...], NN) * vectors[2:3, :]).astype(BF16)
        heads_grad = mm(wo[...], c_s[...], NT).astype(BF16)

        @pl.when(half == 0)
        def _():
            heads_far[0] = heads_grad
            near_f[...] = near
            other_f[micro, at] = other
            over_core(0, micro, at).start()

        @pl.when(half == 1)
        def _():
            heads_own[0] = heads_grad
            near_o[micro, at] = near.astype(BF16)
            other_o[micro, at] = other
            over_core(1, micro, at).start()

    @pl.when(now == 2 * steps - 2)
    def _():
        g_row.wait_recv()
        g_col.start()

    @pl.when(now == 2 * steps - 1)
    def _():
        g_col.wait_recv()
        load_near.start()
        load_far.start()

    @pl.when(now == end)
    def _():
        lo = heads * out_part
        summed = column_of(dbias[...])
        gain_grad = jnp.zeros((1, width), F32)
        bias_grad = jnp.zeros((1, width), F32)
        for p in range(count):
            here = slice(p * hid, (p + 1) * hid)
            small = [dwo[h * HS + p * out_part : h * HS + (p + 1) * out_part, :] for h in range(heads)]
            tiles[p, :lo] = jnp.concatenate(small, axis=0).astype(BF16)
            tiles[p, lo : lo + hid] = (dw1[here, :] * vectors[2:3, :] + summed[here] * vectors[3:4, :]).astype(BF16)
            tiles[p, lo + hid :] = dw2[here, :].astype(BF16)
            weight = w1[here, :].astype(F32)
            gain_grad += jnp.sum(weight * dw1[here, :], axis=0, keepdims=True)
            bias_grad += jnp.sum(weight * summed[here], axis=0, keepdims=True)
        dvec[0:1, :] = gain_grad
        dvec[1:2, :] = bias_grad
        g_row.wait_send()
        g_col.wait_send()
        for m in range(2):
            for i in range(steps):
                over_core(0, m, i).wait_send()
                over_core(1, m, i).wait_send()
                over_row(m, i).wait_send()


def middle(second, normed, residual, cotangent, cc, cb0, cd0, att_own, att_far, pieces, wo, bias, vectors, out_bias, block=512, chunk=1024):
    micros, tokens, wide = cotangent.shape
    count, rows, width = pieces.shape
    block = min(block, tokens)
    steps = tokens // block
    hidden, head_rows = bias.shape[1], wo.shape[0]
    hid = hidden // count
    out_part = (rows - 2 * hid) * HS // head_rows
    end, top = steps - 1, 4 * steps - 1

    def place(s):
        s = jnp.minimum(s, top)
        return s // (2 * steps), (s // steps) % 2, s % steps

    def own_at(s):
        m, h, i = place(s)
        return m, h * i

    def far_at(s):
        m, h, i = place(s)
        return m, i * (1 - h) + end * h

    def finished(s):
        late = s > 3 * steps
        number = jnp.where(late, s - 3 * steps - 1, jnp.clip(s - 2 * steps, 0, end))
        return jnp.where(late, 1, 0), number, 0

    both = lambda n: pl.BlockSpec((1, 1, block, n), lambda s: (*place(s), 0))
    own = pl.BlockSpec((1, block, wide), lambda s: (*own_at(s), 0))
    far0 = pl.BlockSpec((block, wide), lambda s: (jnp.minimum(s, end), 0))
    cols_own = pl.BlockSpec((1, head_rows, block), lambda s: (own_at(s)[0], 0, own_at(s)[1]))
    cols_far = pl.BlockSpec((1, head_rows, block), lambda s: (far_at(s)[0], 0, far_at(s)[1]))
    fin = pl.BlockSpec((1, block, wide), finished)
    halves = jax.ShapeDtypeStruct((tokens, wide), BF16)
    stack = lambda dtype: pltpu.VMEM((micros, steps, block, wide), dtype)
    return pl.pallas_call(
        partial(middle_kernel, block=block, chunk=min(chunk, hidden), out_part=out_part),
        grid=(4 * steps + 1,),
        in_specs=[
            both(width), both(width), own, own, far0, far0, cols_own, cols_far, ANYWHERE, whole(wo.shape),
            whole(bias.shape), whole(vectors.shape), whole(out_bias.shape), ANYWHERE, fin,
        ],
        out_specs=[
            fin, cols_own, cols_far, both(width), whole(pieces.shape), whole((8, width)), whole(bias.shape),
            ANYWHERE, ANYWHERE,
        ],
        out_shape=[
            jax.ShapeDtypeStruct((micros, tokens, wide), BF16),
            jax.ShapeDtypeStruct((micros, head_rows, tokens), BF16),
            jax.ShapeDtypeStruct((micros, head_rows, tokens), BF16),
            jax.ShapeDtypeStruct((micros, 2, tokens, width), BF16),
            jax.ShapeDtypeStruct(pieces.shape, BF16),
            jax.ShapeDtypeStruct((8, width), F32),
            jax.ShapeDtypeStruct(bias.shape, F32),
            halves, halves,
        ],
        scratch_shapes=[
            pltpu.VMEM((hidden, width), BF16),
            pltpu.VMEM((hidden, width), BF16),
            pltpu.VMEM((hidden, width), F32),
            pltpu.VMEM((hidden, width), F32),
            pltpu.VMEM((head_rows, width), F32),
            pltpu.VMEM((tokens, wide), BF16),
            pltpu.VMEM((tokens, wide), BF16),
            pltpu.VMEM((block, width), BF16),
            pltpu.VMEM((head_rows, block), BF16),
            pltpu.VMEM((block, hidden), BF16),
            pltpu.VMEM((block, hidden), BF16),
            pltpu.VMEM((block, wide), F32), stack(BF16), stack(BF16), stack(BF16), stack(BF16), stack(BF16),
            stack(BF16), stack(BF16),
            Gather.sems(2 * count), Gather.sems(2),
            pltpu.SemaphoreType.DMA, pltpu.SemaphoreType.DMA, pltpu.SemaphoreType.DMA, pltpu.SemaphoreType.DMA,
            *[Gather.sems(micros * steps) for _ in range(6)],
        ],
        compiler_params=params(collective_id=2, has_side_effects=True),
        cost_estimate=cost(2 * micros * tokens * 2 * width * (6 * hidden + 3 * head_rows), 80 << 20),
        name="middle",
    )(
        second, normed, cotangent, cc, cb0, cd0, att_own, att_far, pieces, wo, bias, vectors, out_bias, cotangent,
        residual,
    )


class Scatter:
    def __init__(self, spot, tiles, own, rx, rz, x_sems, z_sems):
        self.spot, self.own, self.rx, self.rz = spot, own, rx, rz
        self.order = [*range(1, spot.depth), 0]
        self.cross, self.along = {}, {}
        for s in self.order:
            away = spot.along(s) + 1 - 2 * spot.x
            self.cross[s] = remote(spot, "x", tiles(away), rx(s), x_sems[0](s), x_sems[1](s))
            if s:
                self.along[s] = pltpu.make_async_remote_copy(
                    src_ref=rx(s), dst_ref=rz(s - 1), send_sem=z_sems[0](s), recv_sem=z_sems[1](s),
                    device_id={"dp": spot.along(s)}, device_id_type=MESH,
                )

    def begin(self):
        for s in self.order:
            self.cross[s].start()

    def fold(self, s):
        self.cross[s].wait_recv()
        rx = self.rx(s)
        if s:
            rx[...] = (self.own(s)[...].astype(F32) + rx[...].astype(F32)).astype(BF16)
            self.along[s].start()

    def total(self):
        added = self.own(0)[...].astype(F32) + self.rx(0)[...].astype(F32)
        for s in self.order[:-1]:
            self.along[s].wait_recv()
            added = added + self.rz(s - 1)[...].astype(F32)
        return added

    def close(self):
        for s in self.order:
            self.cross[s].wait_send()
            if s:
                self.along[s].wait_send()


def back_kernel(
    triple, h_own, h_far, att_own, att_far, logsum, cosine, sine, part, weight, vectors, early, normed, tiles,
    x_fin, xc_fin, g_fin,
    grad_out, rest_out, dq_out, vec_out,
    g_s, delta_s, dq_s, dk_s, dv_s, t_s, norm_in, total, bias_s, gain_s, shift_s,
    near_f, near_o, other_f, other_o, cross_f, cross_o, moved, sum_s, sum_r, ng_s, norm_s, inv_s,
    a_own, a_rx, a_rz, a_total, b_tiles, b_rx, b_rz, b_total, held, arrived,
    n_load, a_load, a_xs, a_xr, a_zs, a_zr, b_xs, b_xr, b_zs, b_zr, k_send, k_recv, k_loc,
    v_send, v_recv, cf_send, cf_recv, co_send, co_recv, m_send, m_recv, s_send, s_recv,
    *, block, wider, step,
):
    spot = Spot()
    now = pl.program_id(0)
    tokens, wide = h_own.shape[2], x_fin.shape[2]
    width, length = 2 * wide, 2 * tokens
    heads = weight.shape[0] // (3 * HS)
    steps = tokens // block
    group = wider // block
    slow = tokens // wider
    count, depth = spot.count, spot.depth
    size = 3 * HS // count
    l0 = heads
    b1 = l0 + 2 * slow
    l1 = b1 + heads
    e0 = l1 + 2 * slow
    end = e0 + 2 * steps
    here, there = spot.row, 1 - spot.row
    at_step = lambda k: pl.when(now == k)

    sem = lambda ref, base=0: (lambda s: ref.at[base + s])
    first_sum = Scatter(
        spot, lambda p: tiles.at[p], lambda s: a_own.at[s], lambda s: a_rx.at[s], lambda s: a_rz.at[s],
        (sem(a_xs), sem(a_xr)), (sem(a_zs), sem(a_zr)),
    )

    def head_sum(h):
        return Scatter(
            spot, lambda p: b_tiles.at[p, h], lambda s: b_tiles.at[spot.along(s), h], lambda s: b_rx.at[h, s],
            lambda s: b_rz.at[h, s], (sem(b_xs, h * depth), sem(b_xr, h * depth)), (sem(b_zs, h * depth), sem(b_zr, h * depth)),
        )

    loads = [pltpu.make_async_copy(tiles.at[spot.along(s)], a_own.at[s], a_load.at[s]) for s in range(depth)]
    load_norm = [pltpu.make_async_copy(normed.at[m], norm_in, n_load.at[m]) for m in range(2)]

    def to_core(k, source, out):
        return (
            remote(spot, "col", source.at[:, pl.ds(wide, wide)], out.at[spot.col], k_send.at[k], k_recv.at[k]),
            pltpu.make_async_copy(source.at[:, pl.ds(0, wide)], out.at[spot.col], k_loc.at[k]),
        )

    a_core, b_core = to_core(0, a_total, rest_out), to_core(1, b_total, dq_out)

    partners = [{"col": 1 - spot.col}, {"row": 1 - spot.row}, {"dp": spot.z * 2 + (1 - spot.x)}]
    stride = 1
    while stride < depth:
        other_z = spot.z + stride * (1 - 2 * ((spot.z // stride) % 2))
        partners.append({"dp": other_z * 2 + spot.x})
        stride *= 2
    hops = [
        pltpu.make_async_remote_copy(
            src_ref=held.at[k], dst_ref=arrived.at[k], send_sem=v_send.at[k], recv_sem=v_recv.at[k],
            device_id=partner, device_id_type=MESH,
        )
        for k, partner in enumerate(partners)
    ]

    def over_core(which, m, i):
        k = m * steps + i
        if which == 0:
            return remote(spot, "col", other_f.at[i], cross_f.at[m, i], cf_send.at[k], cf_recv.at[k])
        return remote(spot, "col", other_o.at[i], cross_o.at[m, i], co_send.at[k], co_recv.at[k])

    def over_row(m, i):
        k = m * steps + i
        return remote(spot, "row", cross_f.at[m, i], moved.at[m, i], m_send.at[k], m_recv.at[k])

    def sums_over(m, i):
        k = m * steps + i
        return remote(spot, "col", sum_s.at[m, i], sum_r.at[m, i], s_send.at[k], s_recv.at[k])

    @at_step(0)
    def _():
        barrier = pltpu.get_barrier_semaphore()
        near = [{"col": 1 - spot.col}, {"row": 1 - spot.row}, {"dp": spot.z * 2 + (1 - spot.x)}]
        for device in near + [{"dp": spot.along(s)} for s in range(1, depth)]:
            pl.semaphore_signal(barrier, inc=1, device_id=device, device_id_type=MESH)
        load_norm[0].start()
        for load in loads:
            load.start()
        bias_s[...] = jnp.zeros_like(bias_s)
        gain_s[...] = jnp.zeros_like(gain_s)
        shift_s[...] = jnp.zeros_like(shift_s)
        pl.semaphore_wait(barrier, depth + 2)
        first_sum.begin()
        load_norm[0].wait()

    @at_step(1)
    def _():
        for load in loads:
            load.wait()

    @at_step(l0)
    def _():
        load_norm[1].start()

    @at_step(b1)
    def _():
        load_norm[1].wait()
        for i in range(steps):
            over_core(0, 0, i).wait_send()
            over_core(1, 0, i).wait_send()

    @pl.when((now < l0) | ((now >= b1) & (now < l1)))
    def _():
        head = jnp.where(now < l0, now, now - b1)
        for grad, att, place in ((h_own, att_own, here), (h_far, att_far, there)):
            at = lanes(place, tokens)
            g_s[:, at] = grad[0]
            delta_s[:, at] = jnp.sum(grad[0].astype(F32) * att[0].astype(F32), axis=0, keepdims=True)
        q_s, k_s, v_s = (triple.at[0, i * HS : (i + 1) * HS] for i in range(3))
        dk_s[...] = jnp.zeros_like(dk_s)
        dv_s[...] = jnp.zeros_like(dv_s)
        allowed = causal_tile(step)
        for i in range(length // step):
            lo, hi = i * step, (i + 1) * step
            query, grad = q_s[:, lo:hi], g_s[:, lo:hi]
            base, delta = logsum[0, 0, :, lo:hi], delta_s[:, lo:hi]
            query_grad = None
            cuts = [*range(0, lo, 512), lo, hi]
            for begin, stop in zip(cuts[:-1], cuts[1:]):
                if stop == begin:
                    continue
                raised = jnp.exp(mm(k_s[:, begin:stop], query, TN) - base)
                if begin == lo:
                    raised = jnp.where(allowed, raised, 0.0)
                prob_grad = mm(v_s[:, begin:stop], grad, TN)
                raised = raised.astype(BF16)
                score_grad = raised * (prob_grad - delta).astype(BF16)
                dv_s[:, begin:stop] += mm(grad, raised, NT)
                dk_s[:, begin:stop] += mm(query, score_grad, NT)
                term = mm(k_s[:, begin:stop], score_grad, NN)
                query_grad = term if query_grad is None else query_grad + term
            dq_s[:, lo:hi] = query_grad * HS ** (-0.5)
        cos, sin = cosine[...], sine[...]
        pieces = []
        for ref in (dq_s, dk_s):
            g1, g2 = ref[0:HALF, :], ref[HALF:ROT, :]
            pieces += [g1 * cos + g2 * sin, g2 * cos - g1 * sin, ref[ROT:HS, :]]
        pieces.append(dv_s[...])
        rounded = jnp.concatenate(pieces, axis=0).astype(BF16)
        at = pl.ds(pl.multiple_of(head * 3 * HS, HS), 3 * HS)
        t_s[at, :] = rounded
        bias_s[at, :] += jnp.sum(rounded.astype(F32), axis=1, keepdims=True)
        term = mm(t_s[at, lanes(there, tokens)], norm_in[0], NN) + mm(t_s[at, lanes(here, tokens)], norm_in[1], NN)

        @pl.when(now < l0)
        def _():
            total[head] = term

        @pl.when(now >= b1)
        def _():
            gain, shift = vectors[0:1, :], vectors[1:2, :]
            every = total[head] + term
            weights = weight[at, :].astype(F32)
            summed = bias_s[at, :]
            gain_s[...] += jnp.sum(weights * every, axis=0, keepdims=True)
            shift_s[...] += jnp.sum(weights * summed, axis=0, keepdims=True)
            every = every * gain + summed * shift
            for p in range(count):
                b_tiles[p, head] = every[p * size : (p + 1) * size].astype(BF16)
            head_sum(head).begin()

    moments = {1: 3, 2: l0 + 3, 3: b1 + 2, 0: l1} if depth == 4 else {}
    for s in first_sum.order:
        @at_step(moments.get(s, b1 + 2))
        def _():
            first_sum.fold(s)

    @pl.when((now > b1) & (now < l1))
    def _():
        before = head_sum(now - 1 - b1)
        for s in before.order:
            before.fold(s)

    @at_step(l1 + 1)
    def _():
        used = early.shape[0]
        lanes_here = held.shape[2]
        part_rows = width // (2 * lanes_here)
        held[0] = jnp.zeros_like(held[0])
        held[0, 0:used, :] = early[...]
        at = used
        for vector in (gain_s, shift_s):
            for r in range(2 * part_rows):
                mirror = (r + part_rows) % (2 * part_rows)
                plain = vector[:, r * lanes_here : (r + 1) * lanes_here]
                turned = vector[:, mirror * lanes_here : (mirror + 1) * lanes_here]
                held[0, at : at + 1, :] = jnp.where(spot.col == 0, plain, turned)
                at += 1
        line = jnp.transpose(jnp.broadcast_to(bias_s[...], (bias_s.shape[0], 128)))[0:1, :]
        mine = spot.row * 2 + spot.col
        for h in range(4 * heads):
            k = h % heads
            values = line[:, k * 3 * HS : (k + 1) * 3 * HS]
            held[0, at : at + 1, 0 : 3 * HS] = jnp.where(mine == h // heads, values, 0.0)
            at += 1

    later = now >= b1
    lead = jnp.where(later, now - l1, now - l0)

    @pl.when((lead >= 0) & (lead < 2 * slow))
    def _():
        m, half, at = jnp.where(later, 1, 0), lead // slow, lead % slow
        place = jnp.where(half == 0, there, here)
        blocks = [(j, at * group + j, slice(j * block, (j + 1) * block)) for j in range(group)]
        turned = lambda i: t_s[:, pl.ds(pl.multiple_of(place * tokens + i * block, block), block)]
        for j, i, rows in blocks:
            other = (mm(turned(i), weight[:, wide:], TN) * vectors[0:1, wide:] + part[0, 0, rows, wide:].astype(F32)).astype(BF16)

            @pl.when(half == 0)
            def _():
                other_f[i] = other
                over_core(0, m, i).start()

            @pl.when(half == 1)
            def _():
                other_o[i] = other
                over_core(1, m, i).start()

        for j, i, rows in blocks:
            near = mm(turned(i), weight[:, :wide], TN) * vectors[0:1, :wide] + part[0, 0, rows, :wide].astype(F32)

            @pl.when(half == 0)
            def _():
                near_f[j] = near

            @pl.when(half == 1)
            def _():
                near_o[m, i] = near.astype(BF16)

        @pl.when(half == 0)
        def _():
            for j, i, rows in blocks:
                over_core(0, m, i).wait_recv()
                cross_f[m, i] = (near_f[j] + cross_f[m, i].astype(F32)).astype(BF16)
                over_row(m, i).start()

    @at_step(l1 + 2)
    def _():
        before = head_sum(heads - 1)
        for s in before.order:
            before.fold(s)

    for k in range(len(hops) + 1):
        @at_step(l1 + 1 + k)
        def _():
            if k:
                hops[k - 1].wait_recv()
            if 0 < k < len(hops):
                held[k] = held[k - 1] + arrived[k - 1]
            if k < len(hops):
                hops[k].start()
            else:
                vec_out[...] = held[k - 1] + arrived[k - 1]

    @at_step(e0)
    def _():
        a_total[...] = first_sum.total()
        for copy in a_core:
            copy.start()

    @at_step(e0 + steps)
    def _():
        first_sum.close()
        for h in range(heads):
            head_sum(h).close()
        for i in range(steps):
            over_core(0, 1, i).wait_send()
            over_core(1, 1, i).wait_send()
            over_row(0, i).wait_send()

    trail = now - e0

    @at_step(e0 + steps - 1)
    def _():
        for h in range(heads):
            b_total[h * size : (h + 1) * size, :] = head_sum(h).total()
        for copy in b_core:
            copy.start()

    @pl.when((trail >= 0) & (trail < 2 * steps))
    def _():
        m, i, slot = trail // steps, trail % steps, trail % 2
        over_row(m, i).wait_recv()
        over_core(1, m, i).wait_recv()
        grad = near_o[m, i].astype(F32) + cross_o[m, i].astype(F32) + moved[m, i].astype(F32)
        near_x, far_x = x_fin[0].astype(F32), xc_fin[0].astype(F32)
        center = jnp.sum(near_x + far_x, axis=1, keepdims=True) / width
        spread = jnp.sum(near_x * near_x + far_x * far_x, axis=1, keepdims=True) / width - center * center
        inv = lax.rsqrt(spread + EPSILON)
        normed_x = (near_x - center) * inv
        ng_s[slot] = grad
        norm_s[slot] = normed_x
        inv_s[slot] = inv
        column = lax.broadcasted_iota(jnp.int32, (block, 128), 1)
        one = jnp.sum(grad, axis=1, keepdims=True)
        two = jnp.sum(grad * normed_x, axis=1, keepdims=True)
        sum_s[m, i] = jnp.where(column == 0, one, jnp.where(column == 1, two, 0.0))
        sums_over(m, i).start()

    @pl.when(trail > 0)
    def _():
        m, i, slot = (trail - 1) // steps, (trail - 1) % steps, (trail - 1) % 2
        sums_over(m, i).wait_recv()
        sums = (sum_s[m, i] + sum_r[m, i]) / width
        grad_out[0] = g_fin[0].astype(F32) + inv_s[slot] * (ng_s[slot] - sums[:, 0:1] - norm_s[slot] * sums[:, 1:2])

    @at_step(end)
    def _():
        for copy in (*a_core, *b_core):
            copy.wait()
        for k in hops:
            k.wait_send()
        for i in range(steps):
            over_row(1, i).wait_send()
            for m in range(2):
                sums_over(m, i).wait_send()


def backward(
    triple, h_own, h_far, att_own, att_far, logsum, cosine, sine, normed, part, weight, vectors, tiles, early,
    residual, xc, cotangent, block=512, wider=512, step=512,
):
    micros, rows, length = triple.shape
    tokens, wide = length // 2, residual.shape[2]
    width = 2 * wide
    heads = rows // (3 * HS)
    block, wider, step = min(block, tokens), min(wider, tokens), min(step, length)
    steps, slow = tokens // block, tokens // wider
    count, piece = tiles.shape[:2]
    depth = count // 2
    small = rows // count
    l0 = heads
    b1 = l0 + 2 * slow
    l1 = b1 + heads
    e0 = l1 + 2 * slow

    def head_of(s):
        late = s >= b1
        return jnp.where(late, 1, 0), jnp.minimum(jnp.where(late, s - b1, s), heads - 1)

    def part_at(s):
        late = s >= b1
        number = jnp.clip(jnp.where(late, s - l1, s - l0), 0, 2 * slow - 1)
        return jnp.where(late, 1, 0), number // slow, number % slow, 0

    def in_at(s):
        number = jnp.clip(s - e0, 0, 2 * steps - 1)
        return number // steps, number % steps, 0

    def out_at(s):
        number = jnp.clip(s - e0 - 1, 0, 2 * steps - 1)
        return number // steps, number % steps, 0

    narrow = pl.BlockSpec((1, HS, tokens), lambda s: (*head_of(s), 0))
    fin_in = pl.BlockSpec((1, block, wide), in_at)
    fin_out = pl.BlockSpec((1, block, wide), out_at)
    hops = 3 + max(depth - 1, 0).bit_length()
    vec_rows = early.shape[0] + 2 * (width // early.shape[1]) + 4 * heads
    pair = lambda dtype: pltpu.VMEM((micros, steps, block, wide), dtype)
    single = lambda dtype: pltpu.VMEM((steps, block, wide), dtype)
    sems = Gather.sems
    return pl.pallas_call(
        partial(back_kernel, block=block, wider=wider, step=step),
        grid=(e0 + 2 * steps + 1,),
        in_specs=[
            pl.BlockSpec((1, 3 * HS, length), lambda s: (*head_of(s), 0)), narrow, narrow, narrow, narrow,
            pl.BlockSpec((1, 1, 1, length), lambda s: (*head_of(s), 0, 0)), whole(cosine.shape), whole(sine.shape),
            pl.BlockSpec((1, 1, wider, width), part_at),
            whole(weight.shape), whole(vectors.shape), whole(early.shape), ANYWHERE, ANYWHERE, fin_in, fin_in, fin_out,
        ],
        out_specs=[fin_out, ANYWHERE, ANYWHERE, whole((vec_rows, early.shape[1]))],
        out_shape=[
            jax.ShapeDtypeStruct((micros, tokens, wide), F32),
            jax.ShapeDtypeStruct((2, piece, wide), F32),
            jax.ShapeDtypeStruct((2, small, wide), F32),
            jax.ShapeDtypeStruct((vec_rows, early.shape[1]), F32),
        ],
        scratch_shapes=[
            pltpu.VMEM((HS, length), BF16),
            pltpu.VMEM((1, length), F32),
            pltpu.VMEM((HS, length), F32),
            pltpu.VMEM((HS, length), F32),
            pltpu.VMEM((HS, length), F32),
            pltpu.VMEM((rows, length), BF16),
            pltpu.VMEM((2, tokens, width), BF16),
            pltpu.VMEM((heads, 3 * HS, width), F32),
            pltpu.VMEM((rows, 1), F32),
            pltpu.VMEM((1, width), F32), pltpu.VMEM((1, width), F32),
            pltpu.VMEM((wider // block, block, wide), F32), pair(BF16), single(BF16), single(BF16), pair(BF16), pair(BF16),
            pair(BF16),
            pltpu.VMEM((micros, steps, block, 128), F32), pltpu.VMEM((micros, steps, block, 128), F32),
            pltpu.VMEM((2, block, wide), F32), pltpu.VMEM((2, block, wide), F32), pltpu.VMEM((2, block, 1), F32),
            pltpu.VMEM((depth, piece, width), BF16), pltpu.VMEM((depth, piece, width), BF16),
            pltpu.VMEM((depth - 1, piece, width), BF16), pltpu.VMEM((piece, width), F32),
            pltpu.VMEM((count, heads, small // heads, width), BF16),
            pltpu.VMEM((heads, depth, small // heads, width), BF16),
            pltpu.VMEM((heads, depth - 1, small // heads, width), BF16),
            pltpu.VMEM((small, width), F32),
            pltpu.VMEM((hops, vec_rows, early.shape[1]), F32), pltpu.VMEM((hops, vec_rows, early.shape[1]), F32),
            sems(2), sems(depth), sems(depth), sems(depth), sems(depth), sems(depth),
            *[sems(depth * heads) for _ in range(4)], sems(2), sems(2), sems(2),
            sems(hops), sems(hops), *[sems(micros * steps) for _ in range(8)],
        ],
        compiler_params=params(collective_id=3, has_side_effects=True),
        cost_estimate=cost(micros * (heads * length * length * 256 * 5 + length * width * 4 * rows), 100 << 20),
        name="backward",
    )(
        triple, h_own, h_far, att_own, att_far, logsum, cosine, sine, part, weight, vectors, early, normed, tiles,
        residual, xc, cotangent,
    )


def pick(value, index, axis=0):
    return lax.dynamic_index_in_dim(value, index, axis, keepdims=False)


def body(
    residual, attend_norm_gain, attend_norm_bias, expand_norm_gain, expand_norm_bias,
    attend_weight, attend_bias, output_weight, output_bias, expand_weight, expand_bias,
    shrink_weight, shrink_bias, cotangent,
):
    count = lax.axis_size("dp")
    row, col = lax.axis_index("row"), lax.axis_index("col")
    micros, tokens, wide = residual.shape
    width, length = 2 * wide, 2 * tokens
    heads = attend_weight.shape[1] // 2
    head_part, out_part = attend_weight.shape[2], output_weight.shape[1]
    hid = expand_weight.shape[1] // 2

    def sides(rows):
        return pick(rows, col), pick(rows, 1 - col)

    head_mine, head_theirs = sides(attend_weight.transpose(1, 2, 0).reshape(2, heads * head_part, wide))
    rest_mine, rest_theirs = sides(
        jnp.concatenate(
            [
                output_weight.reshape(2, heads * out_part, wide),
                expand_weight.T.reshape(2, hid, wide),
                shrink_weight.reshape(2, hid, wide),
            ],
            axis=1,
        )
    )

    vectors = jnp.stack([attend_norm_gain, attend_norm_bias, expand_norm_gain, expand_norm_bias])
    vectors = jnp.concatenate([jnp.roll(vectors, -col * wide, axis=1), jnp.zeros((4, width), F32)])
    head_begin = row * 2 * heads + col * heads
    bias_q = lax.dynamic_slice_in_dim(attend_bias, head_begin, heads, 0).reshape(-1, 1)
    bias_1 = pick(expand_bias.reshape(count, 4, hid), row * 2 + col, 1).reshape(1, -1)
    out_bias = lax.dynamic_slice_in_dim(output_bias + shrink_bias, col * wide, wide, 0).reshape(1, -1)
    powers = 10000.0 ** (-np.arange(HALF) * (2.0 / ROT))
    angles = powers[:, None] * np.arange(length)[None, :]
    cosine, sine = jnp.asarray(np.cos(angles), F32), jnp.asarray(np.sin(angles), F32)

    normed, second, triple, wq, att_own, att_far, logsum, pieces, xc, cb0, cc, cd0 = forward(
        residual, bias_q, vectors, cosine, sine, head_mine, head_theirs, rest_mine, rest_theirs, cotangent, count
    )
    lo = heads * out_part
    wo = pieces[:, :lo].reshape(count, heads, out_part, width).transpose(1, 0, 2, 3).reshape(heads * HS, width)
    outputs, h_own, h_far, part, tiles, dvec, db1, _, _ = middle(
        second, normed, residual, cotangent, cc, cb0, cd0, att_own, att_far, pieces, wo, bias_1, vectors, out_bias
    )

    dout = jnp.sum(cotangent.astype(F32), axis=(0, 1))
    dout = lax.dynamic_update_slice_in_dim(jnp.zeros((width,), F32), dout, col * wide, 0)
    dvec = jnp.roll(dvec[:2], col * wide, axis=1)
    db1 = lax.dynamic_update_slice_in_dim(
        jnp.zeros((count, 4, hid), F32), db1.reshape(count, 1, hid), row * 2 + col, 1
    )
    lane = 256
    early = jnp.concatenate([db1.reshape(-1, lane), dout.reshape(-1, lane), dvec.reshape(-1, lane)])
    early = jnp.pad(early, ((0, -early.shape[0] % 8), (0, 0)))

    grads, rest_sum, dq_sum, vec = backward(
        triple, h_own, h_far, att_own, att_far, logsum, cosine, sine, normed, part, wq, vectors, tiles, early,
        residual, xc, cotangent,
    )
    attend_weight_grad = dq_sum.reshape(2 * heads, head_part, wide).transpose(2, 0, 1)
    output_weight_grad = rest_sum[:, :lo].reshape(2 * heads, out_part, wide)
    expand_weight_grad = rest_sum[:, lo : lo + hid].reshape(2 * hid, wide).T
    shrink_weight_grad = rest_sum[:, lo + hid :].reshape(2 * hid, wide)

    n1, nw, ne = db1.size // lane, width // lane, early.shape[0]
    cut = lambda at, rows: vec[at : at + rows].reshape(-1)
    dout = cut(n1, nw)
    return (
        outputs, grads, cut(ne, nw), cut(ne + nw, nw), cut(n1 + nw, nw), cut(n1 + 2 * nw, nw),
        attend_weight_grad, vec[ne + 2 * nw :, : 3 * HS], output_weight_grad, dout, expand_weight_grad, cut(0, n1),
        shrink_weight_grad, dout,
    )


def solution(mesh):
    tokens = P(None, ("dp", "row"), "col")
    weights = (P("col", "row", "dp"), P("row", "dp", "col"), P("col", ("dp", "row")), P(("dp", "row"), "col"))
    one = P()
    in_specs = (tokens, one, one, one, one, weights[0], one, weights[1], one, weights[2], one, weights[3], one, tokens)
    out_specs = (tokens, tokens, one, one, one, one, weights[0], one, weights[1], one, weights[2], one, weights[3], one)
    return jax.shard_map(body, mesh=mesh, in_specs=in_specs, out_specs=out_specs, check_vma=False)
```
